32 devices in a mesh: groups: 2 (over x), queue: 16 (over z, y, core).
Axes of the slice: x: 2, y: 2, z: 4, core: 2. Of those that a mesh axis runs over, the one named last changes fastest.
Arguments:
- hidden: bfloat16 [256, 5120], P(('groups', 'queue')), parts along dimension 0, may hold values from -6 to 6
- incoming: bfloat16 [2, 16, 5120], P(None, 'groups'), parts along dimension 1, may hold values from -6 to 6
- levels: int32 [16], replicated, may hold values from 0 to 95, as said below
- mod_table: bfloat16 [96, 3, 5120], replicated, may hold values from -3 to 3
- query_weight: bfloat16 [5120, 5120], P(None, 'queue'), may hold values from -0.078125 to 0.078125
- key_weight: bfloat16 [5120, 5120], P(None, 'queue'), may hold values from -0.078125 to 0.078125
- value_weight: bfloat16 [5120, 5120], P(None, 'queue'), may hold values from -0.078125 to 0.078125
- output_weight: bfloat16 [5120, 5120], P(None, 'queue'), may hold values from -0.078125 to 0.078125
- query_gain: float32 [5120], replicated, may hold values from 0.5 to 1.5
- key_gain: float32 [5120], replicated, may hold values from 0.5 to 1.5
- text_keys: bfloat16 [1024, 5120], P(('groups', 'queue')), parts along dimension 0, may hold values from -6 to 6
- text_values: bfloat16 [1024, 5120], P(('groups', 'queue')), parts along dimension 0, may hold values from -6 to 6
Outputs:
- updated: bfloat16 [256, 5120], P(('groups', 'queue')), parts along dimension 0
The draws below stay inside these ranges and needn't reach their ends.
There are 2 independent parts, one for each index of `groups`. The reference program is written for one: setup_inputs(seed, part) draws one part's arguments, and reference() takes and returns one part's arrays. A program takes and returns all parts, laid end to end along the dimension named above; an argument that names none is the same for every part. Nothing has to cross between parts.
Inputs may be any that keep to these rules, and one draw needn't show every extreme that they name: `levels`: strictly rising along the queue positions; the last position always has level 95.
All inputs are finite; a program needn't handle non-finite values.
Results may differ from the reference program's by a relative error of at most 0.0085.
Values may be sent and summed in bfloat16 or wider, within the bound.
No kernel may reach another device: no remote copies, remote signals or barrier semaphores. Data moves between devices by JAX's collectives and lax.ppermute only.
A program may use at most 128 MiB of HBM per device.

```python
import math
import jax
import jax.numpy as jnp
from jax import lax

D = 5120
HEADS = 40
HD = 128
TOK_DEV = 8
STEPS = 2
LEVELS = 96
TEXT = 512
SPANS = 16
TOKENS = 128


def draw_levels(key, part):
    order = jax.random.permutation(key, LEVELS - 1)
    picked = jnp.sort(order[:SPANS - 1])
    return jnp.concatenate([picked, jnp.array([LEVELS - 1])]).astype(jnp.int32)


def block_levels(own_key, extent, cuts, low, top_value):
    gain = 1.0
    for dim, parts in cuts:
        heights = jax.random.uniform(jax.random.fold_in(jax.random.fold_in(own_key, 6), dim), (parts,), jnp.float32, low / len(cuts), top_value / len(cuts))
        gain = gain * jnp.repeat(jnp.exp(heights), extent[dim] // parts).reshape((-1,) + (1,) * (len(extent) - 1 - dim))
    return gain


def normal_values(key, extent, deviation, most, cuts=(), held_as=jnp.bfloat16):
    drawn = jax.random.normal(key, extent, jnp.float32) * deviation
    if len(cuts) > 0:
        drawn = block_levels(key, extent, cuts, -0.22, 0.18) * drawn
    return jnp.clip(drawn, min=-most, max=most).astype(held_as)


def setup_inputs(seed: int = 0, part: int = 0) -> dict:
    key_list = jax.random.split(jax.random.key(seed), 13)
    part_splits = jax.random.split(jax.random.fold_in(key_list[12], part), 13)
    return {
        "hidden": normal_values(part_splits[0], (TOKENS, D), 1.0, 6.0, ((0, 16),)),
        "incoming": normal_values(part_splits[1], (STEPS, TOK_DEV, D), 1.0, 6.0),
        "levels": draw_levels(jax.random.fold_in(key_list[12], 71), part),
        "mod_table": normal_values(key_list[3], (LEVELS, 3, D), 0.5, 3.0),
        "query_weight": normal_values(key_list[4], (D, D), D ** -0.5, 0.078125, ((1, 16),)),
        "key_weight": normal_values(key_list[5], (D, D), D ** -0.5, 0.078125, ((1, 16),)),
        "value_weight": normal_values(key_list[6], (D, D), D ** -0.5, 0.078125, ((1, 16),)),
        "output_weight": normal_values(key_list[7], (D, D), D ** -0.5, 0.078125, ((1, 16),)),
        "query_gain": jnp.clip(1.0 + 0.1 * jax.random.normal(key_list[8], (D,), jnp.float32), 0.5, 1.5),
        "key_gain": jnp.clip(1.0 + 0.1 * jax.random.normal(key_list[9], (D,), jnp.float32), 0.5, 1.5),
        "text_keys": normal_values(part_splits[10], (TEXT, D), 1.0, 6.0, ((0, 16),)),
        "text_values": normal_values(part_splits[11], (TEXT, D), 1.0, 6.0, ((0, 16),)),
    }


def normalize(values):
    return values * lax.rsqrt(lax.optimization_barrier(jnp.mean(values * values, axis=-1, keepdims=True)) + 1e-06)

def softmax_rounded(scores):
    row_max = lax.optimization_barrier(jnp.max(scores, axis=-1, keepdims=True))
    weights = jnp.exp(scores - row_max)
    return (weights / lax.optimization_barrier(jnp.sum(weights, axis=-1, keepdims=True))).astype(jnp.bfloat16)

def reference(hidden, incoming, levels, mod_table, query_weight, key_weight, value_weight, output_weight, query_gain, key_gain, text_keys, text_values):
    modulation = jnp.take(mod_table, levels.astype(jnp.int32), axis=0).astype(jnp.float32)[:, None]
    score_scale = 1.0 / math.sqrt(HD)
    total_rows = SPANS * TOK_DEV
    span_of = (jnp.arange(total_rows) // TOK_DEV).astype(jnp.int32)
    allowed = span_of[:, None] >= span_of[None, :]
    text_k = text_keys.reshape(TEXT, HEADS, HD).transpose(1, 0, 2)
    text_v = text_values.reshape(TEXT, HEADS, HD).transpose(1, 0, 2)

    def one_head(operands):
        q_one, k_one, v_one, tk_one, tv_one = operands
        scores = jnp.dot(q_one, k_one.T, preferred_element_type=jnp.float32) * score_scale
        scores = jnp.where(allowed, scores, -1e+30)
        attended = jnp.dot(softmax_rounded(scores), v_one, preferred_element_type=jnp.float32).astype(jnp.bfloat16)
        text_scores = jnp.dot(q_one, tk_one.T, preferred_element_type=jnp.float32) * score_scale
        crossed = jnp.dot(softmax_rounded(text_scores), tv_one, preferred_element_type=jnp.float32).astype(jnp.bfloat16)
        return (attended.astype(jnp.float32) + crossed.astype(jnp.float32)).astype(jnp.bfloat16)
    queue_state = hidden
    for section_index in range(STEPS):
        queue_state = jnp.concatenate([incoming[section_index], queue_state[:-TOK_DEV]], axis=0)
        current = queue_state.astype(jnp.float32).reshape(SPANS, TOK_DEV, D)
        modulated = (normalize(current) * (1.0 + modulation[:, :, 1]) + modulation[:, :, 0]).astype(jnp.bfloat16)
        modulated = modulated.reshape(total_rows, D)
        query_rows = (normalize(jnp.dot(modulated, query_weight, preferred_element_type=jnp.float32)) * query_gain).astype(jnp.bfloat16)
        key_rows = (normalize(jnp.dot(modulated, key_weight, preferred_element_type=jnp.float32)) * key_gain).astype(jnp.bfloat16)
        value_rows = jnp.dot(modulated, value_weight, preferred_element_type=jnp.float32).astype(jnp.bfloat16)
        query_heads = query_rows.reshape(total_rows, HEADS, HD).transpose(1, 0, 2)
        key_heads = key_rows.reshape(total_rows, HEADS, HD).transpose(1, 0, 2)
        value_heads = value_rows.reshape(total_rows, HEADS, HD).transpose(1, 0, 2)
        combined = lax.map(one_head, (query_heads, key_heads, value_heads, text_k, text_v))
        combined = combined.transpose(1, 0, 2).reshape(total_rows, D)
        projected = jnp.dot(combined, output_weight, preferred_element_type=jnp.float32).reshape(SPANS, TOK_DEV, D)
        queue_state = (current + modulation[:, :, 2] * projected).astype(jnp.bfloat16).reshape(total_rows, D)
    return queue_state
```

```python
import functools
import math

import jax
import jax.numpy as jnp
from jax import lax
from jax.experimental import pallas as pl
from jax.experimental.pallas import tpu as pltpu
from jax.sharding import PartitionSpec as P

HEADS = 40
STEPS = 2


def passed_along(value, axis, steps):
    count = lax.axis_size(axis)
    initial, last = (max(0, -steps), min(count, count - steps))
    return lax.ppermute(value, axis, [(source, source + steps) for source in range(initial, last)])


def normalize(values):
    return values * lax.rsqrt(jnp.mean(values * values, axis=-1, keepdims=True) + 1e-06)


def softmax_rounded(scores):
    row_max = jnp.max(scores, axis=-1, keepdims=True)
    weights = jnp.exp(scores - row_max)
    return (weights / jnp.sum(weights, axis=-1, keepdims=True)).astype(jnp.bfloat16)


def pad_slots(values, slot_total):
    missing = slot_total - values.shape[1]
    filler = jnp.zeros((values.shape[0], missing, values.shape[2]), values.dtype)
    return jnp.concatenate([values, filler], axis=1)


def causal_block(queries, keys_all, values_all, span_rows, score_scale):
    total_rows = queries.shape[0]
    block_rows = min(512, total_rows)
    scores = (
        jnp.einsum("qsd,ksd->sqk", queries, keys_all, preferred_element_type=jnp.float32)
        * score_scale
    )
    allowed = (
        jnp.arange(0, block_rows)[:, None] // span_rows
        >= jnp.arange(block_rows)[None, :] // span_rows
    )
    scores = jnp.where(allowed[None], scores, -1e30)
    result = jnp.einsum(
        "sqk,ksd->qsd", softmax_rounded(scores), values_all, preferred_element_type=jnp.float32
    )
    pieces = result.astype(jnp.bfloat16)
    return pieces


def text_attend(queries, text_k, text_v, score_scale):
    scores = (
        jnp.einsum("qsd,tsd->sqt", queries, text_k, preferred_element_type=jnp.float32)
        * score_scale
    )
    return jnp.einsum(
        "sqt,tsd->qsd", softmax_rounded(scores), text_v, preferred_element_type=jnp.float32
    ).astype(jnp.bfloat16)


def per_device(
    hidden,
    incoming,
    levels,
    mod_table,
    query_weight,
    key_weight,
    value_weight,
    output_weight,
    query_gain,
    key_gain,
    text_keys,
    text_values,
):
    own_index = lax.axis_index("queue")
    queue_size = lax.axis_size("queue")
    span_rows, model_width = hidden.shape
    head_size = model_width // HEADS
    score_scale = 1.0 / math.sqrt(head_size)
    slot_total = -(-HEADS // queue_size) * queue_size
    own_level = lax.dynamic_index_in_dim(levels, own_index, 0, keepdims=False)
    modulation = lax.dynamic_index_in_dim(mod_table, own_level, 0, keepdims=False).astype(
        jnp.float32
    )
    stacked_weights = jnp.stack([query_weight, key_weight, value_weight])
    text_local = text_keys.shape[0]
    text_k_slots, text_v_slots = (
        lax.all_to_all(
            pad_slots(text_keys.reshape(text_local, HEADS, head_size), slot_total),
            "queue",
            split_axis=1,
            concat_axis=0,
            tiled=True,
        ),
        lax.all_to_all(
            pad_slots(text_values.reshape(text_local, HEADS, head_size), slot_total),
            "queue",
            split_axis=1,
            concat_axis=0,
            tiled=True,
        ),
    )
    queue_state = hidden
    for section_index in range(STEPS):
        shifted = passed_along(queue_state, "queue", 1)
        queue_state = jnp.where(own_index == 0, incoming[section_index], shifted)
        current = queue_state.astype(jnp.float32)
        modulated = (normalize(current) * (1.0 + modulation[1]) + modulation[0]).astype(
            jnp.bfloat16
        )
        columns = jnp.einsum(
            "rd,cdw->crw",
            lax.all_gather(modulated, "queue", axis=0, tiled=True),
            stacked_weights,
            preferred_element_type=jnp.float32,
        )
        own_rows = lax.all_to_all(
            columns.astype(jnp.bfloat16), "queue", split_axis=1, concat_axis=2, tiled=True
        ).astype(columns.dtype)
        query_heads = (
            (normalize(own_rows[0]) * query_gain)
            .astype(jnp.bfloat16)
            .reshape(span_rows, HEADS, head_size)
        )
        key_heads = (
            (normalize(own_rows[1]) * key_gain)
            .astype(jnp.bfloat16)
            .reshape(span_rows, HEADS, head_size)
        )
        value_heads = own_rows[2].astype(jnp.bfloat16).reshape(span_rows, HEADS, head_size)
        query_slots, key_slots, value_slots = (
            lax.all_to_all(
                pad_slots(query_heads, slot_total), "queue", split_axis=1, concat_axis=0, tiled=True
            ),
            lax.all_to_all(
                pad_slots(key_heads, slot_total), "queue", split_axis=1, concat_axis=0, tiled=True
            ),
            lax.all_to_all(
                pad_slots(value_heads, slot_total), "queue", split_axis=1, concat_axis=0, tiled=True
            ),
        )
        attended_slots = causal_block(query_slots, key_slots, value_slots, span_rows, score_scale)
        crossed_slots = text_attend(query_slots, text_k_slots, text_v_slots, score_scale)
        attended_back, crossed_back = (
            lax.all_to_all(attended_slots, "queue", split_axis=0, concat_axis=1, tiled=True),
            lax.all_to_all(crossed_slots, "queue", split_axis=0, concat_axis=1, tiled=True),
        )
        attended = attended_back[:, :HEADS]
        crossed = crossed_back[:, :HEADS]
        combined = (
            (attended.astype(jnp.float32) + crossed.astype(jnp.float32))
            .astype(jnp.bfloat16)
            .reshape(span_rows, model_width)
        )
        out_columns = jnp.dot(
            lax.all_gather(combined, "queue", axis=0, tiled=True),
            output_weight,
            preferred_element_type=jnp.float32,
        )
        projected = lax.all_to_all(
            out_columns.astype(jnp.bfloat16), "queue", split_axis=0, concat_axis=1, tiled=True
        ).astype(out_columns.dtype)
        queue_state = (current + modulation[2] * projected).astype(jnp.bfloat16)
    return queue_state


def swapped(value, bit):
    count = lax.axis_size("queue")
    return lax.ppermute(value, "queue", [(source, source ^ bit) for source in range(count)])


def gathered_over_chips(block):
    chips = lax.axis_size("queue") // 2
    blocks = {0: block}
    bits = [1 << b for b in reversed(range(chips.bit_length() - 1))]
    for bit in bits:
        for mask in list(blocks):
            blocks[mask | bit] = swapped(blocks[mask], 2 * bit)
    return [blocks[mask] for mask in range(chips)]


def contract_last(left, right):
    return lax.dot_general(
        left, right, (((1,), (1,)), ((), ())), preferred_element_type=jnp.float32
    )


VMEM_SPEC = pl.BlockSpec(memory_space=pltpu.VMEM)
SMEM_SPEC = pl.BlockSpec(memory_space=pltpu.SMEM)
ANY_SPEC = pl.BlockSpec(memory_space=pl.ANY)


def kernel_params():
    return pltpu.CompilerParams(vmem_limit_bytes=48 * 1024 * 1024)


def project_kernel(
    step, spans, place_ref, shift_ref, scale_ref, gain_ref, incoming_ref, *refs
):
    chips = spans // 2
    mine, others = refs[:chips], refs[chips : 2 * chips]
    refs = refs[2 * chips :]
    weight_refs, refs = refs[:3], refs[3:]
    own_ref, send_ref, squares_ref = refs[:3]
    refs = refs[3:]
    if step == 0:
        current_ref, refs = refs[0], refs[1:]
    state, modulated, held, sems = refs
    chip, core = place_ref[0], place_ref[1]
    tokens, width = state.shape
    half = tokens // 2
    rows = tokens // spans
    pair = 2 * rows
    cols = held.shape[1]
    copies = [
        pltpu.make_async_copy(weight_refs[i], held.at[i], sems.at[i]) for i in range(3)
    ]
    for copy in copies:
        copy.start()
    first = core == 0
    for mask in range(chips):
        other_chip = chip ^ mask
        if step == 0:
            at = pl.multiple_of(other_chip * pair, pair)
            for low in range(0, width, width // 4):
                part = pl.ds(low, width // 4)
                a = mine[mask][:, part].astype(jnp.float32)
                b = others[mask][:, part].astype(jnp.float32)
                upper = jnp.where(first, b, a)
                upper = jnp.where(
                    other_chip == chips - 1, incoming_ref[:, part].astype(jnp.float32), upper
                )
                both = jnp.concatenate([jnp.where(first, a, b), upper], axis=0)
                state[pl.ds(at, pair), part] = both.astype(jnp.bfloat16)
        else:
            lanes = pl.ds(pl.multiple_of(other_chip * 2 * cols, 2 * cols), 2 * cols)
            state[pl.ds(pl.multiple_of(core * half, half), half), lanes] = mine[mask][...]
            state[pl.ds(pl.multiple_of((1 - core) * half, half), half), lanes] = others[mask][...]
    if step == 0:
        lanes = pl.ds(pl.multiple_of(chip * 2 * cols, 2 * cols), 2 * cols)
        current_ref[...] = state[pl.ds(pl.multiple_of(core * half, half), half), lanes]
    pieces = 4
    piece = width // pieces
    for slab in range(chips):
        band = slice(slab * pair, (slab + 1) * pair)
        total = jnp.zeros((pair, 1), jnp.float32)
        for low in range(0, width, piece):
            x = state[band, low : low + piece].astype(jnp.float32)
            total = total + jnp.sum(x * x, axis=1, keepdims=True)
        factor = lax.rsqrt(total / width + 1e-06)
        at = [(2 * slab + e + step + 1) % spans for e in range(2)]
        for low in range(0, width, piece):
            part = slice(low, low + piece)
            x = state[band, part].astype(jnp.float32) * factor
            scale, shift = (
                jnp.concatenate(
                    [jnp.broadcast_to(ref[s : s + 1, part], (rows, piece)) for s in at], axis=0
                )
                for ref in (scale_ref, shift_ref)
            )
            modulated[band, part] = (x * (1.0 + scale) + shift).astype(jnp.bfloat16)
    ident = lax.broadcasted_iota(jnp.int32, (tokens, tokens), 0) == lax.broadcasted_iota(
        jnp.int32, (tokens, tokens), 1
    )
    for i in range(3):
        copies[i].wait()

        def add(step_k, total):
            part = pl.ds(pl.multiple_of(step_k * piece, piece), piece)
            return total + contract_last(modulated[:, part], held[i, :, part])

        product = lax.fori_loop(0, pieces, add, jnp.zeros((tokens, cols), jnp.float32))
        if i < 2:
            column = jnp.sum(product * product, axis=1, keepdims=True)
            squares_ref[i : i + 1, :] = jnp.sum(
                jnp.where(ident, column, 0.0), axis=0, keepdims=True
            )
            product = product * gain_ref[i : i + 1, :]
        if i == 0:
            low, high = product[:half], product[half:]
            own_ref[:half, :] = jnp.where(first, low, high).astype(jnp.bfloat16)
            send_ref[:half, :] = jnp.where(first, high, low).astype(jnp.bfloat16)
        else:
            band = slice(half + (i - 1) * tokens, half + i * tokens)
            own_ref[band, :] = product.astype(jnp.bfloat16)
            send_ref[band, :] = product.astype(jnp.bfloat16)


def project(step, spans, place, shift, scale, gain, incoming, mine, others, weights):
    tokens = spans * incoming.shape[0]
    cols, width = weights[0].shape
    half = tokens // 2
    own = jax.ShapeDtypeStruct((half + 2 * tokens, cols), jnp.bfloat16)
    out_shape = [own, own, jax.ShapeDtypeStruct((2, tokens), jnp.float32)]
    if step == 0:
        out_shape.append(jax.ShapeDtypeStruct((half, 2 * cols), jnp.bfloat16))
    return pl.pallas_call(
        functools.partial(project_kernel, step, spans),
        out_shape=out_shape,
        in_specs=[SMEM_SPEC] + [VMEM_SPEC] * (4 + len(mine) + len(others)) + [ANY_SPEC] * 3,
        out_specs=[VMEM_SPEC] * len(out_shape),
        scratch_shapes=[
            pltpu.VMEM((tokens, width), jnp.bfloat16),
            pltpu.VMEM((tokens, width), jnp.bfloat16),
            pltpu.VMEM((3, cols, width), jnp.bfloat16),
            pltpu.SemaphoreType.DMA((3,)),
        ],
        compiler_params=kernel_params(),
        name="project",
    )(place, shift, scale, gain, incoming, *mine, *others, *weights)


def attend_kernel(step, spans, head_size, count, place_ref, own_ref, got_ref, text_ref, more_ref, *refs):
    square_refs, (out_ref, queries, keys, values) = refs[:count], refs[count:]
    core = place_ref[1]
    first = core == 0
    half, width = queries.shape
    tokens = 2 * half
    rows = tokens // spans
    cols = width // 2
    for target, low, size in (
        (queries, 0, half),
        (keys, half, tokens),
        (values, half + tokens, tokens),
    ):
        mine = own_ref[low : low + size, :]
        other = got_ref[low : low + size, :]
        target[:, :cols] = jnp.where(first, mine, other)
        target[:, cols:] = jnp.where(first, other, mine)
    squares = square_refs[0][...]
    for ref in square_refs[1:]:
        squares = squares + ref[...]
    factors = lax.rsqrt(squares / (width * (spans // 2)) + 1e-06)
    ident = lax.broadcasted_iota(jnp.int32, (tokens, tokens), 0) == lax.broadcasted_iota(
        jnp.int32, (tokens, tokens), 1
    )
    column = jnp.sum(jnp.where(ident, factors[0:1, :], 0.0), axis=1, keepdims=True)
    column = jnp.where(first, column[:half], column[half:]) * (1.0 / math.sqrt(head_size))
    row = factors[1:2, :]
    shape = (half, tokens)
    own_block = lax.broadcasted_iota(jnp.int32, shape, 0) // rows + core * (spans // 2)
    key_block = lax.broadcasted_iota(jnp.int32, shape, 1) // rows
    allowed = lax.rem(own_block + step + 1, spans) >= lax.rem(key_block + step + 1, spans)
    text_rows = text_ref.shape[0] * text_ref.shape[2]
    for head in range(width // head_size):
        lanes = slice(head * head_size, (head + 1) * head_size)
        q = queries[:, lanes]
        scores = contract_last(q, keys[:, lanes]) * column * row
        scores = jnp.where(allowed, scores, -1e30)
        weights = jnp.exp(scores - jnp.max(scores, axis=1, keepdims=True))
        weights = weights / jnp.sum(weights, axis=1, keepdims=True)
        attended = jnp.dot(
            weights.astype(jnp.bfloat16), values[:, lanes], preferred_element_type=jnp.float32
        ).astype(jnp.bfloat16)
        parts = []
        for ref in (text_ref, more_ref):
            text_keys = ref[:, 0, :, lanes].reshape(text_rows, head_size)
            parts.append(contract_last(q, text_keys) * column)
        most = jnp.maximum(
            jnp.max(parts[0], axis=1, keepdims=True), jnp.max(parts[1], axis=1, keepdims=True)
        )
        parts = [jnp.exp(part - most) for part in parts]
        total = jnp.sum(parts[0], axis=1, keepdims=True) + jnp.sum(parts[1], axis=1, keepdims=True)
        crossed = jnp.zeros((half, head_size), jnp.float32)
        for ref, part in zip((text_ref, more_ref), parts):
            text_values = ref[:, 1, :, lanes].reshape(text_rows, head_size)
            crossed = crossed + jnp.dot(
                (part / total).astype(jnp.bfloat16), text_values, preferred_element_type=jnp.float32
            )
        crossed = crossed.astype(jnp.bfloat16)
        out_ref[:, lanes] = (attended.astype(jnp.float32) + crossed.astype(jnp.float32)).astype(
            jnp.bfloat16
        )


def attend(step, spans, head_size, place, own, got, text, more, squares):
    cols = own.shape[1]
    tokens = squares[0].shape[1]
    half = tokens // 2
    return pl.pallas_call(
        functools.partial(attend_kernel, step, spans, head_size, len(squares)),
        out_shape=jax.ShapeDtypeStruct((half, 2 * cols), jnp.bfloat16),
        in_specs=[SMEM_SPEC] + [VMEM_SPEC] * (4 + len(squares)),
        out_specs=VMEM_SPEC,
        scratch_shapes=[
            pltpu.VMEM((half, 2 * cols), jnp.bfloat16),
            pltpu.VMEM((tokens, 2 * cols), jnp.bfloat16),
            pltpu.VMEM((tokens, 2 * cols), jnp.bfloat16),
        ],
        compiler_params=kernel_params(),
        name="attend",
    )(place, own, got, text, more, *squares)


def output_kernel(step, spans, last, place_ref, current_ref, gate_ref, incoming_ref, own_ref, other_ref, *refs):
    chips = spans // 2
    blocks, refs = refs[:chips], refs[chips:]
    chip, core = place_ref[0], place_ref[1]
    first = core == 0
    half, width = current_ref.shape
    cols = width // 2
    rows = 2 * half // spans
    mine = jnp.zeros((half, cols), jnp.float32)
    other = jnp.zeros((half, cols), jnp.float32)
    for mask in range(chips):
        lanes = pl.ds(pl.multiple_of((chip ^ mask) * width, width), width)
        block = blocks[mask][...]
        mine = mine + contract_last(block, own_ref[:, lanes])
        other = other + contract_last(block, other_ref[:, lanes])
    totals = refs[-1]
    totals[:, :cols] = jnp.where(first, mine, other)
    totals[:, cols:] = jnp.where(first, other, mine)
    for block in range(chips):
        band = slice(block * rows, (block + 1) * rows)
        places = [(block + e * chips + step + 1) % spans for e in range(2)]
        gates = [gate_ref[s : s + 1, :] for s in places]
        gate = jnp.where(first, gates[0], gates[1])
        totals[band, :] = current_ref[band, :].astype(jnp.float32) + gate * totals[band, :]
    if last:
        for turn in range(chips):
            at = pl.multiple_of((chip ^ turn) * rows, rows)
            refs[turn][...] = totals[pl.ds(at, rows), :].astype(jnp.bfloat16)
    else:
        leaving = spans - 2 - step - chips
        band = slice(leaving * rows, (leaving + 1) * rows)
        lanes = pl.ds(pl.multiple_of(chip * width, width), width)
        totals[band, :] = jnp.where(
            first, totals[band, :], incoming_ref[:, lanes].astype(jnp.float32)
        )
        refs[0][...] = totals[...].astype(jnp.bfloat16)


def output(step, spans, last, place, current, gate, incoming, own, other, blocks):
    half, width = current.shape
    chips = spans // 2
    rows = 2 * half // spans
    if last:
        out_shape = [jax.ShapeDtypeStruct((rows, width), jnp.bfloat16)] * chips
    else:
        out_shape = [jax.ShapeDtypeStruct((half, width), jnp.bfloat16)]
    return pl.pallas_call(
        functools.partial(output_kernel, step, spans, last),
        out_shape=out_shape,
        in_specs=[SMEM_SPEC] + [VMEM_SPEC] * (5 + chips),
        out_specs=[VMEM_SPEC] * len(out_shape),
        scratch_shapes=[pltpu.VMEM((half, width), jnp.float32)],
        compiler_params=kernel_params(),
        name="output",
    )(place, current, gate, incoming, own, other, *blocks)


def join_kernel(place_ref, *refs):
    out_ref = refs[-1]
    for turn, ref in enumerate(refs[:-1]):
        width = ref.shape[1]
        lanes = pl.ds(pl.multiple_of((place_ref[2] ^ turn) * width, width), width)
        out_ref[:, lanes] = ref[...]


def join(place, blocks):
    rows, width = blocks[0].shape
    return pl.pallas_call(
        join_kernel,
        out_shape=jax.ShapeDtypeStruct((rows, width * len(blocks)), jnp.bfloat16),
        in_specs=[SMEM_SPEC] + [VMEM_SPEC] * len(blocks),
        out_specs=VMEM_SPEC,
        compiler_params=kernel_params(),
        name="join",
    )(place, *blocks)


def paired_device(
    hidden,
    incoming,
    levels,
    mod_table,
    query_weight,
    key_weight,
    value_weight,
    output_weight,
    query_gain,
    key_gain,
    text_keys,
    text_values,
):
    own_index = lax.axis_index("queue")
    spans = lax.axis_size("queue")
    chips = spans // 2
    chip, core = own_index // 2, own_index % 2
    rows, width = hidden.shape
    cols = query_weight.shape[1]
    head_size = width // HEADS
    home = (own_index + spans - STEPS) % spans
    place = jnp.stack([chip, core, home % chips]).astype(jnp.int32)
    hidden_mine = gathered_over_chips(hidden)
    hidden_others = [swapped(block, 1) for block in hidden_mine]
    picked = (levels[:, None] == jnp.arange(mod_table.shape[0])[None, :]).astype(mod_table.dtype)
    shift, scale, gate = jnp.einsum(
        "sl,ltd->tsd", picked, mod_table, preferred_element_type=jnp.float32
    )
    gate = lax.dynamic_slice_in_dim(gate, chip * 2 * cols, 2 * cols, 1)
    gain = lax.dynamic_slice_in_dim(jnp.stack([query_gain, key_gain]), own_index * cols, cols, 1)
    weights = [w.T for w in (query_weight, key_weight, value_weight)]
    output_own = output_weight.T
    output_other = swapped(output_own, 1)
    text_half = text_keys.shape[0] // 2
    text = jnp.stack([text_keys, text_values]).reshape(2, 2, text_half, chips, 2 * cols)
    text = text.transpose(3, 1, 0, 2, 4).reshape(spans, 2, text_half, 2 * cols)
    text = lax.all_to_all(text, "queue", split_axis=0, concat_axis=0, tiled=True)
    more = swapped(text, 1)
    mine, others = hidden_mine, hidden_others
    current = None
    for step in range(STEPS):
        own, send, squares, *rest = project(
            step, spans, place, shift, scale, gain, incoming[step], mine, others, weights
        )
        if step == 0:
            current = rest[0]
        got = swapped(send, 1)
        squares = gathered_over_chips(squares + swapped(squares, 1))
        block = attend(step, spans, head_size, place, own, got, text, more, squares)
        blocks = gathered_over_chips(block)
        last = step == STEPS - 1
        result = output(
            step, spans, last, place, current, gate, incoming[min(step + 1, STEPS - 1)],
            output_own, output_other, blocks,
        )
        if not last:
            current = result[0]
            mine = gathered_over_chips(current)
            others = [swapped(block, 1) for block in mine]
    rounds = []
    for turn in range(chips):
        pairs = []
        for source in range(spans):
            source_chip, source_core = source // 2, source % 2
            ring = source_core * chips + (source_chip ^ turn)
            pairs.append((source, (ring + STEPS) % spans))
        rounds.append(lax.ppermute(result[turn], "queue", pairs))
    return join(place, rounds)


def held_in_pairs(mesh, hidden, query_weight):
    spans = mesh.shape["queue"]
    rows = hidden.shape[0] // (mesh.shape["groups"] * spans)
    cols = query_weight.shape[1] // spans
    head_size = query_weight.shape[0] // HEADS
    power = spans & (spans - 1) == 0
    return power and spans >= 4 and 2 * cols % head_size == 0 and rows * spans == 128 and rows == 8


def solution(mesh):
    in_specs = (
        P(("groups", "queue"), None),
        P(None, "groups", None),
        P(),
        P(),
        P(None, "queue"),
        P(None, "queue"),
        P(None, "queue"),
        P(None, "queue"),
        P(),
        P(),
        P(("groups", "queue"), None),
        P(("groups", "queue"), None),
    )
    out_specs = P(("groups", "queue"), None)

    def apply(*args):
        body = paired_device if held_in_pairs(mesh, args[0], args[4]) else per_device
        return jax.shard_map(
            body, mesh=mesh, in_specs=in_specs, out_specs=out_specs, check_vma=False
        )(*args)

    return apply
```

```python
import functools
import math

import jax
import jax.numpy as jnp
from jax import lax
from jax.experimental import pallas as pl
from jax.experimental.pallas import tpu as pltpu
from jax.sharding import PartitionSpec as P

HEADS = 40
STEPS = 2


def passed_along(value, axis, steps):
    count = lax.axis_size(axis)
    initial, last = (max(0, -steps), min(count, count - steps))
    return lax.ppermute(value, axis, [(source, source + steps) for source in range(initial, last)])


def normalize(values):
    return values * lax.rsqrt(jnp.mean(values * values, axis=-1, keepdims=True) + 1e-06)


def softmax_rounded(scores):
    row_max = jnp.max(scores, axis=-1, keepdims=True)
    weights = jnp.exp(scores - row_max)
    return (weights / jnp.sum(weights, axis=-1, keepdims=True)).astype(jnp.bfloat16)


def pad_slots(values, slot_total):
    missing = slot_total - values.shape[1]
    filler = jnp.zeros((values.shape[0], missing, values.shape[2]), values.dtype)
    return jnp.concatenate([values, filler], axis=1)


def causal_block(queries, keys_all, values_all, span_rows, score_scale):
    total_rows = queries.shape[0]
    block_rows = min(512, total_rows)
    scores = (
        jnp.einsum("qsd,ksd->sqk", queries, keys_all, preferred_element_type=jnp.float32)
        * score_scale
    )
    allowed = (
        jnp.arange(0, block_rows)[:, None] // span_rows
        >= jnp.arange(block_rows)[None, :] // span_rows
    )
    scores = jnp.where(allowed[None], scores, -1e30)
    result = jnp.einsum(
        "sqk,ksd->qsd", softmax_rounded(scores), values_all, preferred_element_type=jnp.float32
    )
    pieces = result.astype(jnp.bfloat16)
    return pieces


def text_attend(queries, text_k, text_v, score_scale):
    scores = (
        jnp.einsum("qsd,tsd->sqt", queries, text_k, preferred_element_type=jnp.float32)
        * score_scale
    )
    return jnp.einsum(
        "sqt,tsd->qsd", softmax_rounded(scores), text_v, preferred_element_type=jnp.float32
    ).astype(jnp.bfloat16)


def per_device(
    hidden,
    incoming,
    levels,
    mod_table,
    query_weight,
    key_weight,
    value_weight,
    output_weight,
    query_gain,
    key_gain,
    text_keys,
    text_values,
):
    own_index = lax.axis_index("queue")
    queue_size = lax.axis_size("queue")
    span_rows, model_width = hidden.shape
    head_size = model_width // HEADS
    score_scale = 1.0 / math.sqrt(head_size)
    slot_total = -(-HEADS // queue_size) * queue_size
    own_level = lax.dynamic_index_in_dim(levels, own_index, 0, keepdims=False)
    modulation = lax.dynamic_index_in_dim(mod_table, own_level, 0, keepdims=False).astype(
        jnp.float32
    )
    stacked_weights = jnp.stack([query_weight, key_weight, value_weight])
    text_local = text_keys.shape[0]
    text_k_slots, text_v_slots = (
        lax.all_to_all(
            pad_slots(text_keys.reshape(text_local, HEADS, head_size), slot_total),
            "queue",
            split_axis=1,
            concat_axis=0,
            tiled=True,
        ),
        lax.all_to_all(
            pad_slots(text_values.reshape(text_local, HEADS, head_size), slot_total),
            "queue",
            split_axis=1,
            concat_axis=0,
            tiled=True,
        ),
    )
    queue_state = hidden
    for section_index in range(STEPS):
        shifted = passed_along(queue_state, "queue", 1)
        queue_state = jnp.where(own_index == 0, incoming[section_index], shifted)
        current = queue_state.astype(jnp.float32)
        modulated = (normalize(current) * (1.0 + modulation[1]) + modulation[0]).astype(
            jnp.bfloat16
        )
        columns = jnp.einsum(
            "rd,cdw->crw",
            lax.all_gather(modulated, "queue", axis=0, tiled=True),
            stacked_weights,
            preferred_element_type=jnp.float32,
        )
        own_rows = lax.all_to_all(
            columns.astype(jnp.bfloat16), "queue", split_axis=1, concat_axis=2, tiled=True
        ).astype(columns.dtype)
        query_heads = (
            (normalize(own_rows[0]) * query_gain)
            .astype(jnp.bfloat16)
            .reshape(span_rows, HEADS, head_size)
        )
        key_heads = (
            (normalize(own_rows[1]) * key_gain)
            .astype(jnp.bfloat16)
            .reshape(span_rows, HEADS, head_size)
        )
        value_heads = own_rows[2].astype(jnp.bfloat16).reshape(span_rows, HEADS, head_size)
        query_slots, key_slots, value_slots = (
            lax.all_to_all(
                pad_slots(query_heads, slot_total), "queue", split_axis=1, concat_axis=0, tiled=True
            ),
            lax.all_to_all(
                pad_slots(key_heads, slot_total), "queue", split_axis=1, concat_axis=0, tiled=True
            ),
            lax.all_to_all(
                pad_slots(value_heads, slot_total), "queue", split_axis=1, concat_axis=0, tiled=True
            ),
        )
        attended_slots = causal_block(query_slots, key_slots, value_slots, span_rows, score_scale)
        crossed_slots = text_attend(query_slots, text_k_slots, text_v_slots, score_scale)
        attended_back, crossed_back = (
            lax.all_to_all(attended_slots, "queue", split_axis=0, concat_axis=1, tiled=True),
            lax.all_to_all(crossed_slots, "queue", split_axis=0, concat_axis=1, tiled=True),
        )
        attended = attended_back[:, :HEADS]
        crossed = crossed_back[:, :HEADS]
        combined = (
            (attended.astype(jnp.float32) + crossed.astype(jnp.float32))
            .astype(jnp.bfloat16)
            .reshape(span_rows, model_width)
        )
        out_columns = jnp.dot(
            lax.all_gather(combined, "queue", axis=0, tiled=True),
            output_weight,
            preferred_element_type=jnp.float32,
        )
        projected = lax.all_to_all(
            out_columns.astype(jnp.bfloat16), "queue", split_axis=0, concat_axis=1, tiled=True
        ).astype(out_columns.dtype)
        queue_state = (current + modulation[2] * projected).astype(jnp.bfloat16)
    return queue_state


def swapped(value, bit):
    count = lax.axis_size("queue")
    return lax.ppermute(value, "queue", [(source, source ^ bit) for source in range(count)])


def gathered_over_chips(block):
    chips = lax.axis_size("queue") // 2
    blocks = {0: block}
    bits = [1 << b for b in reversed(range(chips.bit_length() - 1))]
    for bit in bits:
        for mask in list(blocks):
            blocks[mask | bit] = swapped(blocks[mask], 2 * bit)
    return [blocks[mask] for mask in range(chips)]


def contract_last(left, right):
    return lax.dot_general(
        left, right, (((1,), (1,)), ((), ())), preferred_element_type=jnp.float32
    )


VMEM_SPEC = pl.BlockSpec(memory_space=pltpu.VMEM)
SMEM_SPEC = pl.BlockSpec(memory_space=pltpu.SMEM)
ANY_SPEC = pl.BlockSpec(memory_space=pl.ANY)


def kernel_params(mebibytes):
    return pltpu.CompilerParams(vmem_limit_bytes=mebibytes * 1024 * 1024)


def span_at(position, step, spans):
    chips = spans // 2
    return (2 * (position % chips) + position // chips + step + 1) % spans


def project_kernel(step, spans, place_ref, shift_ref, scale_ref, gain_ref, incoming_ref, *refs):
    chips = spans // 2
    weight_refs, refs = refs[:3], refs[3:]
    mine, others = refs[:chips], refs[chips : 2 * chips]
    refs = refs[2 * chips :]
    own_ref, send_ref, squares_ref = refs[:3]
    refs = refs[3:]
    if step == 0:
        current_ref, refs = refs[0], refs[1:]
    state, modulated, sems = refs
    chip, core = place_ref[0], place_ref[1]
    tokens, width = modulated.shape
    half = tokens // 2
    rows = tokens // spans
    pair = 2 * rows
    cols = weight_refs[0].shape[0]
    first = core == 0
    copies = []
    for side, blocks in enumerate((mine, others)):
        owner = core if side == 0 else 1 - core
        for mask in range(chips):
            other_chip = chip ^ mask
            if step == 0:
                target = state.at[owner * chips + other_chip]
            else:
                lanes = pl.ds(pl.multiple_of(other_chip * 2 * cols, 2 * cols), 2 * cols)
                target = state.at[pl.ds(pl.multiple_of(owner * half, half), half), lanes]
            copies.append(
                pltpu.make_async_copy(blocks[mask], target, sems.at[side * chips + mask])
            )
    for copy in copies:
        copy.start()
    for copy in copies:
        copy.wait()
    if step == 0:
        state[spans - 1] = incoming_ref[...]
        lanes = pl.ds(pl.multiple_of(chip * 2 * cols, 2 * cols), 2 * cols)
        for slab in range(chips // 2):
            at = core * chips + 2 * slab
            both = [state[at + e, :, lanes].astype(jnp.float32) for e in range(2)]
            current_ref[slab * pair : (slab + 1) * pair, :] = jnp.concatenate(
                both, axis=0
            ).astype(jnp.bfloat16)
    pieces = 4
    piece = width // pieces
    for slab in range(chips):
        band = slice(slab * pair, (slab + 1) * pair)

        def load(part):
            if step == 0:
                both = [state[2 * slab + e, :, part].astype(jnp.float32) for e in range(2)]
                return jnp.concatenate(both, axis=0)
            return state[band, part].astype(jnp.float32)

        total = jnp.zeros((pair, 1), jnp.float32)
        for low in range(0, width, piece):
            x = load(slice(low, low + piece))
            total = total + jnp.sum(x * x, axis=1, keepdims=True)
        factor = lax.rsqrt(total / width + 1e-06)
        at = [span_at(2 * slab + e, step, spans) for e in range(2)]
        for low in range(0, width, piece):
            part = slice(low, low + piece)
            x = load(part) * factor
            scale, shift = (
                jnp.concatenate(
                    [jnp.broadcast_to(ref[s : s + 1, part], (rows, piece)) for s in at], axis=0
                )
                for ref in (scale_ref, shift_ref)
            )
            modulated[band, part] = (x * (1.0 + scale) + shift).astype(jnp.bfloat16)
    for i in range(3):

        def add(step_k, total):
            part = pl.ds(pl.multiple_of(step_k * piece, piece), piece)
            return total + contract_last(weight_refs[i][:, part], modulated[:, part])

        product = lax.fori_loop(0, pieces, add, jnp.zeros((cols, tokens), jnp.float32))
        if i < 2:
            line = jnp.sum(product * product, axis=0, keepdims=True)
            squares_ref[:, i : i + 1, :] = jnp.broadcast_to(line[None], (spans, 1, tokens))
            product = product * gain_ref[:, i : i + 1]
        product = product.T
        if i == 0:
            low, high = product[:half], product[half:]
            own_ref[:half, :] = jnp.where(first, low, high).astype(jnp.bfloat16)
            send_ref[:half, :] = jnp.where(first, high, low).astype(jnp.bfloat16)
        else:
            band = slice(half + (i - 1) * tokens, half + i * tokens)
            own_ref[band, :] = product.astype(jnp.bfloat16)
            send_ref[band, :] = product.astype(jnp.bfloat16)


def project(step, spans, place, shift, scale, gain, incoming, mine, others, weights):
    rows = incoming.shape[0]
    tokens = spans * rows
    cols, width = weights[0].shape
    half = tokens // 2
    own = jax.ShapeDtypeStruct((half + 2 * tokens, cols), jnp.bfloat16)
    out_shape = [own, own, jax.ShapeDtypeStruct((spans, 2, tokens), jnp.float32)]
    if step == 0:
        out_shape.append(jax.ShapeDtypeStruct((half, 2 * cols), jnp.bfloat16))
        state = (spans, rows, width)
    else:
        state = (tokens, width)
    return pl.pallas_call(
        functools.partial(project_kernel, step, spans),
        out_shape=out_shape,
        in_specs=[SMEM_SPEC] + [VMEM_SPEC] * 7 + [ANY_SPEC] * (2 * len(mine)),
        out_specs=[VMEM_SPEC] * len(out_shape),
        scratch_shapes=[
            pltpu.VMEM(state, jnp.bfloat16),
            pltpu.VMEM((tokens, width), jnp.bfloat16),
            pltpu.SemaphoreType.DMA((spans,)),
        ],
        compiler_params=kernel_params(24),
        name="project",
    )(place, shift, scale, gain, incoming, *weights, *mine, *others)


def attend_kernel(
    step, spans, head_size, place_ref, own_ref, got_ref, text_ref, more_ref, squares_ref,
    out_ref, queries, keys, values,
):
    core = place_ref[1]
    first = core == 0
    half, width = queries.shape
    tokens = 2 * half
    rows = tokens // spans
    cols = width // 2
    for target, low, size in (
        (queries, 0, half),
        (keys, half, tokens),
        (values, half + tokens, tokens),
    ):
        mine = own_ref[low : low + size, :]
        other = got_ref[low : low + size, :]
        target[:, :cols] = jnp.where(first, mine, other)
        target[:, cols:] = jnp.where(first, other, mine)
    squares = jnp.sum(squares_ref[...], axis=0)
    factors = lax.rsqrt(squares / (width * (spans // 2)) + 1e-06)
    ident = lax.broadcasted_iota(jnp.int32, (tokens, tokens), 0) == lax.broadcasted_iota(
        jnp.int32, (tokens, tokens), 1
    )
    column = jnp.sum(jnp.where(ident, factors[0:1, :], 0.0), axis=1, keepdims=True)
    column = jnp.where(first, column[:half], column[half:]) * (1.0 / math.sqrt(head_size))
    row = factors[1:2, :]
    shape = (half, tokens)
    own_block = lax.broadcasted_iota(jnp.int32, shape, 0) // rows + core * (spans // 2)
    key_block = lax.broadcasted_iota(jnp.int32, shape, 1) // rows
    allowed = span_at(own_block, step, spans) >= span_at(key_block, step, spans)
    text_rows = text_ref.shape[0] * text_ref.shape[2]
    for head in range(width // head_size):
        lanes = slice(head * head_size, (head + 1) * head_size)
        q = queries[:, lanes]
        scores = contract_last(q, keys[:, lanes]) * column * row
        scores = jnp.where(allowed, scores, -1e30)
        weights = jnp.exp(scores - jnp.max(scores, axis=1, keepdims=True))
        weights = weights / jnp.sum(weights, axis=1, keepdims=True)
        attended = jnp.dot(
            weights.astype(jnp.bfloat16), values[:, lanes], preferred_element_type=jnp.float32
        ).astype(jnp.bfloat16)
        parts = []
        for ref in (text_ref, more_ref):
            text_keys = ref[:, 0, :, lanes].reshape(text_rows, head_size)
            parts.append(contract_last(q, text_keys) * column)
        most = jnp.maximum(
            jnp.max(parts[0], axis=1, keepdims=True), jnp.max(parts[1], axis=1, keepdims=True)
        )
        parts = [jnp.exp(part - most) for part in parts]
        total = jnp.sum(parts[0], axis=1, keepdims=True) + jnp.sum(parts[1], axis=1, keepdims=True)
        crossed = jnp.zeros((half, head_size), jnp.float32)
        for ref, part in zip((text_ref, more_ref), parts):
            text_values = ref[:, 1, :, lanes].reshape(text_rows, head_size)
            crossed = crossed + jnp.dot(
                (part / total).astype(jnp.bfloat16), text_values, preferred_element_type=jnp.float32
            )
        crossed = crossed.astype(jnp.bfloat16)
        out_ref[:, lanes] = (attended.astype(jnp.float32) + crossed.astype(jnp.float32)).astype(
            jnp.bfloat16
        )


def attend(step, spans, head_size, place, own, got, text, more, squares):
    cols = own.shape[1]
    tokens = squares.shape[2]
    half = tokens // 2
    return pl.pallas_call(
        functools.partial(attend_kernel, step, spans, head_size),
        out_shape=jax.ShapeDtypeStruct((half, 2 * cols), jnp.bfloat16),
        in_specs=[SMEM_SPEC] + [VMEM_SPEC] * 5,
        out_specs=VMEM_SPEC,
        scratch_shapes=[
            pltpu.VMEM((half, 2 * cols), jnp.bfloat16),
            pltpu.VMEM((tokens, 2 * cols), jnp.bfloat16),
            pltpu.VMEM((tokens, 2 * cols), jnp.bfloat16),
        ],
        compiler_params=kernel_params(16),
        name="attend",
    )(place, own, got, text, more, squares)


def output_kernel(
    step, spans, last, place_ref, current_ref, gate_ref, incoming_ref, own_ref, other_ref, *refs
):
    chips = spans // 2
    blocks, (out_ref, totals) = refs[:chips], refs[chips:]
    chip, core = place_ref[0], place_ref[1]
    first = core == 0
    half, width = current_ref.shape
    cols = width // 2
    rows = 2 * half // spans
    mine = jnp.zeros((cols, half), jnp.float32)
    other = jnp.zeros((cols, half), jnp.float32)
    for mask in range(chips):
        lanes = pl.ds(pl.multiple_of((chip ^ mask) * width, width), width)
        block = blocks[mask][...]
        mine = mine + contract_last(own_ref[:, lanes], block)
        other = other + contract_last(other_ref[:, lanes], block)
    both = jnp.concatenate([jnp.where(first, mine, other), jnp.where(first, other, mine)], axis=0)
    totals[...] = both.T
    for block in range(chips):
        band = slice(block * rows, (block + 1) * rows)
        places = [span_at(block + e * chips, step, spans) for e in range(2)]
        gates = [gate_ref[s : s + 1, :] for s in places]
        gate = jnp.where(first, gates[0], gates[1])
        totals[band, :] = current_ref[band, :].astype(jnp.float32) + gate * totals[band, :]
    if last:
        for target in range(chips):
            block = (target - STEPS // 2) % chips
            out_ref[target] = totals[block * rows : (block + 1) * rows, :].astype(jnp.bfloat16)
    else:
        parity, block = (spans - 2 - step) % 2, (spans - 2 - step) // 2
        band = slice(block * rows, (block + 1) * rows)
        lanes = pl.ds(pl.multiple_of(chip * width, width), width)
        totals[band, :] = jnp.where(
            core == parity, incoming_ref[:, lanes].astype(jnp.float32), totals[band, :]
        )
        out_ref[...] = totals[...].astype(jnp.bfloat16)


def output(step, spans, last, place, current, gate, incoming, own, other, blocks):
    half, width = current.shape
    chips = spans // 2
    rows = 2 * half // spans
    return pl.pallas_call(
        functools.partial(output_kernel, step, spans, last),
        out_shape=jax.ShapeDtypeStruct(
            (chips, rows, width) if last else (half, width), jnp.bfloat16
        ),
        in_specs=[SMEM_SPEC] + [VMEM_SPEC] * (5 + chips),
        out_specs=VMEM_SPEC,
        scratch_shapes=[pltpu.VMEM((half, width), jnp.float32)],
        compiler_params=kernel_params(16),
        name="output",
    )(place, current, gate, incoming, own, other, *blocks)


def join_kernel(in_ref, out_ref):
    chips, _, width = in_ref.shape
    for source in range(chips):
        out_ref[:, source * width : (source + 1) * width] = in_ref[source]


def join(blocks):
    chips, rows, width = blocks.shape
    return pl.pallas_call(
        join_kernel,
        out_shape=jax.ShapeDtypeStruct((rows, width * chips), jnp.bfloat16),
        in_specs=[VMEM_SPEC],
        out_specs=VMEM_SPEC,
        compiler_params=kernel_params(4),
        name="join",
    )(blocks)


def arrange_kernel(spans, keys_ref, values_ref, out_ref):
    width = out_ref.shape[3]
    text_half = out_ref.shape[2]
    for device in range(spans):
        lanes = slice(device // 2 * width, (device // 2 + 1) * width)
        band = slice(device % 2 * text_half, (device % 2 + 1) * text_half)
        out_ref[device, 0] = keys_ref[band, lanes]
        out_ref[device, 1] = values_ref[band, lanes]


def arrange(spans, keys, values):
    text_half = keys.shape[0] // 2
    return pl.pallas_call(
        functools.partial(arrange_kernel, spans),
        out_shape=jax.ShapeDtypeStruct(
            (spans, 2, text_half, 2 * keys.shape[1] // spans), jnp.bfloat16
        ),
        in_specs=[VMEM_SPEC] * 2,
        out_specs=VMEM_SPEC,
        compiler_params=kernel_params(8),
        name="arrange",
    )(keys, values)


def paired_device(
    hidden,
    incoming,
    levels,
    mod_table,
    query_weight,
    key_weight,
    value_weight,
    output_weight,
    query_gain,
    key_gain,
    text_keys,
    text_values,
):
    own_index = lax.axis_index("queue")
    spans = lax.axis_size("queue")
    chips = spans // 2
    chip, core = own_index // 2, own_index % 2
    width = hidden.shape[1]
    cols = query_weight.shape[1]
    head_size = width // HEADS
    place = jnp.stack([chip, core]).astype(jnp.int32)
    mine = gathered_over_chips(hidden)
    others = [swapped(block, 1) for block in mine]
    picked = (levels[:, None] == jnp.arange(mod_table.shape[0])[None, :]).astype(mod_table.dtype)
    shift, scale, gate = jnp.einsum(
        "sl,ltd->tsd", picked, mod_table, preferred_element_type=jnp.float32
    )
    gate = lax.dynamic_slice_in_dim(gate, chip * 2 * cols, 2 * cols, 1)
    gain = lax.dynamic_slice_in_dim(jnp.stack([query_gain, key_gain]), own_index * cols, cols, 1).T
    weights = [w.T for w in (query_weight, key_weight, value_weight)]
    output_own = output_weight.T
    output_other = swapped(output_own, 1)
    text = arrange(spans, text_keys, text_values)
    text, *mine = lax.optimization_barrier((text, *mine))
    text = lax.all_to_all(text, "queue", split_axis=0, concat_axis=0, tiled=True)
    more = swapped(text, 1)
    current = None
    for step in range(STEPS):
        last = step == STEPS - 1
        own, send, squares, *rest = project(
            step, spans, place, shift, scale, gain, incoming[step], mine, others, weights
        )
        got = swapped(send, 1)
        squares = lax.all_to_all(squares, "queue", split_axis=0, concat_axis=0, tiled=True)
        if step == 0:
            current = rest[0]
            got, output_other = lax.optimization_barrier((got, output_other))
        block = attend(step, spans, head_size, place, own, got, text, more, squares)
        result = output(
            step,
            spans,
            last,
            place,
            current,
            gate,
            incoming[min(step + 1, STEPS - 1)],
            output_own,
            output_other,
            gathered_over_chips(block),
        )
        if not last:
            current = result
            mine = gathered_over_chips(current)
            others = [swapped(block, 1) for block in mine]
    same_core = [[2 * c + core_index for c in range(chips)] for core_index in range(2)]
    result = lax.all_to_all(
        result, "queue", split_axis=0, concat_axis=0, tiled=True, axis_index_groups=same_core
    )
    return join(result)


def held_in_pairs(mesh, hidden, query_weight):
    spans = mesh.shape["queue"]
    rows = hidden.shape[0] // (mesh.shape["groups"] * spans)
    cols = query_weight.shape[1] // spans
    head_size = query_weight.shape[0] // HEADS
    power = spans & (spans - 1) == 0
    return STEPS % 2 == 0 and power and spans >= 4 and 2 * cols % head_size == 0 and rows * spans == 128 and rows == 8


def solution(mesh):
    in_specs = (
        P(("groups", "queue"), None),
        P(None, "groups", None),
        P(),
        P(),
        P(None, "queue"),
        P(None, "queue"),
        P(None, "queue"),
        P(None, "queue"),
        P(),
        P(),
        P(("groups", "queue"), None),
        P(("groups", "queue"), None),
    )
    out_specs = P(("groups", "queue"), None)

    def apply(*args):
        body = paired_device if held_in_pairs(mesh, args[0], args[4]) else per_device
        return jax.shard_map(
            body, mesh=mesh, in_specs=in_specs, out_specs=out_specs, check_vma=False
        )(*args)

    return apply
```

```python
import functools
import math

import jax
import jax.numpy as jnp
from jax import lax
from jax.experimental import pallas as pl
from jax.experimental.pallas import tpu as pltpu
from jax.sharding import PartitionSpec as P

HEADS = 40
STEPS = 2


def passed_along(value, axis, steps):
    count = lax.axis_size(axis)
    initial, last = (max(0, -steps), min(count, count - steps))
    return lax.ppermute(value, axis, [(source, source + steps) for source in range(initial, last)])


def normalize(values):
    return values * lax.rsqrt(jnp.mean(values * values, axis=-1, keepdims=True) + 1e-06)


def softmax_rounded(scores):
    row_max = jnp.max(scores, axis=-1, keepdims=True)
    weights = jnp.exp(scores - row_max)
    return (weights / jnp.sum(weights, axis=-1, keepdims=True)).astype(jnp.bfloat16)


def pad_slots(values, slot_total):
    missing = slot_total - values.shape[1]
    filler = jnp.zeros((values.shape[0], missing, values.shape[2]), values.dtype)
    return jnp.concatenate([values, filler], axis=1)


def causal_block(queries, keys_all, values_all, span_rows, score_scale):
    total_rows = queries.shape[0]
    block_rows = min(512, total_rows)
    scores = (
        jnp.einsum("qsd,ksd->sqk", queries, keys_all, preferred_element_type=jnp.float32)
        * score_scale
    )
    allowed = (
        jnp.arange(0, block_rows)[:, None] // span_rows
        >= jnp.arange(block_rows)[None, :] // span_rows
    )
    scores = jnp.where(allowed[None], scores, -1e30)
    result = jnp.einsum(
        "sqk,ksd->qsd", softmax_rounded(scores), values_all, preferred_element_type=jnp.float32
    )
    pieces = result.astype(jnp.bfloat16)
    return pieces


def text_attend(queries, text_k, text_v, score_scale):
    scores = (
        jnp.einsum("qsd,tsd->sqt", queries, text_k, preferred_element_type=jnp.float32)
        * score_scale
    )
    return jnp.einsum(
        "sqt,tsd->qsd", softmax_rounded(scores), text_v, preferred_element_type=jnp.float32
    ).astype(jnp.bfloat16)


def per_device(
    hidden,
    incoming,
    levels,
    mod_table,
    query_weight,
    key_weight,
    value_weight,
    output_weight,
    query_gain,
    key_gain,
    text_keys,
    text_values,
):
    own_index = lax.axis_index("queue")
    queue_size = lax.axis_size("queue")
    span_rows, model_width = hidden.shape
    head_size = model_width // HEADS
    score_scale = 1.0 / math.sqrt(head_size)
    slot_total = -(-HEADS // queue_size) * queue_size
    own_level = lax.dynamic_index_in_dim(levels, own_index, 0, keepdims=False)
    modulation = lax.dynamic_index_in_dim(mod_table, own_level, 0, keepdims=False).astype(
        jnp.float32
    )
    stacked_weights = jnp.stack([query_weight, key_weight, value_weight])
    text_local = text_keys.shape[0]
    text_k_slots, text_v_slots = (
        lax.all_to_all(
            pad_slots(text_keys.reshape(text_local, HEADS, head_size), slot_total),
            "queue",
            split_axis=1,
            concat_axis=0,
            tiled=True,
        ),
        lax.all_to_all(
            pad_slots(text_values.reshape(text_local, HEADS, head_size), slot_total),
            "queue",
            split_axis=1,
            concat_axis=0,
            tiled=True,
        ),
    )
    queue_state = hidden
    for section_index in range(STEPS):
        shifted = passed_along(queue_state, "queue", 1)
        queue_state = jnp.where(own_index == 0, incoming[section_index], shifted)
        current = queue_state.astype(jnp.float32)
        modulated = (normalize(current) * (1.0 + modulation[1]) + modulation[0]).astype(
            jnp.bfloat16
        )
        columns = jnp.einsum(
            "rd,cdw->crw",
            lax.all_gather(modulated, "queue", axis=0, tiled=True),
            stacked_weights,
            preferred_element_type=jnp.float32,
        )
        own_rows = lax.all_to_all(
            columns.astype(jnp.bfloat16), "queue", split_axis=1, concat_axis=2, tiled=True
        ).astype(columns.dtype)
        query_heads = (
            (normalize(own_rows[0]) * query_gain)
            .astype(jnp.bfloat16)
            .reshape(span_rows, HEADS, head_size)
        )
        key_heads = (
            (normalize(own_rows[1]) * key_gain)
            .astype(jnp.bfloat16)
            .reshape(span_rows, HEADS, head_size)
        )
        value_heads = own_rows[2].astype(jnp.bfloat16).reshape(span_rows, HEADS, head_size)
        query_slots, key_slots, value_slots = (
            lax.all_to_all(
                pad_slots(query_heads, slot_total), "queue", split_axis=1, concat_axis=0, tiled=True
            ),
            lax.all_to_all(
                pad_slots(key_heads, slot_total), "queue", split_axis=1, concat_axis=0, tiled=True
            ),
            lax.all_to_all(
                pad_slots(value_heads, slot_total), "queue", split_axis=1, concat_axis=0, tiled=True
            ),
        )
        attended_slots = causal_block(query_slots, key_slots, value_slots, span_rows, score_scale)
        crossed_slots = text_attend(query_slots, text_k_slots, text_v_slots, score_scale)
        attended_back, crossed_back = (
            lax.all_to_all(attended_slots, "queue", split_axis=0, concat_axis=1, tiled=True),
            lax.all_to_all(crossed_slots, "queue", split_axis=0, concat_axis=1, tiled=True),
        )
        attended = attended_back[:, :HEADS]
        crossed = crossed_back[:, :HEADS]
        combined = (
            (attended.astype(jnp.float32) + crossed.astype(jnp.float32))
            .astype(jnp.bfloat16)
            .reshape(span_rows, model_width)
        )
        out_columns = jnp.dot(
            lax.all_gather(combined, "queue", axis=0, tiled=True),
            output_weight,
            preferred_element_type=jnp.float32,
        )
        projected = lax.all_to_all(
            out_columns.astype(jnp.bfloat16), "queue", split_axis=0, concat_axis=1, tiled=True
        ).astype(out_columns.dtype)
        queue_state = (current + modulation[2] * projected).astype(jnp.bfloat16)
    return queue_state


def swapped(value, bit):
    count = lax.axis_size("queue")
    return lax.ppermute(value, "queue", [(source, source ^ bit) for source in range(count)])


def gathered_over_chips(block):
    chips = lax.axis_size("queue") // 2
    blocks = {0: block}
    bits = [1 << b for b in reversed(range(chips.bit_length() - 1))]
    for bit in bits:
        for mask in list(blocks):
            blocks[mask | bit] = swapped(blocks[mask], 2 * bit)
    return [blocks[mask] for mask in range(chips)]


def contract_last(left, right):
    return lax.dot_general(
        left, right, (((1,), (1,)), ((), ())), preferred_element_type=jnp.float32
    )


VMEM_SPEC = pl.BlockSpec(memory_space=pltpu.VMEM)
SMEM_SPEC = pl.BlockSpec(memory_space=pltpu.SMEM)
HBM_SPEC = pl.BlockSpec(memory_space=pltpu.HBM)


def kernel_params(mebibytes):
    return pltpu.CompilerParams(vmem_limit_bytes=mebibytes * 1024 * 1024)


def span_at(position, step, spans):
    chips = spans // 2
    return (2 * (position % chips) + position // chips + step + 1) % spans


def project_kernel(step, spans, place_ref, gain_ref, table_ref, incoming_ref, *refs):
    chips = spans // 2
    weight_refs, refs = refs[:3], refs[3:]
    mine, others = refs[:chips], refs[chips : 2 * chips]
    refs = refs[2 * chips :]
    own_ref, send_ref, squares_ref = refs[:3]
    refs = refs[3:]
    if step == 0:
        current_ref, refs = refs[0], refs[1:]
    state, modulated, table, entering, shift_ref, scale_ref, weights, sems = refs
    chip, core = place_ref[0], place_ref[1]
    tokens, width = modulated.shape
    half = tokens // 2
    rows = tokens // spans
    pair = 2 * rows
    cols = weight_refs[0].shape[0]
    first = core == 0
    copies = [pltpu.make_async_copy(table_ref, table, sems.at[spans])]
    if step == 0:
        copies.append(pltpu.make_async_copy(incoming_ref, entering, sems.at[spans + 1]))
    for side, blocks in enumerate((mine, others)):
        owner = core if side == 0 else 1 - core
        for mask in range(chips):
            other_chip = chip ^ mask
            if step == 0:
                target = state.at[owner * chips + other_chip]
            else:
                lanes = pl.ds(pl.multiple_of(other_chip * 2 * cols, 2 * cols), 2 * cols)
                target = state.at[pl.ds(pl.multiple_of(owner * half, half), half), lanes]
            copies.append(
                pltpu.make_async_copy(blocks[mask], target, sems.at[side * chips + mask])
            )
    fetches = [
        pltpu.make_async_copy(weight_refs[i], weights.at[i], sems.at[spans + 2 + i])
        for i in range(3)
    ]
    for copy in copies + fetches:
        copy.start()
    for copy in copies:
        copy.wait()
    shift_ref[...] = table[0].astype(jnp.float32)
    scale_ref[...] = table[1].astype(jnp.float32) + 1.0
    if step == 0:
        state[spans - 1] = entering[step]
        lanes = pl.ds(pl.multiple_of(chip * 2 * cols, 2 * cols), 2 * cols)
        for slab in range(chips // 2):
            at = core * chips + 2 * slab
            both = [state[at + e, :, lanes].astype(jnp.float32) for e in range(2)]
            current_ref[slab * pair : (slab + 1) * pair, :] = jnp.concatenate(
                both, axis=0
            ).astype(jnp.bfloat16)
    pieces = 4
    piece = width // pieces
    for slab in range(chips):
        band = slice(slab * pair, (slab + 1) * pair)

        def load(part):
            if step == 0:
                both = [state[2 * slab + e, :, part].astype(jnp.float32) for e in range(2)]
                return jnp.concatenate(both, axis=0)
            return state[band, part].astype(jnp.float32)

        total = jnp.zeros((pair, 1), jnp.float32)
        for low in range(0, width, piece):
            x = load(slice(low, low + piece))
            total = total + jnp.sum(x * x, axis=1, keepdims=True)
        factor = lax.rsqrt(total / width + 1e-06)
        at = [span_at(2 * slab + e, step, spans) for e in range(2)]
        for low in range(0, width, piece):
            part = slice(low, low + piece)
            x = load(part) * factor
            scale, shift = (
                jnp.concatenate(
                    [jnp.broadcast_to(ref[s : s + 1, part], (rows, piece)) for s in at], axis=0
                )
                for ref in (scale_ref, shift_ref)
            )
            modulated[band, part] = (x * scale + shift).astype(jnp.bfloat16)
    for i in range(3):
        fetches[i].wait()

        def add(step_k, total):
            part = pl.ds(pl.multiple_of(step_k * piece, piece), piece)
            return total + contract_last(weights[i, :, part], modulated[:, part])

        product = lax.fori_loop(0, pieces, add, jnp.zeros((cols, tokens), jnp.float32))
        if i < 2:
            line = jnp.sum(product * product, axis=0, keepdims=True)
            squares_ref[:, i : i + 1, :] = jnp.broadcast_to(line[None], (spans, 1, tokens))
            product = product * gain_ref[:, i : i + 1]
        product = product.T
        if i == 0:
            low, high = product[:half], product[half:]
            own_ref[:half, :] = jnp.where(first, low, high).astype(jnp.bfloat16)
            send_ref[:half, :] = jnp.where(first, high, low).astype(jnp.bfloat16)
        else:
            band = slice(half + (i - 1) * tokens, half + i * tokens)
            own_ref[band, :] = product.astype(jnp.bfloat16)
            send_ref[band, :] = product.astype(jnp.bfloat16)


def project(step, spans, place, gain, table, incoming, mine, others, weights):
    rows = incoming.shape[1]
    tokens = spans * rows
    cols, width = weights[0].shape
    half = tokens // 2
    own = jax.ShapeDtypeStruct((half + 2 * tokens, cols), jnp.bfloat16)
    out_shape = [own, own, jax.ShapeDtypeStruct((spans, 2, tokens), jnp.float32)]
    if step == 0:
        out_shape.append(jax.ShapeDtypeStruct((half, 2 * cols), jnp.bfloat16))
        state = (spans, rows, width)
    else:
        state = (tokens, width)
    return pl.pallas_call(
        functools.partial(project_kernel, step, spans),
        out_shape=out_shape,
        in_specs=[SMEM_SPEC, VMEM_SPEC] + [HBM_SPEC] * (5 + 2 * len(mine)),
        out_specs=[VMEM_SPEC] * len(out_shape),
        scratch_shapes=[
            pltpu.VMEM(state, jnp.bfloat16),
            pltpu.VMEM((tokens, width), jnp.bfloat16),
            pltpu.VMEM(table.shape, jnp.bfloat16),
            pltpu.VMEM(incoming.shape, jnp.bfloat16),
            pltpu.VMEM((spans, width), jnp.float32),
            pltpu.VMEM((spans, width), jnp.float32),
            pltpu.VMEM((3, cols, width), jnp.bfloat16),
            pltpu.SemaphoreType.DMA((spans + 5,)),
        ],
        compiler_params=kernel_params(24),
        name="project",
    )(place, gain, table, incoming, *weights, *mine, *others)


def attend_kernel(
    step, spans, head_size, place_ref, own_ref, got_ref, squares_ref, text_hbm, more_hbm,
    out_ref, queries, keys, values, text_ref, more_ref, sems,
):
    copies = [
        pltpu.make_async_copy(text_hbm, text_ref, sems.at[0]),
        pltpu.make_async_copy(more_hbm, more_ref, sems.at[1]),
    ]
    for copy in copies:
        copy.start()
    core = place_ref[1]
    first = core == 0
    half, width = queries.shape
    tokens = 2 * half
    rows = tokens // spans
    cols = width // 2
    for target, low, size in (
        (queries, 0, half),
        (keys, half, tokens),
        (values, half + tokens, tokens),
    ):
        mine = own_ref[low : low + size, :]
        other = got_ref[low : low + size, :]
        target[:, :cols] = jnp.where(first, mine, other)
        target[:, cols:] = jnp.where(first, other, mine)
    squares = jnp.sum(squares_ref[...], axis=0)
    factors = lax.rsqrt(squares / (width * (spans // 2)) + 1e-06)
    ident = lax.broadcasted_iota(jnp.int32, (tokens, tokens), 0) == lax.broadcasted_iota(
        jnp.int32, (tokens, tokens), 1
    )
    column = jnp.sum(jnp.where(ident, factors[0:1, :], 0.0), axis=1, keepdims=True)
    column = jnp.where(first, column[:half], column[half:]) * (1.0 / math.sqrt(head_size))
    row = factors[1:2, :]
    shape = (half, tokens)
    own_block = lax.broadcasted_iota(jnp.int32, shape, 0) // rows + core * (spans // 2)
    key_block = lax.broadcasted_iota(jnp.int32, shape, 1) // rows
    allowed = span_at(own_block, step, spans) >= span_at(key_block, step, spans)
    text_rows = text_ref.shape[0] * text_ref.shape[2]
    for copy in copies:
        copy.wait()
    for head in range(width // head_size):
        lanes = slice(head * head_size, (head + 1) * head_size)
        q = queries[:, lanes]
        scores = contract_last(q, keys[:, lanes]) * column * row
        scores = jnp.where(allowed, scores, -1e30)
        weights = jnp.exp(scores - jnp.max(scores, axis=1, keepdims=True))
        weights = weights / jnp.sum(weights, axis=1, keepdims=True)
        attended = jnp.dot(
            weights.astype(jnp.bfloat16), values[:, lanes], preferred_element_type=jnp.float32
        ).astype(jnp.bfloat16)
        parts = []
        for ref in (text_ref, more_ref):
            text_keys = ref[:, 0, :, lanes].reshape(text_rows, head_size)
            parts.append(contract_last(q, text_keys) * column)
        most = jnp.maximum(
            jnp.max(parts[0], axis=1, keepdims=True), jnp.max(parts[1], axis=1, keepdims=True)
        )
        parts = [jnp.exp(part - most) for part in parts]
        total = jnp.sum(parts[0], axis=1, keepdims=True) + jnp.sum(parts[1], axis=1, keepdims=True)
        crossed = jnp.zeros((half, head_size), jnp.float32)
        for ref, part in zip((text_ref, more_ref), parts):
            text_values = ref[:, 1, :, lanes].reshape(text_rows, head_size)
            crossed = crossed + jnp.dot(
                (part / total).astype(jnp.bfloat16), text_values, preferred_element_type=jnp.float32
            )
        crossed = crossed.astype(jnp.bfloat16)
        out_ref[:, lanes] = (attended.astype(jnp.float32) + crossed.astype(jnp.float32)).astype(
            jnp.bfloat16
        )


def attend(step, spans, head_size, place, own, got, text, more, squares):
    cols = own.shape[1]
    tokens = squares.shape[2]
    half = tokens // 2
    return pl.pallas_call(
        functools.partial(attend_kernel, step, spans, head_size),
        out_shape=jax.ShapeDtypeStruct((half, 2 * cols), jnp.bfloat16),
        in_specs=[SMEM_SPEC] + [VMEM_SPEC] * 3 + [HBM_SPEC] * 2,
        out_specs=VMEM_SPEC,
        scratch_shapes=[
            pltpu.VMEM((half, 2 * cols), jnp.bfloat16),
            pltpu.VMEM((tokens, 2 * cols), jnp.bfloat16),
            pltpu.VMEM((tokens, 2 * cols), jnp.bfloat16),
            pltpu.VMEM(text.shape, jnp.bfloat16),
            pltpu.VMEM(more.shape, jnp.bfloat16),
            pltpu.SemaphoreType.DMA((2,)),
        ],
        compiler_params=kernel_params(16),
        name="attend",
    )(place, own, got, squares, text, more)


def output_kernel(
    step, spans, last, place_ref, current_ref, gate_ref, incoming_ref, own_ref, other_ref, *refs
):
    chips = spans // 2
    blocks, (out_ref, totals, weights, sems) = refs[:chips], refs[chips:]
    chip, core = place_ref[0], place_ref[1]
    first = core == 0
    half, width = current_ref.shape
    cols = width // 2
    rows = 2 * half // spans
    fetches = []
    for mask in range(chips):
        lanes = pl.ds(pl.multiple_of((chip ^ mask) * width, width), width)
        for side, ref in enumerate((own_ref, other_ref)):
            fetches.append(
                pltpu.make_async_copy(
                    ref.at[:, lanes], weights.at[mask, side], sems.at[mask, side]
                )
            )
    for fetch in fetches:
        fetch.start()
    mine = jnp.zeros((half, cols), jnp.float32)
    other = jnp.zeros((half, cols), jnp.float32)
    for mask in range(chips):
        block = blocks[mask][...]
        fetches[2 * mask].wait()
        mine = mine + contract_last(block, weights[mask, 0])
        fetches[2 * mask + 1].wait()
        other = other + contract_last(block, weights[mask, 1])
    totals[:, :cols] = jnp.where(first, mine, other)
    totals[:, cols:] = jnp.where(first, other, mine)
    for block in range(chips):
        band = slice(block * rows, (block + 1) * rows)
        places = [span_at(block + e * chips, step, spans) for e in range(2)]
        gates = [gate_ref[s : s + 1, :] for s in places]
        gate = jnp.where(first, gates[0], gates[1])
        totals[band, :] = current_ref[band, :].astype(jnp.float32) + gate * totals[band, :]
    if last:
        for target in range(chips):
            block = (target - STEPS // 2) % chips
            out_ref[target] = totals[block * rows : (block + 1) * rows, :].astype(jnp.bfloat16)
    else:
        parity, block = (spans - 2 - step) % 2, (spans - 2 - step) // 2
        band = slice(block * rows, (block + 1) * rows)
        lanes = pl.ds(pl.multiple_of(chip * width, width), width)
        totals[band, :] = jnp.where(
            core == parity, incoming_ref[:, lanes].astype(jnp.float32), totals[band, :]
        )
        out_ref[...] = totals[...].astype(jnp.bfloat16)


def output(step, spans, last, place, current, gate, incoming, own, other, blocks):
    half, width = current.shape
    chips = spans // 2
    rows = 2 * half // spans
    return pl.pallas_call(
        functools.partial(output_kernel, step, spans, last),
        out_shape=jax.ShapeDtypeStruct(
            (chips, rows, width) if last else (half, width), jnp.bfloat16
        ),
        in_specs=[SMEM_SPEC] + [VMEM_SPEC] * 3 + [HBM_SPEC] * 2 + [VMEM_SPEC] * chips,
        out_specs=VMEM_SPEC,
        scratch_shapes=[
            pltpu.VMEM((half, width), jnp.float32),
            pltpu.VMEM((chips, 2, width // 2, width), jnp.bfloat16),
            pltpu.SemaphoreType.DMA((chips, 2)),
        ],
        compiler_params=kernel_params(16),
        name="output",
    )(place, current, gate, incoming, own, other, *blocks)


def join_kernel(in_ref, out_ref):
    chips, _, width = in_ref.shape
    for source in range(chips):
        out_ref[:, source * width : (source + 1) * width] = in_ref[source]


def join(blocks):
    chips, rows, width = blocks.shape
    return pl.pallas_call(
        join_kernel,
        out_shape=jax.ShapeDtypeStruct((rows, width * chips), jnp.bfloat16),
        in_specs=[VMEM_SPEC],
        out_specs=VMEM_SPEC,
        compiler_params=kernel_params(4),
        name="join",
    )(blocks)


def arrange_kernel(spans, keys_ref, values_ref, out_ref):
    width = out_ref.shape[3]
    text_half = out_ref.shape[2]
    for device in range(spans):
        lanes = slice(device // 2 * width, (device // 2 + 1) * width)
        band = slice(device % 2 * text_half, (device % 2 + 1) * text_half)
        out_ref[device, 0] = keys_ref[band, lanes]
        out_ref[device, 1] = values_ref[band, lanes]


def arrange(spans, keys, values):
    text_half = keys.shape[0] // 2
    return pl.pallas_call(
        functools.partial(arrange_kernel, spans),
        out_shape=jax.ShapeDtypeStruct(
            (spans, 2, text_half, 2 * keys.shape[1] // spans), jnp.bfloat16
        ),
        in_specs=[VMEM_SPEC] * 2,
        out_specs=VMEM_SPEC,
        compiler_params=kernel_params(8),
        name="arrange",
    )(keys, values)


def paired_device(
    hidden,
    incoming,
    levels,
    mod_table,
    query_weight,
    key_weight,
    value_weight,
    output_weight,
    query_gain,
    key_gain,
    text_keys,
    text_values,
):
    own_index = lax.axis_index("queue")
    spans = lax.axis_size("queue")
    chips = spans // 2
    chip, core = own_index // 2, own_index % 2
    width = hidden.shape[1]
    cols = query_weight.shape[1]
    head_size = width // HEADS
    place = jnp.stack([chip, core]).astype(jnp.int32)
    mine = gathered_over_chips(hidden)
    others = [swapped(block, 1) for block in mine]
    picked = (levels[:, None] == jnp.arange(mod_table.shape[0])[None, :]).astype(mod_table.dtype)
    table = jnp.einsum("sl,ltd->tsd", picked, mod_table, preferred_element_type=jnp.float32)
    table = table.astype(jnp.bfloat16)
    gate = lax.dynamic_slice_in_dim(table[2], chip * 2 * cols, 2 * cols, 1).astype(jnp.float32)
    gain = lax.dynamic_slice_in_dim(jnp.stack([query_gain, key_gain]), own_index * cols, cols, 1).T
    weights = [w.T for w in (query_weight, key_weight, value_weight)]
    output_own = output_weight.T
    output_other = swapped(output_own, 1)
    text = arrange(spans, text_keys, text_values)
    text = lax.optimization_barrier((text, *mine))[0]
    text = lax.all_to_all(text, "queue", split_axis=0, concat_axis=0, tiled=True)
    current = None
    for step in range(STEPS):
        last = step == STEPS - 1
        own, send, squares, *rest = project(
            step, spans, place, gain, table, incoming, mine, others, weights
        )
        got = swapped(send, 1)
        squares = lax.all_to_all(squares, "queue", split_axis=0, concat_axis=0, tiled=True)
        if step == 0:
            current = rest[0]
            text = lax.optimization_barrier((text, send))[0]
            more = swapped(text, 1)
        block = attend(step, spans, head_size, place, own, got, text, more, squares)
        result = output(
            step,
            spans,
            last,
            place,
            current,
            gate,
            incoming[min(step + 1, STEPS - 1)],
            output_own,
            output_other,
            gathered_over_chips(block),
        )
        if not last:
            current = result
            mine = gathered_over_chips(current)
            others = [swapped(block, 1) for block in mine]
    same_core = [[2 * c + core_index for c in range(chips)] for core_index in range(2)]
    result = lax.all_to_all(
        result, "queue", split_axis=0, concat_axis=0, tiled=True, axis_index_groups=same_core
    )
    return join(result)


def held_in_pairs(mesh, hidden, query_weight):
    spans = mesh.shape["queue"]
    rows = hidden.shape[0] // (mesh.shape["groups"] * spans)
    cols = query_weight.shape[1] // spans
    head_size = query_weight.shape[0] // HEADS
    power = spans & (spans - 1) == 0
    return STEPS % 2 == 0 and power and spans >= 4 and 2 * cols % head_size == 0 and rows * spans == 128 and rows == 8


def solution(mesh):
    in_specs = (
        P(("groups", "queue"), None),
        P(None, "groups", None),
        P(),
        P(),
        P(None, "queue"),
        P(None, "queue"),
        P(None, "queue"),
        P(None, "queue"),
        P(),
        P(),
        P(("groups", "queue"), None),
        P(("groups", "queue"), None),
    )
    out_specs = P(("groups", "queue"), None)

    def apply(*args):
        body = paired_device if held_in_pairs(mesh, args[0], args[4]) else per_device
        return jax.shard_map(
            body, mesh=mesh, in_specs=in_specs, out_specs=out_specs, check_vma=False
        )(*args)

    return apply
```

```python
import functools
import math

import jax
import jax.numpy as jnp
from jax import lax
from jax.experimental import pallas as pl
from jax.experimental.pallas import tpu as pltpu
from jax.sharding import PartitionSpec as P

HEADS = 40
STEPS = 2


def passed_along(value, axis, steps):
    count = lax.axis_size(axis)
    initial, last = (max(0, -steps), min(count, count - steps))
    return lax.ppermute(value, axis, [(source, source + steps) for source in range(initial, last)])


def normalize(values):
    return values * lax.rsqrt(jnp.mean(values * values, axis=-1, keepdims=True) + 1e-06)


def softmax_rounded(scores):
    row_max = jnp.max(scores, axis=-1, keepdims=True)
    weights = jnp.exp(scores - row_max)
    return (weights / jnp.sum(weights, axis=-1, keepdims=True)).astype(jnp.bfloat16)


def pad_slots(values, slot_total):
    missing = slot_total - values.shape[1]
    filler = jnp.zeros((values.shape[0], missing, values.shape[2]), values.dtype)
    return jnp.concatenate([values, filler], axis=1)


def causal_block(queries, keys_all, values_all, span_rows, score_scale):
    total_rows = queries.shape[0]
    block_rows = min(512, total_rows)
    scores = (
        jnp.einsum("qsd,ksd->sqk", queries, keys_all, preferred_element_type=jnp.float32)
        * score_scale
    )
    allowed = (
        jnp.arange(0, block_rows)[:, None] // span_rows
        >= jnp.arange(block_rows)[None, :] // span_rows
    )
    scores = jnp.where(allowed[None], scores, -1e30)
    result = jnp.einsum(
        "sqk,ksd->qsd", softmax_rounded(scores), values_all, preferred_element_type=jnp.float32
    )
    pieces = result.astype(jnp.bfloat16)
    return pieces


def text_attend(queries, text_k, text_v, score_scale):
    scores = (
        jnp.einsum("qsd,tsd->sqt", queries, text_k, preferred_element_type=jnp.float32)
        * score_scale
    )
    return jnp.einsum(
        "sqt,tsd->qsd", softmax_rounded(scores), text_v, preferred_element_type=jnp.float32
    ).astype(jnp.bfloat16)


def per_device(
    hidden,
    incoming,
    levels,
    mod_table,
    query_weight,
    key_weight,
    value_weight,
    output_weight,
    query_gain,
    key_gain,
    text_keys,
    text_values,
):
    own_index = lax.axis_index("queue")
    queue_size = lax.axis_size("queue")
    span_rows, model_width = hidden.shape
    head_size = model_width // HEADS
    score_scale = 1.0 / math.sqrt(head_size)
    slot_total = -(-HEADS // queue_size) * queue_size
    own_level = lax.dynamic_index_in_dim(levels, own_index, 0, keepdims=False)
    modulation = lax.dynamic_index_in_dim(mod_table, own_level, 0, keepdims=False).astype(
        jnp.float32
    )
    stacked_weights = jnp.stack([query_weight, key_weight, value_weight])
    text_local = text_keys.shape[0]
    text_k_slots, text_v_slots = (
        lax.all_to_all(
            pad_slots(text_keys.reshape(text_local, HEADS, head_size), slot_total),
            "queue",
            split_axis=1,
            concat_axis=0,
            tiled=True,
        ),
        lax.all_to_all(
            pad_slots(text_values.reshape(text_local, HEADS, head_size), slot_total),
            "queue",
            split_axis=1,
            concat_axis=0,
            tiled=True,
        ),
    )
    queue_state = hidden
    for section_index in range(STEPS):
        shifted = passed_along(queue_state, "queue", 1)
        queue_state = jnp.where(own_index == 0, incoming[section_index], shifted)
        current = queue_state.astype(jnp.float32)
        modulated = (normalize(current) * (1.0 + modulation[1]) + modulation[0]).astype(
            jnp.bfloat16
        )
        columns = jnp.einsum(
            "rd,cdw->crw",
            lax.all_gather(modulated, "queue", axis=0, tiled=True),
            stacked_weights,
            preferred_element_type=jnp.float32,
        )
        own_rows = lax.all_to_all(
            columns.astype(jnp.bfloat16), "queue", split_axis=1, concat_axis=2, tiled=True
        ).astype(columns.dtype)
        query_heads = (
            (normalize(own_rows[0]) * query_gain)
            .astype(jnp.bfloat16)
            .reshape(span_rows, HEADS, head_size)
        )
        key_heads = (
            (normalize(own_rows[1]) * key_gain)
            .astype(jnp.bfloat16)
            .reshape(span_rows, HEADS, head_size)
        )
        value_heads = own_rows[2].astype(jnp.bfloat16).reshape(span_rows, HEADS, head_size)
        query_slots, key_slots, value_slots = (
            lax.all_to_all(
                pad_slots(query_heads, slot_total), "queue", split_axis=1, concat_axis=0, tiled=True
            ),
            lax.all_to_all(
                pad_slots(key_heads, slot_total), "queue", split_axis=1, concat_axis=0, tiled=True
            ),
            lax.all_to_all(
                pad_slots(value_heads, slot_total), "queue", split_axis=1, concat_axis=0, tiled=True
            ),
        )
        attended_slots = causal_block(query_slots, key_slots, value_slots, span_rows, score_scale)
        crossed_slots = text_attend(query_slots, text_k_slots, text_v_slots, score_scale)
        attended_back, crossed_back = (
            lax.all_to_all(attended_slots, "queue", split_axis=0, concat_axis=1, tiled=True),
            lax.all_to_all(crossed_slots, "queue", split_axis=0, concat_axis=1, tiled=True),
        )
        attended = attended_back[:, :HEADS]
        crossed = crossed_back[:, :HEADS]
        combined = (
            (attended.astype(jnp.float32) + crossed.astype(jnp.float32))
            .astype(jnp.bfloat16)
            .reshape(span_rows, model_width)
        )
        out_columns = jnp.dot(
            lax.all_gather(combined, "queue", axis=0, tiled=True),
            output_weight,
            preferred_element_type=jnp.float32,
        )
        projected = lax.all_to_all(
            out_columns.astype(jnp.bfloat16), "queue", split_axis=0, concat_axis=1, tiled=True
        ).astype(out_columns.dtype)
        queue_state = (current + modulation[2] * projected).astype(jnp.bfloat16)
    return queue_state


def swapped(value, bit):
    count = lax.axis_size("queue")
    return lax.ppermute(value, "queue", [(source, source ^ bit) for source in range(count)])


def gathered_over_chips(block):
    chips = lax.axis_size("queue") // 2
    blocks = {0: block}
    for mask in range(2, chips, 2):
        blocks[mask] = swapped(block, 2 * mask)
    for mask in range(0, chips, 2):
        blocks[mask + 1] = swapped(blocks[mask], 2)
    return [blocks[mask] for mask in range(chips)]


def contract_last(left, right):
    return lax.dot_general(
        left, right, (((1,), (1,)), ((), ())), preferred_element_type=jnp.float32
    )


HBM_SPEC = pl.BlockSpec(memory_space=pltpu.HBM)
VMEM_SPEC = pl.BlockSpec(memory_space=pltpu.VMEM)
PARAMS = pltpu.CompilerParams(vmem_limit_bytes=60 * 1024 * 1024)


def span_at(position, step, spans):
    chips = spans // 2
    return (2 * (position % chips) + position // chips + step + 1) % spans


def own_place():
    own_index = lax.axis_index("queue")
    return own_index // 2, own_index % 2


def started(pairs, sems):
    copies = [
        pltpu.make_async_copy(source, target, sems.at[i]) for i, (source, target) in enumerate(pairs)
    ]
    for copy in copies:
        copy.start()
    return copies


def finished(copies):
    for copy in copies:
        copy.wait()


def project_kernel(step, spans, gain_hbm, table_hbm, incoming_hbm, *refs):
    chips = spans // 2
    weight_refs, refs = refs[:3], refs[3:]
    mine, others = refs[:chips], refs[chips : 2 * chips]
    refs = refs[2 * chips :]
    own_hbm, send_hbm, squares_ref = refs[:3]
    refs = refs[3:]
    if step == 0:
        current_hbm, refs = refs[0], refs[1:]
    state, modulated, table, entering, gain, scale_ref, shift_ref, weights, own, send, current, sems = refs
    chip, core = own_place()
    tokens, width = modulated.shape
    half = tokens // 2
    rows = tokens // spans
    pair = 2 * rows
    cols = weight_refs[0].shape[0]
    first = core == 0
    own_lanes = pl.ds(pl.multiple_of(chip * 2 * cols, 2 * cols), 2 * cols)
    pairs = []
    for side, blocks in enumerate((mine, others)):
        owner = core if side == 0 else 1 - core
        for mask in range(chips):
            other_chip = chip ^ mask
            if step == 0:
                target = state.at[owner * chips + other_chip]
            else:
                lanes = pl.ds(pl.multiple_of(other_chip * 2 * cols, 2 * cols), 2 * cols)
                target = state.at[pl.ds(pl.multiple_of(owner * half, half), half), lanes]
            pairs.append((blocks[mask], target))
    pairs += [(table_hbm, table), (gain_hbm.at[:, own_lanes], gain), (incoming_hbm, entering)]
    pairs += [(weight_refs[i], weights.at[i]) for i in range(3)]
    copies = started(pairs, sems)
    copies, fetches = copies[:-3], copies[-3:]
    finished(copies)
    shift_ref[...] = table[0].astype(jnp.float32)
    scale_ref[...] = table[1].astype(jnp.float32) + 1.0
    leaving = []
    if step == 0:
        state[spans - 1] = entering[step]
        for slab in range(chips // 2):
            at = core * chips + 2 * slab
            both = [state[at + e, :, own_lanes].astype(jnp.float32) for e in range(2)]
            current[slab * pair : (slab + 1) * pair, :] = jnp.concatenate(both, axis=0).astype(
                jnp.bfloat16
            )
        leaving += started([(current, current_hbm)], sems.at[pl.ds(0, 1)])
    pieces = 4
    piece = width // pieces
    for slab in range(chips):
        band = slice(slab * pair, (slab + 1) * pair)

        def load(part):
            if step == 0:
                both = [state[2 * slab + e, :, part].astype(jnp.float32) for e in range(2)]
                return jnp.concatenate(both, axis=0)
            return state[band, part].astype(jnp.float32)

        total = jnp.zeros((pair, 1), jnp.float32)
        for low in range(0, width, piece):
            x = load(slice(low, low + piece))
            total = total + jnp.sum(x * x, axis=1, keepdims=True)
        factor = lax.rsqrt(total / width + 1e-06)
        at = [span_at(2 * slab + e, step, spans) for e in range(2)]
        for low in range(0, width, piece):
            part = slice(low, low + piece)
            x = load(part) * factor
            scale, shift = (
                jnp.concatenate(
                    [jnp.broadcast_to(ref[s : s + 1, part], (rows, piece)) for s in at], axis=0
                )
                for ref in (scale_ref, shift_ref)
            )
            modulated[band, part] = (x * scale + shift).astype(jnp.bfloat16)
    ident = lax.broadcasted_iota(jnp.int32, (tokens, tokens), 0) == lax.broadcasted_iota(
        jnp.int32, (tokens, tokens), 1
    )
    for i in range(3):
        fetches[i].wait()
        product = contract_last(modulated[...], weights[i])
        if i < 2:
            column = jnp.sum(product * product, axis=1, keepdims=True)
            line = jnp.sum(jnp.where(ident, column, 0.0), axis=0, keepdims=True)
            squares_ref[:, i : i + 1, :] = jnp.broadcast_to(line[None], (spans, 1, tokens))
            line = gain[i : i + 1, :]
            product = product * jnp.where(first, line[:, :cols], line[:, cols:])
        if i == 0:
            low, high = product[:half], product[half:]
            own[...] = jnp.where(first, low, high).astype(jnp.bfloat16)
            send[:half, :] = jnp.where(first, high, low).astype(jnp.bfloat16)
            leaving += started(
                [(own, own_hbm), (send.at[pl.ds(0, half)], send_hbm.at[pl.ds(0, half)])],
                sems.at[pl.ds(1, 2)],
            )
        else:
            band = pl.ds(half + (i - 1) * tokens, tokens)
            send[band, :] = product.astype(jnp.bfloat16)
            leaving += started([(send.at[band], send_hbm.at[band])], sems.at[pl.ds(2 + i, 1)])
    finished(leaving)


def project(step, spans, gain, table, incoming, mine, others, weights):
    rows = incoming.shape[1]
    tokens = spans * rows
    cols, width = weights[0].shape
    half = tokens // 2
    out_shape = [
        jax.ShapeDtypeStruct((half, cols), jnp.bfloat16),
        jax.ShapeDtypeStruct((half + 2 * tokens, cols), jnp.bfloat16),
        jax.ShapeDtypeStruct((spans, 2, tokens), jnp.float32),
    ]
    if step == 0:
        out_shape.append(jax.ShapeDtypeStruct((half, 2 * cols), jnp.bfloat16))
        state = (spans, rows, width)
    else:
        state = (tokens, width)
    return pl.pallas_call(
        functools.partial(project_kernel, step, spans),
        out_shape=out_shape,
        in_specs=[HBM_SPEC] * (6 + 2 * len(mine)),
        out_specs=[HBM_SPEC, HBM_SPEC, VMEM_SPEC, HBM_SPEC][: len(out_shape)],
        scratch_shapes=[
            pltpu.VMEM(state, jnp.bfloat16),
            pltpu.VMEM((tokens, width), jnp.bfloat16),
            pltpu.VMEM(table.shape, jnp.bfloat16),
            pltpu.VMEM(incoming.shape, jnp.bfloat16),
            pltpu.VMEM((2, 2 * cols), jnp.float32),
            pltpu.VMEM((spans, width), jnp.float32),
            pltpu.VMEM((spans, width), jnp.float32),
            pltpu.VMEM((3, cols, width), jnp.bfloat16),
            pltpu.VMEM((half, cols), jnp.bfloat16),
            pltpu.VMEM((half + 2 * tokens, cols), jnp.bfloat16),
            pltpu.VMEM((half, 2 * cols), jnp.bfloat16),
            pltpu.SemaphoreType.DMA((spans + 6,)),
        ],
        compiler_params=PARAMS,
        name="project",
    )(gain, table, incoming, *weights, *mine, *others)


def attend_kernel(
    step, spans, head_size, own_hbm, sent_hbm, got_hbm, squares_hbm, text_hbm, more_hbm,
    out_ref, own, sent, got, squares_ref, queries, keys, values, text_ref, more_ref, sems,
):
    copies = started(
        [
            (own_hbm, own),
            (sent_hbm, sent),
            (got_hbm, got),
            (squares_hbm, squares_ref),
            (text_hbm, text_ref),
            (more_hbm, more_ref),
        ],
        sems,
    )
    chip, core = own_place()
    first = core == 0
    half, width = queries.shape
    tokens = 2 * half
    rows = tokens // spans
    cols = width // 2
    finished(copies[:3])
    for target, mine_ref, low, size in (
        (queries, own, 0, half),
        (keys, sent, half, tokens),
        (values, sent, half + tokens, tokens),
    ):
        mine = mine_ref[low : low + size, :]
        other = got[low : low + size, :]
        target[:, :cols] = jnp.where(first, mine, other)
        target[:, cols:] = jnp.where(first, other, mine)
    copies[3].wait()
    factors = lax.rsqrt(jnp.sum(squares_ref[...], axis=0) / (width * (spans // 2)) + 1e-06)
    ident = lax.broadcasted_iota(jnp.int32, (tokens, tokens), 0) == lax.broadcasted_iota(
        jnp.int32, (tokens, tokens), 1
    )
    column = jnp.sum(jnp.where(ident, factors[0:1, :], 0.0), axis=1, keepdims=True)
    column = jnp.where(first, column[:half], column[half:]) * (1.0 / math.sqrt(head_size))
    row = factors[1:2, :]
    shape = (half, tokens)
    own_block = lax.broadcasted_iota(jnp.int32, shape, 0) // rows + core * (spans // 2)
    key_block = lax.broadcasted_iota(jnp.int32, shape, 1) // rows
    allowed = span_at(own_block, step, spans) >= span_at(key_block, step, spans)
    text_rows = text_ref.shape[0] * text_ref.shape[2]
    finished(copies[4:])
    for head in range(width // head_size):
        lanes = slice(head * head_size, (head + 1) * head_size)
        q = queries[:, lanes]
        scores = contract_last(q, keys[:, lanes]) * column * row
        scores = jnp.where(allowed, scores, -1e30)
        weights = jnp.exp(scores - jnp.max(scores, axis=1, keepdims=True))
        weights = weights * (1.0 / jnp.sum(weights, axis=1, keepdims=True))
        attended = jnp.dot(
            weights.astype(jnp.bfloat16), values[:, lanes], preferred_element_type=jnp.float32
        ).astype(jnp.bfloat16)
        parts = []
        for ref in (text_ref, more_ref):
            text_keys = ref[:, 0, :, lanes].reshape(text_rows, head_size)
            parts.append(contract_last(q, text_keys) * column)
        most = jnp.maximum(
            jnp.max(parts[0], axis=1, keepdims=True), jnp.max(parts[1], axis=1, keepdims=True)
        )
        parts = [jnp.exp(part - most) for part in parts]
        total = jnp.sum(parts[0], axis=1, keepdims=True) + jnp.sum(parts[1], axis=1, keepdims=True)
        share = 1.0 / total
        crossed = jnp.zeros((half, head_size), jnp.float32)
        for ref, part in zip((text_ref, more_ref), parts):
            text_values = ref[:, 1, :, lanes].reshape(text_rows, head_size)
            crossed = crossed + jnp.dot(
                (part * share).astype(jnp.bfloat16), text_values, preferred_element_type=jnp.float32
            )
        crossed = crossed.astype(jnp.bfloat16)
        out_ref[:, lanes] = (attended.astype(jnp.float32) + crossed.astype(jnp.float32)).astype(
            jnp.bfloat16
        )


def attend(step, spans, head_size, own, sent, got, squares, text, more):
    half, cols = own.shape
    tokens = 2 * half
    return pl.pallas_call(
        functools.partial(attend_kernel, step, spans, head_size),
        out_shape=jax.ShapeDtypeStruct((half, 2 * cols), jnp.bfloat16),
        in_specs=[HBM_SPEC] * 6,
        out_specs=VMEM_SPEC,
        scratch_shapes=[
            pltpu.VMEM(own.shape, jnp.bfloat16),
            pltpu.VMEM(sent.shape, jnp.bfloat16),
            pltpu.VMEM(got.shape, jnp.bfloat16),
            pltpu.VMEM(squares.shape, jnp.float32),
            pltpu.VMEM((half, 2 * cols), jnp.bfloat16),
            pltpu.VMEM((tokens, 2 * cols), jnp.bfloat16),
            pltpu.VMEM((tokens, 2 * cols), jnp.bfloat16),
            pltpu.VMEM(text.shape, jnp.bfloat16),
            pltpu.VMEM(more.shape, jnp.bfloat16),
            pltpu.SemaphoreType.DMA((6,)),
        ],
        compiler_params=PARAMS,
        name="attend",
    )(own, sent, got, squares, text, more)


def output_kernel(
    step, spans, last, current_hbm, table_hbm, incoming_hbm, own_hbm, other_hbm, *refs
):
    chips = spans // 2
    block_refs, refs = refs[:chips], refs[chips:]
    out_ref, blocks, current, gate_ref, entering, totals, weights, sems = refs
    chip, core = own_place()
    first = core == 0
    half, width = current.shape
    cols = width // 2
    rows = 2 * half // spans
    own_lanes = pl.ds(pl.multiple_of(chip * width, width), width)
    pairs = []
    for mask in range(chips):
        lanes = pl.ds(pl.multiple_of((chip ^ mask) * width, width), width)
        pairs.append((block_refs[mask], blocks.at[mask]))
        for side, ref in enumerate((own_hbm, other_hbm)):
            pairs.append((ref.at[:, lanes], weights.at[mask, side]))
    pairs.append((current_hbm, current))
    pairs.append((table_hbm.at[2, :, own_lanes], gate_ref))
    if not last:
        pairs.append((incoming_hbm.at[step + 1, :, own_lanes], entering))
    copies = started(pairs, sems)
    mine = jnp.zeros((half, cols), jnp.float32)
    other = jnp.zeros((half, cols), jnp.float32)
    for mask in range(chips):
        finished(copies[3 * mask : 3 * mask + 3])
        block = blocks[mask]
        mine = mine + contract_last(block, weights[mask, 0])
        other = other + contract_last(block, weights[mask, 1])
    totals[:, :cols] = jnp.where(first, mine, other)
    totals[:, cols:] = jnp.where(first, other, mine)
    finished(copies[3 * chips :])
    gates = gate_ref[...].astype(jnp.float32)
    for block in range(chips):
        band = slice(block * rows, (block + 1) * rows)
        places = [span_at(block + e * chips, step, spans) for e in range(2)]
        gate = jnp.where(first, *(gates[s : s + 1, :] for s in places))
        totals[band, :] = current[band, :].astype(jnp.float32) + gate * totals[band, :]
    if last:
        for target in range(chips):
            block = (target - STEPS // 2) % chips
            out_ref[target] = totals[block * rows : (block + 1) * rows, :].astype(jnp.bfloat16)
    else:
        parity, block = (spans - 2 - step) % 2, (spans - 2 - step) // 2
        band = slice(block * rows, (block + 1) * rows)
        totals[band, :] = jnp.where(
            core == parity, entering[...].astype(jnp.float32), totals[band, :]
        )
        out_ref[...] = totals[...].astype(jnp.bfloat16)


def output(step, spans, last, current, table, incoming, own, other, blocks):
    half, width = current.shape
    chips = spans // 2
    rows = 2 * half // spans
    return pl.pallas_call(
        functools.partial(output_kernel, step, spans, last),
        out_shape=jax.ShapeDtypeStruct(
            (chips, rows, width) if last else (half, width), jnp.bfloat16
        ),
        in_specs=[HBM_SPEC] * (5 + chips),
        out_specs=VMEM_SPEC,
        scratch_shapes=[
            pltpu.VMEM((chips, half, width), jnp.bfloat16),
            pltpu.VMEM((half, width), jnp.bfloat16),
            pltpu.VMEM((spans, width), jnp.bfloat16),
            pltpu.VMEM((rows, width), jnp.bfloat16),
            pltpu.VMEM((half, width), jnp.float32),
            pltpu.VMEM((chips, 2, width // 2, width), jnp.bfloat16),
            pltpu.SemaphoreType.DMA((3 * chips + 3,)),
        ],
        compiler_params=PARAMS,
        name="output",
    )(current, table, incoming, own, other, *blocks)


def join_kernel(in_ref, out_ref):
    chips, _, width = in_ref.shape
    for source in range(chips):
        out_ref[:, source * width : (source + 1) * width] = in_ref[source]


def join(blocks):
    chips, rows, width = blocks.shape
    return pl.pallas_call(
        join_kernel,
        out_shape=jax.ShapeDtypeStruct((rows, width * chips), jnp.bfloat16),
        in_specs=[VMEM_SPEC],
        out_specs=VMEM_SPEC,
        compiler_params=PARAMS,
        name="join",
    )(blocks)


def arrange_kernel(spans, keys_ref, values_ref, out_ref):
    width = out_ref.shape[3]
    text_half = out_ref.shape[2]
    for device in range(spans):
        lanes = slice(device // 2 * width, (device // 2 + 1) * width)
        band = slice(device % 2 * text_half, (device % 2 + 1) * text_half)
        out_ref[device, 0] = keys_ref[band, lanes]
        out_ref[device, 1] = values_ref[band, lanes]


def arrange(spans, keys, values):
    text_half = keys.shape[0] // 2
    return pl.pallas_call(
        functools.partial(arrange_kernel, spans),
        out_shape=jax.ShapeDtypeStruct(
            (spans, 2, text_half, 2 * keys.shape[1] // spans), jnp.bfloat16
        ),
        in_specs=[VMEM_SPEC] * 2,
        out_specs=VMEM_SPEC,
        compiler_params=PARAMS,
        name="arrange",
    )(keys, values)


def paired_device(
    hidden,
    incoming,
    levels,
    mod_table,
    query_weight,
    key_weight,
    value_weight,
    output_weight,
    query_gain,
    key_gain,
    text_keys,
    text_values,
):
    spans = lax.axis_size("queue")
    chips = spans // 2
    head_size = hidden.shape[1] // HEADS
    mine = gathered_over_chips(hidden)
    others = [swapped(block, 1) for block in mine]
    picked = (levels[:, None] == jnp.arange(mod_table.shape[0])[None, :]).astype(mod_table.dtype)
    table = jnp.einsum("sl,ltd->tsd", picked, mod_table, preferred_element_type=jnp.float32)
    table = table.astype(jnp.bfloat16)
    gain = jnp.stack([query_gain, key_gain])
    weights = [w.T for w in (query_weight, key_weight, value_weight)]
    output_own = output_weight.T
    output_other = swapped(output_own, 1)
    text = arrange(spans, text_keys, text_values)
    text, table, gain = lax.optimization_barrier((text, table, gain, *mine))[:3]
    text = lax.all_to_all(text, "queue", split_axis=0, concat_axis=0, tiled=True)
    current = None
    for step in range(STEPS):
        last = step == STEPS - 1
        own, send, squares, *rest = project(
            step, spans, gain, table, incoming, mine, others, weights
        )
        got = swapped(send, 1)
        squares = lax.all_to_all(squares, "queue", split_axis=0, concat_axis=0, tiled=True)
        if step == 0:
            current = rest[0]
            text = lax.optimization_barrier((text, send))[0]
            more = swapped(text, 1)
        block = attend(step, spans, head_size, own, send, got, squares, text, more)
        blocks = gathered_over_chips(block)
        result = output(
            step, spans, last, current, table, incoming, output_own, output_other, blocks
        )
        if not last:
            current = result
            mine = gathered_over_chips(current)
            others = [swapped(block, 1) for block in mine]
    same_core = [[2 * c + core for c in range(chips)] for core in range(2)]
    result = lax.all_to_all(
        result, "queue", split_axis=0, concat_axis=0, tiled=True, axis_index_groups=same_core
    )
    return join(result)


def held_in_pairs(mesh, hidden, query_weight):
    spans = mesh.shape["queue"]
    rows = hidden.shape[0] // (mesh.shape["groups"] * spans)
    cols = query_weight.shape[1] // spans
    head_size = query_weight.shape[0] // HEADS
    power = spans & (spans - 1) == 0
    return STEPS % 2 == 0 and power and spans >= 4 and 2 * cols % head_size == 0 and rows * spans == 128 and rows == 8


def solution(mesh):
    in_specs = (
        P(("groups", "queue"), None),
        P(None, "groups", None),
        P(),
        P(),
        P(None, "queue"),
        P(None, "queue"),
        P(None, "queue"),
        P(None, "queue"),
        P(),
        P(),
        P(("groups", "queue"), None),
        P(("groups", "queue"), None),
    )
    out_specs = P(("groups", "queue"), None)

    def apply(*args):
        body = paired_device if held_in_pairs(mesh, args[0], args[4]) else per_device
        return jax.shard_map(
            body, mesh=mesh, in_specs=in_specs, out_specs=out_specs, check_vma=False
        )(*args)

    return apply
```

```python
import functools
import math

import jax
import jax.numpy as jnp
from jax import lax
from jax.experimental import pallas as pl
from jax.experimental.pallas import tpu as pltpu
from jax.sharding import PartitionSpec as P

HEADS = 40
STEPS = 2


def passed_along(value, axis, steps):
    count = lax.axis_size(axis)
    initial, last = (max(0, -steps), min(count, count - steps))
    return lax.ppermute(value, axis, [(source, source + steps) for source in range(initial, last)])


def normalize(values):
    return values * lax.rsqrt(jnp.mean(values * values, axis=-1, keepdims=True) + 1e-06)


def softmax_rounded(scores):
    row_max = jnp.max(scores, axis=-1, keepdims=True)
    weights = jnp.exp(scores - row_max)
    return (weights / jnp.sum(weights, axis=-1, keepdims=True)).astype(jnp.bfloat16)


def pad_slots(values, slot_total):
    missing = slot_total - values.shape[1]
    filler = jnp.zeros((values.shape[0], missing, values.shape[2]), values.dtype)
    return jnp.concatenate([values, filler], axis=1)


def causal_block(queries, keys_all, values_all, span_rows, score_scale):
    total_rows = queries.shape[0]
    block_rows = min(512, total_rows)
    scores = (
        jnp.einsum("qsd,ksd->sqk", queries, keys_all, preferred_element_type=jnp.float32)
        * score_scale
    )
    allowed = (
        jnp.arange(0, block_rows)[:, None] // span_rows
        >= jnp.arange(block_rows)[None, :] // span_rows
    )
    scores = jnp.where(allowed[None], scores, -1e30)
    result = jnp.einsum(
        "sqk,ksd->qsd", softmax_rounded(scores), values_all, preferred_element_type=jnp.float32
    )
    pieces = result.astype(jnp.bfloat16)
    return pieces


def text_attend(queries, text_k, text_v, score_scale):
    scores = (
        jnp.einsum("qsd,tsd->sqt", queries, text_k, preferred_element_type=jnp.float32)
        * score_scale
    )
    return jnp.einsum(
        "sqt,tsd->qsd", softmax_rounded(scores), text_v, preferred_element_type=jnp.float32
    ).astype(jnp.bfloat16)


def per_device(
    hidden,
    incoming,
    levels,
    mod_table,
    query_weight,
    key_weight,
    value_weight,
    output_weight,
    query_gain,
    key_gain,
    text_keys,
    text_values,
):
    own_index = lax.axis_index("queue")
    queue_size = lax.axis_size("queue")
    span_rows, model_width = hidden.shape
    head_size = model_width // HEADS
    score_scale = 1.0 / math.sqrt(head_size)
    slot_total = -(-HEADS // queue_size) * queue_size
    own_level = lax.dynamic_index_in_dim(levels, own_index, 0, keepdims=False)
    modulation = lax.dynamic_index_in_dim(mod_table, own_level, 0, keepdims=False).astype(
        jnp.float32
    )
    stacked_weights = jnp.stack([query_weight, key_weight, value_weight])
    text_local = text_keys.shape[0]
    text_k_slots, text_v_slots = (
        lax.all_to_all(
            pad_slots(text_keys.reshape(text_local, HEADS, head_size), slot_total),
            "queue",
            split_axis=1,
            concat_axis=0,
            tiled=True,
        ),
        lax.all_to_all(
            pad_slots(text_values.reshape(text_local, HEADS, head_size), slot_total),
            "queue",
            split_axis=1,
            concat_axis=0,
            tiled=True,
        ),
    )
    queue_state = hidden
    for section_index in range(STEPS):
        shifted = passed_along(queue_state, "queue", 1)
        queue_state = jnp.where(own_index == 0, incoming[section_index], shifted)
        current = queue_state.astype(jnp.float32)
        modulated = (normalize(current) * (1.0 + modulation[1]) + modulation[0]).astype(
            jnp.bfloat16
        )
        columns = jnp.einsum(
            "rd,cdw->crw",
            lax.all_gather(modulated, "queue", axis=0, tiled=True),
            stacked_weights,
            preferred_element_type=jnp.float32,
        )
        own_rows = lax.all_to_all(
            columns.astype(jnp.bfloat16), "queue", split_axis=1, concat_axis=2, tiled=True
        ).astype(columns.dtype)
        query_heads = (
            (normalize(own_rows[0]) * query_gain)
            .astype(jnp.bfloat16)
            .reshape(span_rows, HEADS, head_size)
        )
        key_heads = (
            (normalize(own_rows[1]) * key_gain)
            .astype(jnp.bfloat16)
            .reshape(span_rows, HEADS, head_size)
        )
        value_heads = own_rows[2].astype(jnp.bfloat16).reshape(span_rows, HEADS, head_size)
        query_slots, key_slots, value_slots = (
            lax.all_to_all(
                pad_slots(query_heads, slot_total), "queue", split_axis=1, concat_axis=0, tiled=True
            ),
            lax.all_to_all(
                pad_slots(key_heads, slot_total), "queue", split_axis=1, concat_axis=0, tiled=True
            ),
            lax.all_to_all(
                pad_slots(value_heads, slot_total), "queue", split_axis=1, concat_axis=0, tiled=True
            ),
        )
        attended_slots = causal_block(query_slots, key_slots, value_slots, span_rows, score_scale)
        crossed_slots = text_attend(query_slots, text_k_slots, text_v_slots, score_scale)
        attended_back, crossed_back = (
            lax.all_to_all(attended_slots, "queue", split_axis=0, concat_axis=1, tiled=True),
            lax.all_to_all(crossed_slots, "queue", split_axis=0, concat_axis=1, tiled=True),
        )
        attended = attended_back[:, :HEADS]
        crossed = crossed_back[:, :HEADS]
        combined = (
            (attended.astype(jnp.float32) + crossed.astype(jnp.float32))
            .astype(jnp.bfloat16)
            .reshape(span_rows, model_width)
        )
        out_columns = jnp.dot(
            lax.all_gather(combined, "queue", axis=0, tiled=True),
            output_weight,
            preferred_element_type=jnp.float32,
        )
        projected = lax.all_to_all(
            out_columns.astype(jnp.bfloat16), "queue", split_axis=0, concat_axis=1, tiled=True
        ).astype(out_columns.dtype)
        queue_state = (current + modulation[2] * projected).astype(jnp.bfloat16)
    return queue_state


def swapped(value, bit):
    count = lax.axis_size("queue")
    return lax.ppermute(value, "queue", [(source, source ^ bit) for source in range(count)])


def gathered_over_chips(block):
    chips = lax.axis_size("queue") // 2
    blocks = {0: block}
    for mask in range(2, chips, 2):
        blocks[mask] = swapped(block, 2 * mask)
    for mask in range(0, chips, 2):
        blocks[mask + 1] = swapped(blocks[mask], 2)
    return [blocks[mask] for mask in range(chips)]


def contract_last(left, right):
    return lax.dot_general(
        left, right, (((1,), (1,)), ((), ())), preferred_element_type=jnp.float32
    )


HBM_SPEC = pl.BlockSpec(memory_space=pltpu.HBM)
VMEM_SPEC = pl.BlockSpec(memory_space=pltpu.VMEM)
PARAMS = pltpu.CompilerParams(vmem_limit_bytes=60 * 1024 * 1024)


def span_at(position, step, spans):
    chips = spans // 2
    return (2 * (position % chips) + position // chips + step + 1) % spans


def own_place():
    own_index = lax.axis_index("queue")
    return own_index // 2, own_index % 2


def started(pairs, sems):
    copies = [
        pltpu.make_async_copy(source, target, sems.at[i]) for i, (source, target) in enumerate(pairs)
    ]
    for copy in copies:
        copy.start()
    return copies


def finished(copies):
    for copy in copies:
        copy.wait()


def project_kernel(step, spans, gain_hbm, table_hbm, incoming_hbm, *refs):
    chips = spans // 2
    weight_refs, refs = refs[:3], refs[3:]
    mine, others = refs[:chips], refs[chips : 2 * chips]
    refs = refs[2 * chips :]
    own_hbm, send_hbm, squares_ref = refs[:3]
    refs = refs[3:]
    if step == 0:
        current_hbm, refs = refs[0], refs[1:]
    state, modulated, table, entering, gain, scale_ref, shift_ref, weights, own, send, current, sems = refs
    chip, core = own_place()
    tokens, width = modulated.shape
    half = tokens // 2
    rows = tokens // spans
    pair = 2 * rows
    cols = weight_refs[0].shape[0]
    first = core == 0
    own_lanes = pl.ds(pl.multiple_of(chip * 2 * cols, 2 * cols), 2 * cols)
    pairs = []
    for side, blocks in enumerate((mine, others)):
        owner = core if side == 0 else 1 - core
        for mask in range(chips):
            other_chip = chip ^ mask
            if step == 0:
                target = state.at[owner * chips + other_chip]
            else:
                lanes = pl.ds(pl.multiple_of(other_chip * 2 * cols, 2 * cols), 2 * cols)
                target = state.at[pl.ds(pl.multiple_of(owner * half, half), half), lanes]
            pairs.append((blocks[mask], target))
    pairs += [(table_hbm, table), (gain_hbm.at[:, own_lanes], gain), (incoming_hbm, entering)]
    pairs += [(weight_refs[i], weights.at[i]) for i in range(3)]
    copies = started(pairs, sems)
    copies, fetches = copies[:-3], copies[-3:]
    finished(copies)
    shift_ref[...] = table[0].astype(jnp.float32)
    scale_ref[...] = table[1].astype(jnp.float32) + 1.0
    leaving = []
    if step == 0:
        state[spans - 1] = entering[step]
        for slab in range(chips // 2):
            at = core * chips + 2 * slab
            both = [state[at + e, :, own_lanes].astype(jnp.float32) for e in range(2)]
            current[slab * pair : (slab + 1) * pair, :] = jnp.concatenate(both, axis=0).astype(
                jnp.bfloat16
            )
        leaving += started([(current, current_hbm)], sems.at[pl.ds(0, 1)])
    pieces = 4
    piece = width // pieces
    for slab in range(chips):
        band = slice(slab * pair, (slab + 1) * pair)

        def load(part):
            if step == 0:
                both = [state[2 * slab + e, :, part].astype(jnp.float32) for e in range(2)]
                return jnp.concatenate(both, axis=0)
            return state[band, part].astype(jnp.float32)

        total = jnp.zeros((pair, 1), jnp.float32)
        for low in range(0, width, piece):
            x = load(slice(low, low + piece))
            total = total + jnp.sum(x * x, axis=1, keepdims=True)
        factor = lax.rsqrt(total / width + 1e-06)
        at = [span_at(2 * slab + e, step, spans) for e in range(2)]
        for low in range(0, width, piece):
            part = slice(low, low + piece)
            x = load(part) * factor
            scale, shift = (
                jnp.concatenate(
                    [jnp.broadcast_to(ref[s : s + 1, part], (rows, piece)) for s in at], axis=0
                )
                for ref in (scale_ref, shift_ref)
            )
            modulated[band, part] = (x * scale + shift).astype(jnp.bfloat16)
    ident = lax.broadcasted_iota(jnp.int32, (tokens, tokens), 0) == lax.broadcasted_iota(
        jnp.int32, (tokens, tokens), 1
    )
    for i in range(3):
        fetches[i].wait()
        product = contract_last(modulated[...], weights[i])
        if i < 2:
            column = jnp.sum(product * product, axis=1, keepdims=True)
            line = jnp.sum(jnp.where(ident, column, 0.0), axis=0, keepdims=True)
            squares_ref[:, i : i + 1, :] = jnp.broadcast_to(line[None], (spans, 1, tokens))
            line = gain[i : i + 1, :]
            product = product * jnp.where(first, line[:, :cols], line[:, cols:])
        if i == 0:
            low, high = product[:half], product[half:]
            own[...] = jnp.where(first, low, high).astype(jnp.bfloat16)
            send[:half, :] = jnp.where(first, high, low).astype(jnp.bfloat16)
            leaving += started(
                [(own, own_hbm), (send.at[pl.ds(0, half)], send_hbm.at[pl.ds(0, half)])],
                sems.at[pl.ds(1, 2)],
            )
        else:
            band = pl.ds(half + (i - 1) * tokens, tokens)
            send[band, :] = product.astype(jnp.bfloat16)
            leaving += started([(send.at[band], send_hbm.at[band])], sems.at[pl.ds(2 + i, 1)])
    finished(leaving)


def project(step, spans, gain, table, incoming, mine, others, weights):
    rows = incoming.shape[1]
    tokens = spans * rows
    cols, width = weights[0].shape
    half = tokens // 2
    out_shape = [
        jax.ShapeDtypeStruct((half, cols), jnp.bfloat16),
        jax.ShapeDtypeStruct((half + 2 * tokens, cols), jnp.bfloat16),
        jax.ShapeDtypeStruct((spans, 2, tokens), jnp.float32),
    ]
    if step == 0:
        out_shape.append(jax.ShapeDtypeStruct((half, 2 * cols), jnp.bfloat16))
        state = (spans, rows, width)
    else:
        state = (tokens, width)
    return pl.pallas_call(
        functools.partial(project_kernel, step, spans),
        out_shape=out_shape,
        in_specs=[HBM_SPEC] * (6 + 2 * len(mine)),
        out_specs=[HBM_SPEC, HBM_SPEC, VMEM_SPEC, HBM_SPEC][: len(out_shape)],
        scratch_shapes=[
            pltpu.VMEM(state, jnp.bfloat16),
            pltpu.VMEM((tokens, width), jnp.bfloat16),
            pltpu.VMEM(table.shape, jnp.bfloat16),
            pltpu.VMEM(incoming.shape, jnp.bfloat16),
            pltpu.VMEM((2, 2 * cols), jnp.float32),
            pltpu.VMEM((spans, width), jnp.float32),
            pltpu.VMEM((spans, width), jnp.float32),
            pltpu.VMEM((3, cols, width), jnp.bfloat16),
            pltpu.VMEM((half, cols), jnp.bfloat16),
            pltpu.VMEM((half + 2 * tokens, cols), jnp.bfloat16),
            pltpu.VMEM((half, 2 * cols), jnp.bfloat16),
            pltpu.SemaphoreType.DMA((spans + 6,)),
        ],
        compiler_params=PARAMS,
        name="project",
    )(gain, table, incoming, *weights, *mine, *others)


def attend_kernel(
    step, spans, head_size, own_hbm, sent_hbm, got_hbm, squares_hbm, text_hbm, more_hbm,
    out_ref, own, sent, got, squares_ref, queries, keys, values, text_ref, more_ref, sems,
):
    copies = started(
        [
            (own_hbm, own),
            (sent_hbm, sent),
            (got_hbm, got),
            (squares_hbm, squares_ref),
            (text_hbm, text_ref),
            (more_hbm, more_ref),
        ],
        sems,
    )
    chip, core = own_place()
    first = core == 0
    half, width = queries.shape
    tokens = 2 * half
    rows = tokens // spans
    cols = width // 2
    finished(copies[:3])
    for target, mine_ref, low, size in (
        (queries, own, 0, half),
        (keys, sent, half, tokens),
        (values, sent, half + tokens, tokens),
    ):
        mine = mine_ref[low : low + size, :]
        other = got[low : low + size, :]
        target[:, :cols] = jnp.where(first, mine, other)
        target[:, cols:] = jnp.where(first, other, mine)
    copies[3].wait()
    factors = lax.rsqrt(jnp.sum(squares_ref[...], axis=0) / (width * (spans // 2)) + 1e-06)
    ident = lax.broadcasted_iota(jnp.int32, (tokens, tokens), 0) == lax.broadcasted_iota(
        jnp.int32, (tokens, tokens), 1
    )
    column = jnp.sum(jnp.where(ident, factors[0:1, :], 0.0), axis=1, keepdims=True)
    column = jnp.where(first, column[:half], column[half:]) * (1.0 / math.sqrt(head_size))
    row = factors[1:2, :]
    shape = (half, tokens)
    own_block = lax.broadcasted_iota(jnp.int32, shape, 0) // rows + core * (spans // 2)
    key_block = lax.broadcasted_iota(jnp.int32, shape, 1) // rows
    allowed = span_at(own_block, step, spans) >= span_at(key_block, step, spans)
    text_rows = text_ref.shape[0] * text_ref.shape[2]
    finished(copies[4:])
    for head in range(width // head_size):
        lanes = slice(head * head_size, (head + 1) * head_size)
        q = queries[:, lanes]
        scores = contract_last(q, keys[:, lanes]) * column * row
        scores = jnp.where(allowed, scores, -1e30)
        weights = jnp.exp(scores - jnp.max(scores, axis=1, keepdims=True))
        weights = weights * (1.0 / jnp.sum(weights, axis=1, keepdims=True))
        attended = jnp.dot(
            weights.astype(jnp.bfloat16), values[:, lanes], preferred_element_type=jnp.float32
        ).astype(jnp.bfloat16)
        parts = []
        for ref in (text_ref, more_ref):
            text_keys = ref[:, 0, :, lanes].reshape(text_rows, head_size)
            parts.append(contract_last(q, text_keys) * column)
        most = jnp.maximum(
            jnp.max(parts[0], axis=1, keepdims=True), jnp.max(parts[1], axis=1, keepdims=True)
        )
        parts = [jnp.exp(part - most) for part in parts]
        total = jnp.sum(parts[0], axis=1, keepdims=True) + jnp.sum(parts[1], axis=1, keepdims=True)
        share = 1.0 / total
        crossed = jnp.zeros((half, head_size), jnp.float32)
        for ref, part in zip((text_ref, more_ref), parts):
            text_values = ref[:, 1, :, lanes].reshape(text_rows, head_size)
            crossed = crossed + jnp.dot(
                (part * share).astype(jnp.bfloat16), text_values, preferred_element_type=jnp.float32
            )
        crossed = crossed.astype(jnp.bfloat16)
        out_ref[:, lanes] = (attended.astype(jnp.float32) + crossed.astype(jnp.float32)).astype(
            jnp.bfloat16
        )


def attend(step, spans, head_size, own, sent, got, squares, text, more):
    half, cols = own.shape
    tokens = 2 * half
    return pl.pallas_call(
        functools.partial(attend_kernel, step, spans, head_size),
        out_shape=jax.ShapeDtypeStruct((half, 2 * cols), jnp.bfloat16),
        in_specs=[HBM_SPEC] * 6,
        out_specs=VMEM_SPEC,
        scratch_shapes=[
            pltpu.VMEM(own.shape, jnp.bfloat16),
            pltpu.VMEM(sent.shape, jnp.bfloat16),
            pltpu.VMEM(got.shape, jnp.bfloat16),
            pltpu.VMEM(squares.shape, jnp.float32),
            pltpu.VMEM((half, 2 * cols), jnp.bfloat16),
            pltpu.VMEM((tokens, 2 * cols), jnp.bfloat16),
            pltpu.VMEM((tokens, 2 * cols), jnp.bfloat16),
            pltpu.VMEM(text.shape, jnp.bfloat16),
            pltpu.VMEM(more.shape, jnp.bfloat16),
            pltpu.SemaphoreType.DMA((6,)),
        ],
        compiler_params=PARAMS,
        name="attend",
    )(own, sent, got, squares, text, more)


def output_kernel(
    step, spans, last, current_hbm, table_hbm, incoming_hbm, own_hbm, other_hbm, *refs
):
    chips = spans // 2
    block_refs, refs = refs[:chips], refs[chips:]
    out_ref, blocks, current, gate_ref, entering, totals, weights, sems = refs
    chip, core = own_place()
    first = core == 0
    half, width = current.shape
    cols = width // 2
    rows = 2 * half // spans
    own_lanes = pl.ds(pl.multiple_of(chip * width, width), width)
    pairs = []
    for mask in range(chips):
        lanes = pl.ds(pl.multiple_of((chip ^ mask) * width, width), width)
        pairs.append((block_refs[mask], blocks.at[mask]))
        for side, ref in enumerate((own_hbm, other_hbm)):
            pairs.append((ref.at[:, lanes], weights.at[mask, side]))
    pairs.append((current_hbm, current))
    pairs.append((table_hbm.at[2, :, own_lanes], gate_ref))
    if not last:
        pairs.append((incoming_hbm.at[step + 1, :, own_lanes], entering))
    copies = started(pairs, sems)
    mine = jnp.zeros((half, cols), jnp.float32)
    other = jnp.zeros((half, cols), jnp.float32)
    for mask in range(chips):
        finished(copies[3 * mask : 3 * mask + 3])
        block = blocks[mask]
        mine = mine + contract_last(block, weights[mask, 0])
        other = other + contract_last(block, weights[mask, 1])
    totals[:, :cols] = jnp.where(first, mine, other)
    totals[:, cols:] = jnp.where(first, other, mine)
    finished(copies[3 * chips :])
    gates = gate_ref[...].astype(jnp.float32)
    for block in range(chips):
        band = slice(block * rows, (block + 1) * rows)
        places = [span_at(block + e * chips, step, spans) for e in range(2)]
        gate = jnp.where(first, *(gates[s : s + 1, :] for s in places))
        totals[band, :] = current[band, :].astype(jnp.float32) + gate * totals[band, :]
    if last:
        for target in range(chips):
            block = (target - STEPS // 2) % chips
            out_ref[target] = totals[block * rows : (block + 1) * rows, :].astype(jnp.bfloat16)
    else:
        parity, block = (spans - 2 - step) % 2, (spans - 2 - step) // 2
        band = slice(block * rows, (block + 1) * rows)
        totals[band, :] = jnp.where(
            core == parity, entering[...].astype(jnp.float32), totals[band, :]
        )
        out_ref[...] = totals[...].astype(jnp.bfloat16)


def output(step, spans, last, current, table, incoming, own, other, blocks):
    half, width = current.shape
    chips = spans // 2
    rows = 2 * half // spans
    return pl.pallas_call(
        functools.partial(output_kernel, step, spans, last),
        out_shape=jax.ShapeDtypeStruct(
            (chips, rows, width) if last else (half, width), jnp.bfloat16
        ),
        in_specs=[HBM_SPEC] * (5 + chips),
        out_specs=VMEM_SPEC,
        scratch_shapes=[
            pltpu.VMEM((chips, half, width), jnp.bfloat16),
            pltpu.VMEM((half, width), jnp.bfloat16),
            pltpu.VMEM((spans, width), jnp.bfloat16),
            pltpu.VMEM((rows, width), jnp.bfloat16),
            pltpu.VMEM((half, width), jnp.float32),
            pltpu.VMEM((chips, 2, width // 2, width), jnp.bfloat16),
            pltpu.SemaphoreType.DMA((3 * chips + 3,)),
        ],
        compiler_params=PARAMS,
        name="output",
    )(current, table, incoming, own, other, *blocks)


def join_kernel(in_ref, out_ref):
    chips, _, width = in_ref.shape
    for source in range(chips):
        out_ref[:, source * width : (source + 1) * width] = in_ref[source]


def join(blocks):
    chips, rows, width = blocks.shape
    return pl.pallas_call(
        join_kernel,
        out_shape=jax.ShapeDtypeStruct((rows, width * chips), jnp.bfloat16),
        in_specs=[VMEM_SPEC],
        out_specs=VMEM_SPEC,
        compiler_params=PARAMS,
        name="join",
    )(blocks)


def arrange_kernel(spans, keys_ref, values_ref, out_ref):
    width = out_ref.shape[3]
    text_half = out_ref.shape[2]
    for device in range(spans):
        lanes = slice(device // 2 * width, (device // 2 + 1) * width)
        band = slice(device % 2 * text_half, (device % 2 + 1) * text_half)
        out_ref[device, 0] = keys_ref[band, lanes]
        out_ref[device, 1] = values_ref[band, lanes]


def arrange(spans, keys, values):
    text_half = keys.shape[0] // 2
    return pl.pallas_call(
        functools.partial(arrange_kernel, spans),
        out_shape=jax.ShapeDtypeStruct(
            (spans, 2, text_half, 2 * keys.shape[1] // spans), jnp.bfloat16
        ),
        in_specs=[VMEM_SPEC] * 2,
        out_specs=VMEM_SPEC,
        compiler_params=PARAMS,
        name="arrange",
    )(keys, values)


def paired_device(
    hidden,
    incoming,
    levels,
    mod_table,
    query_weight,
    key_weight,
    value_weight,
    output_weight,
    query_gain,
    key_gain,
    text_keys,
    text_values,
):
    spans = lax.axis_size("queue")
    chips = spans // 2
    head_size = hidden.shape[1] // HEADS
    mine = gathered_over_chips(hidden)
    others = [swapped(block, 1) for block in mine]
    picked = (levels[:, None] == jnp.arange(mod_table.shape[0])[None, :]).astype(mod_table.dtype)
    table = jnp.einsum("sl,ltd->tsd", picked, mod_table, preferred_element_type=jnp.float32)
    table = table.astype(jnp.bfloat16)
    gain = jnp.stack([query_gain, key_gain])
    weights = [w.T for w in (query_weight, key_weight, value_weight)]
    output_own = output_weight.T
    output_other = swapped(output_own, 1)
    text = arrange(spans, text_keys, text_values)
    text, table, gain = lax.optimization_barrier((text, table, gain, *mine))[:3]
    text = lax.all_to_all(text, "queue", split_axis=0, concat_axis=0, tiled=True)
    current = None
    for step in range(STEPS):
        last = step == STEPS - 1
        own, send, squares, *rest = project(
            step, spans, gain, table, incoming, mine, others, weights
        )
        got = swapped(send, 1)
        squares = lax.all_to_all(squares, "queue", split_axis=0, concat_axis=0, tiled=True)
        if step == 0:
            current = rest[0]
            text = lax.optimization_barrier((text, send))[0]
            more = swapped(text, 1)
        block = attend(step, spans, head_size, own, send, got, squares, text, more)
        blocks = gathered_over_chips(block)
        result = output(
            step, spans, last, current, table, incoming, output_own, output_other, blocks
        )
        if not last:
            current = result
            mine = gathered_over_chips(current)
            others = [swapped(block, 1) for block in mine]
    same_core = [[2 * c + core for c in range(chips)] for core in range(2)]
    result = lax.all_to_all(
        result, "queue", split_axis=0, concat_axis=2, tiled=True, axis_index_groups=same_core
    )
    return result[0]


def held_in_pairs(mesh, hidden, query_weight):
    spans = mesh.shape["queue"]
    rows = hidden.shape[0] // (mesh.shape["groups"] * spans)
    cols = query_weight.shape[1] // spans
    head_size = query_weight.shape[0] // HEADS
    power = spans & (spans - 1) == 0
    return STEPS % 2 == 0 and power and spans >= 4 and 2 * cols % head_size == 0 and rows * spans == 128 and rows == 8


def solution(mesh):
    in_specs = (
        P(("groups", "queue"), None),
        P(None, "groups", None),
        P(),
        P(),
        P(None, "queue"),
        P(None, "queue"),
        P(None, "queue"),
        P(None, "queue"),
        P(),
        P(),
        P(("groups", "queue"), None),
        P(("groups", "queue"), None),
    )
    out_specs = P(("groups", "queue"), None)

    def apply(*args):
        body = paired_device if held_in_pairs(mesh, args[0], args[4]) else per_device
        return jax.shard_map(
            body, mesh=mesh, in_specs=in_specs, out_specs=out_specs, check_vma=False
        )(*args)

    return apply
```

```python
import functools
import math

import jax
import jax.numpy as jnp
from jax import lax
from jax.experimental import pallas as pl
from jax.experimental.pallas import tpu as pltpu
from jax.sharding import PartitionSpec as P

HEADS = 40
STEPS = 2


def passed_along(value, axis, steps):
    count = lax.axis_size(axis)
    initial, last = (max(0, -steps), min(count, count - steps))
    return lax.ppermute(value, axis, [(source, source + steps) for source in range(initial, last)])


def normalize(values):
    return values * lax.rsqrt(jnp.mean(values * values, axis=-1, keepdims=True) + 1e-06)


def softmax_rounded(scores):
    row_max = jnp.max(scores, axis=-1, keepdims=True)
    weights = jnp.exp(scores - row_max)
    return (weights / jnp.sum(weights, axis=-1, keepdims=True)).astype(jnp.bfloat16)


def pad_slots(values, slot_total):
    missing = slot_total - values.shape[1]
    filler = jnp.zeros((values.shape[0], missing, values.shape[2]), values.dtype)
    return jnp.concatenate([values, filler], axis=1)


def causal_block(queries, keys_all, values_all, span_rows, score_scale):
    total_rows = queries.shape[0]
    block_rows = min(512, total_rows)
    scores = (
        jnp.einsum("qsd,ksd->sqk", queries, keys_all, preferred_element_type=jnp.float32)
        * score_scale
    )
    allowed = (
        jnp.arange(0, block_rows)[:, None] // span_rows
        >= jnp.arange(block_rows)[None, :] // span_rows
    )
    scores = jnp.where(allowed[None], scores, -1e30)
    result = jnp.einsum(
        "sqk,ksd->qsd", softmax_rounded(scores), values_all, preferred_element_type=jnp.float32
    )
    pieces = result.astype(jnp.bfloat16)
    return pieces


def text_attend(queries, text_k, text_v, score_scale):
    scores = (
        jnp.einsum("qsd,tsd->sqt", queries, text_k, preferred_element_type=jnp.float32)
        * score_scale
    )
    return jnp.einsum(
        "sqt,tsd->qsd", softmax_rounded(scores), text_v, preferred_element_type=jnp.float32
    ).astype(jnp.bfloat16)


def per_device(
    hidden,
    incoming,
    levels,
    mod_table,
    query_weight,
    key_weight,
    value_weight,
    output_weight,
    query_gain,
    key_gain,
    text_keys,
    text_values,
):
    own_index = lax.axis_index("queue")
    queue_size = lax.axis_size("queue")
    span_rows, model_width = hidden.shape
    head_size = model_width // HEADS
    score_scale = 1.0 / math.sqrt(head_size)
    slot_total = -(-HEADS // queue_size) * queue_size
    own_level = lax.dynamic_index_in_dim(levels, own_index, 0, keepdims=False)
    modulation = lax.dynamic_index_in_dim(mod_table, own_level, 0, keepdims=False).astype(
        jnp.float32
    )
    stacked_weights = jnp.stack([query_weight, key_weight, value_weight])
    text_local = text_keys.shape[0]
    text_k_slots, text_v_slots = (
        lax.all_to_all(
            pad_slots(text_keys.reshape(text_local, HEADS, head_size), slot_total),
            "queue",
            split_axis=1,
            concat_axis=0,
            tiled=True,
        ),
        lax.all_to_all(
            pad_slots(text_values.reshape(text_local, HEADS, head_size), slot_total),
            "queue",
            split_axis=1,
            concat_axis=0,
            tiled=True,
        ),
    )
    queue_state = hidden
    for section_index in range(STEPS):
        shifted = passed_along(queue_state, "queue", 1)
        queue_state = jnp.where(own_index == 0, incoming[section_index], shifted)
        current = queue_state.astype(jnp.float32)
        modulated = (normalize(current) * (1.0 + modulation[1]) + modulation[0]).astype(
            jnp.bfloat16
        )
        columns = jnp.einsum(
            "rd,cdw->crw",
            lax.all_gather(modulated, "queue", axis=0, tiled=True),
            stacked_weights,
            preferred_element_type=jnp.float32,
        )
        own_rows = lax.all_to_all(
            columns.astype(jnp.bfloat16), "queue", split_axis=1, concat_axis=2, tiled=True
        ).astype(columns.dtype)
        query_heads = (
            (normalize(own_rows[0]) * query_gain)
            .astype(jnp.bfloat16)
            .reshape(span_rows, HEADS, head_size)
        )
        key_heads = (
            (normalize(own_rows[1]) * key_gain)
            .astype(jnp.bfloat16)
            .reshape(span_rows, HEADS, head_size)
        )
        value_heads = own_rows[2].astype(jnp.bfloat16).reshape(span_rows, HEADS, head_size)
        query_slots, key_slots, value_slots = (
            lax.all_to_all(
                pad_slots(query_heads, slot_total), "queue", split_axis=1, concat_axis=0, tiled=True
            ),
            lax.all_to_all(
                pad_slots(key_heads, slot_total), "queue", split_axis=1, concat_axis=0, tiled=True
            ),
            lax.all_to_all(
                pad_slots(value_heads, slot_total), "queue", split_axis=1, concat_axis=0, tiled=True
            ),
        )
        attended_slots = causal_block(query_slots, key_slots, value_slots, span_rows, score_scale)
        crossed_slots = text_attend(query_slots, text_k_slots, text_v_slots, score_scale)
        attended_back, crossed_back = (
            lax.all_to_all(attended_slots, "queue", split_axis=0, concat_axis=1, tiled=True),
            lax.all_to_all(crossed_slots, "queue", split_axis=0, concat_axis=1, tiled=True),
        )
        attended = attended_back[:, :HEADS]
        crossed = crossed_back[:, :HEADS]
        combined = (
            (attended.astype(jnp.float32) + crossed.astype(jnp.float32))
            .astype(jnp.bfloat16)
            .reshape(span_rows, model_width)
        )
        out_columns = jnp.dot(
            lax.all_gather(combined, "queue", axis=0, tiled=True),
            output_weight,
            preferred_element_type=jnp.float32,
        )
        projected = lax.all_to_all(
            out_columns.astype(jnp.bfloat16), "queue", split_axis=0, concat_axis=1, tiled=True
        ).astype(out_columns.dtype)
        queue_state = (current + modulation[2] * projected).astype(jnp.bfloat16)
    return queue_state


def swapped(value, bit):
    count = lax.axis_size("queue")
    return lax.ppermute(value, "queue", [(source, source ^ bit) for source in range(count)])


def gathered_over_chips(block):
    chips = lax.axis_size("queue") // 2
    blocks = {0: block}
    for mask in range(2, chips, 2):
        blocks[mask] = swapped(block, 2 * mask)
    for mask in range(0, chips, 2):
        blocks[mask + 1] = swapped(blocks[mask], 2)
    return [blocks[mask] for mask in range(chips)]


def contract_last(left, right):
    return lax.dot_general(
        left, right, (((1,), (1,)), ((), ())), preferred_element_type=jnp.float32
    )


HBM_SPEC = pl.BlockSpec(memory_space=pltpu.HBM)
VMEM_SPEC = pl.BlockSpec(memory_space=pltpu.VMEM)
PARAMS = pltpu.CompilerParams(vmem_limit_bytes=60 * 1024 * 1024)


def span_at(position, step, spans):
    chips = spans // 2
    return (2 * (position % chips) + position // chips + step + 1) % spans


def own_place():
    own_index = lax.axis_index("queue")
    return own_index // 2, own_index % 2


def started(pairs, sems):
    copies = [
        pltpu.make_async_copy(source, target, sems.at[i]) for i, (source, target) in enumerate(pairs)
    ]
    for copy in copies:
        copy.start()
    return copies


def finished(copies):
    for copy in copies:
        copy.wait()


def project_kernel(step, spans, gain_hbm, table_hbm, incoming_hbm, *refs):
    chips = spans // 2
    weight_refs, refs = refs[:3], refs[3:]
    mine, others = refs[:chips], refs[chips : 2 * chips]
    refs = refs[2 * chips :]
    own_hbm, send_hbm, squares_ref = refs[:3]
    refs = refs[3:]
    if step == 0:
        current_hbm, refs = refs[0], refs[1:]
    state, modulated, table, entering, gain, scale_ref, shift_ref, weights, own, send, current, sems = refs
    chip, core = own_place()
    tokens, width = modulated.shape
    half = tokens // 2
    rows = tokens // spans
    pair = 2 * rows
    cols = weight_refs[0].shape[0]
    first = core == 0
    own_lanes = pl.ds(pl.multiple_of(chip * 2 * cols, 2 * cols), 2 * cols)
    pairs = []
    for side, blocks in enumerate((mine, others)):
        owner = core if side == 0 else 1 - core
        for mask in range(chips):
            other_chip = chip ^ mask
            if step == 0:
                target = state.at[owner * chips + other_chip]
            else:
                lanes = pl.ds(pl.multiple_of(other_chip * 2 * cols, 2 * cols), 2 * cols)
                target = state.at[pl.ds(pl.multiple_of(owner * half, half), half), lanes]
            pairs.append((blocks[mask], target))
    pairs += [(table_hbm, table), (gain_hbm.at[:, own_lanes], gain), (incoming_hbm, entering)]
    pairs += [(weight_refs[i], weights.at[i]) for i in range(3)]
    copies = started(pairs, sems)
    copies, fetches = copies[:-3], copies[-3:]
    finished(copies)
    shift_ref[...] = table[0].astype(jnp.float32)
    scale_ref[...] = table[1].astype(jnp.float32) + 1.0
    leaving = []
    if step == 0:
        state[spans - 1] = entering[step]
        for slab in range(chips // 2):
            at = core * chips + 2 * slab
            both = [state[at + e, :, own_lanes].astype(jnp.float32) for e in range(2)]
            current[slab * pair : (slab + 1) * pair, :] = jnp.concatenate(both, axis=0).astype(
                jnp.bfloat16
            )
        leaving += started([(current, current_hbm)], sems.at[pl.ds(0, 1)])
    pieces = 4
    piece = width // pieces
    for slab in range(chips):
        band = slice(slab * pair, (slab + 1) * pair)

        def load(part):
            if step == 0:
                both = [state[2 * slab + e, :, part].astype(jnp.float32) for e in range(2)]
                return jnp.concatenate(both, axis=0)
            return state[band, part].astype(jnp.float32)

        total = jnp.zeros((pair, 1), jnp.float32)
        for low in range(0, width, piece):
            x = load(slice(low, low + piece))
            total = total + jnp.sum(x * x, axis=1, keepdims=True)
        factor = lax.rsqrt(total / width + 1e-06)
        at = [span_at(2 * slab + e, step, spans) for e in range(2)]
        for low in range(0, width, piece):
            part = slice(low, low + piece)
            x = load(part) * factor
            scale, shift = (
                jnp.concatenate(
                    [jnp.broadcast_to(ref[s : s + 1, part], (rows, piece)) for s in at], axis=0
                )
                for ref in (scale_ref, shift_ref)
            )
            modulated[band, part] = (x * scale + shift).astype(jnp.bfloat16)
    ident = lax.broadcasted_iota(jnp.int32, (tokens, tokens), 0) == lax.broadcasted_iota(
        jnp.int32, (tokens, tokens), 1
    )
    products = []
    for fetch, weight in ((fetches[:1], 0), (fetches[1:], 1), ([], 2)):
        finished(fetch)
        products.append(contract_last(modulated[...], weights[weight]))
    shape = (tokens, tokens)
    ident = lax.broadcasted_iota(jnp.int32, shape, 0) == lax.broadcasted_iota(jnp.int32, shape, 1)
    for i in range(2):
        column = jnp.sum(products[i] * products[i], axis=1, keepdims=True)
        line = jnp.sum(jnp.where(ident, column, 0.0), axis=0, keepdims=True)
        squares_ref[:, i : i + 1, :] = jnp.broadcast_to(line[None], (spans, 1, tokens))
        line = gain[i : i + 1, :]
        products[i] = products[i] * jnp.where(first, line[:, :cols], line[:, cols:])
    low, high = products[0][:half], products[0][half:]
    own[...] = jnp.where(first, low, high).astype(jnp.bfloat16)
    send[:half, :] = jnp.where(first, high, low).astype(jnp.bfloat16)
    send[half : half + tokens, :] = products[1].astype(jnp.bfloat16)
    send[half + tokens :, :] = products[2].astype(jnp.bfloat16)
    leaving += started([(own, own_hbm), (send, send_hbm)], sems.at[pl.ds(1, 2)])
    finished(leaving)


def project(step, spans, gain, table, incoming, mine, others, weights):
    rows = incoming.shape[1]
    tokens = spans * rows
    cols, width = weights[0].shape
    half = tokens // 2
    out_shape = [
        jax.ShapeDtypeStruct((half, cols), jnp.bfloat16),
        jax.ShapeDtypeStruct((half + 2 * tokens, cols), jnp.bfloat16),
        jax.ShapeDtypeStruct((spans, 2, tokens), jnp.float32),
    ]
    if step == 0:
        out_shape.append(jax.ShapeDtypeStruct((half, 2 * cols), jnp.bfloat16))
        state = (spans, rows, width)
    else:
        state = (tokens, width)
    return pl.pallas_call(
        functools.partial(project_kernel, step, spans),
        out_shape=out_shape,
        in_specs=[HBM_SPEC] * (6 + 2 * len(mine)),
        out_specs=[HBM_SPEC, HBM_SPEC, VMEM_SPEC, HBM_SPEC][: len(out_shape)],
        scratch_shapes=[
            pltpu.VMEM(state, jnp.bfloat16),
            pltpu.VMEM((tokens, width), jnp.bfloat16),
            pltpu.VMEM(table.shape, jnp.bfloat16),
            pltpu.VMEM(incoming.shape, jnp.bfloat16),
            pltpu.VMEM((2, 2 * cols), jnp.float32),
            pltpu.VMEM((spans, width), jnp.float32),
            pltpu.VMEM((spans, width), jnp.float32),
            pltpu.VMEM((3, cols, width), jnp.bfloat16),
            pltpu.VMEM((half, cols), jnp.bfloat16),
            pltpu.VMEM((half + 2 * tokens, cols), jnp.bfloat16),
            pltpu.VMEM((half, 2 * cols), jnp.bfloat16),
            pltpu.SemaphoreType.DMA((spans + 6,)),
        ],
        compiler_params=PARAMS,
        name="project",
    )(gain, table, incoming, *weights, *mine, *others)


def attend_kernel(
    step, spans, head_size, own_hbm, sent_hbm, got_hbm, squares_hbm, text_hbm, more_hbm,
    out_ref, own, sent, got, squares_ref, queries, keys, values, text_ref, more_ref, sems,
):
    copies = started(
        [
            (own_hbm, own),
            (sent_hbm, sent),
            (got_hbm, got),
            (squares_hbm, squares_ref),
            (text_hbm, text_ref),
            (more_hbm, more_ref),
        ],
        sems,
    )
    chip, core = own_place()
    first = core == 0
    half, width = queries.shape
    tokens = 2 * half
    rows = tokens // spans
    cols = width // 2
    finished(copies[:3])
    for target, mine_ref, low, size in (
        (queries, own, 0, half),
        (keys, sent, half, tokens),
        (values, sent, half + tokens, tokens),
    ):
        mine = mine_ref[low : low + size, :]
        other = got[low : low + size, :]
        target[:, :cols] = jnp.where(first, mine, other)
        target[:, cols:] = jnp.where(first, other, mine)
    copies[3].wait()
    factors = lax.rsqrt(jnp.sum(squares_ref[...], axis=0) / (width * (spans // 2)) + 1e-06)
    ident = lax.broadcasted_iota(jnp.int32, (tokens, tokens), 0) == lax.broadcasted_iota(
        jnp.int32, (tokens, tokens), 1
    )
    column = jnp.sum(jnp.where(ident, factors[0:1, :], 0.0), axis=1, keepdims=True)
    column = jnp.where(first, column[:half], column[half:]) * (1.0 / math.sqrt(head_size))
    row = factors[1:2, :]
    shape = (half, tokens)
    own_block = lax.broadcasted_iota(jnp.int32, shape, 0) // rows + core * (spans // 2)
    key_block = lax.broadcasted_iota(jnp.int32, shape, 1) // rows
    allowed = span_at(own_block, step, spans) >= span_at(key_block, step, spans)
    text_rows = text_ref.shape[0] * text_ref.shape[2]
    finished(copies[4:])
    heads = width // head_size
    lanes = [slice(head * head_size, (head + 1) * head_size) for head in range(heads)]
    stacked = jnp.concatenate([column] * heads, axis=0)
    scores = jnp.concatenate([contract_last(queries[:, at], keys[:, at]) for at in lanes], axis=0)
    scores = scores * stacked * row
    scores = jnp.where(jnp.concatenate([allowed] * heads, axis=0), scores, -1e30)
    parts = []
    for ref in (text_ref, more_ref):
        products = [
            contract_last(queries[:, at], ref[:, 0, :, at].reshape(text_rows, head_size))
            for at in lanes
        ]
        parts.append(jnp.concatenate(products, axis=0) * stacked)
    weights = jnp.exp(scores - jnp.max(scores, axis=1, keepdims=True))
    weights = weights * (1.0 / jnp.sum(weights, axis=1, keepdims=True))
    weights = weights.astype(jnp.bfloat16)
    most = jnp.max(jnp.maximum(*parts), axis=1, keepdims=True)
    parts = [jnp.exp(part - most) for part in parts]
    share = 1.0 / jnp.sum(parts[0] + parts[1], axis=1, keepdims=True)
    parts = [(part * share).astype(jnp.bfloat16) for part in parts]
    for head, at in enumerate(lanes):
        band = slice(head * half, (head + 1) * half)
        attended = jnp.dot(weights[band], values[:, at], preferred_element_type=jnp.float32)
        crossed = jnp.zeros((half, head_size), jnp.float32)
        for ref, part in zip((text_ref, more_ref), parts):
            text_values = ref[:, 1, :, at].reshape(text_rows, head_size)
            crossed = crossed + jnp.dot(
                part[band], text_values, preferred_element_type=jnp.float32
            )
        attended, crossed = (
            value.astype(jnp.bfloat16).astype(jnp.float32) for value in (attended, crossed)
        )
        out_ref[:, at] = (attended + crossed).astype(jnp.bfloat16)


def attend(step, spans, head_size, own, sent, got, squares, text, more):
    half, cols = own.shape
    tokens = 2 * half
    return pl.pallas_call(
        functools.partial(attend_kernel, step, spans, head_size),
        out_shape=jax.ShapeDtypeStruct((half, 2 * cols), jnp.bfloat16),
        in_specs=[HBM_SPEC] * 6,
        out_specs=VMEM_SPEC,
        scratch_shapes=[
            pltpu.VMEM(own.shape, jnp.bfloat16),
            pltpu.VMEM(sent.shape, jnp.bfloat16),
            pltpu.VMEM(got.shape, jnp.bfloat16),
            pltpu.VMEM(squares.shape, jnp.float32),
            pltpu.VMEM((half, 2 * cols), jnp.bfloat16),
            pltpu.VMEM((tokens, 2 * cols), jnp.bfloat16),
            pltpu.VMEM((tokens, 2 * cols), jnp.bfloat16),
            pltpu.VMEM(text.shape, jnp.bfloat16),
            pltpu.VMEM(more.shape, jnp.bfloat16),
            pltpu.SemaphoreType.DMA((6,)),
        ],
        compiler_params=PARAMS,
        name="attend",
    )(own, sent, got, squares, text, more)


def output_kernel(
    step, spans, last, current_hbm, table_hbm, incoming_hbm, own_hbm, other_hbm, *refs
):
    chips = spans // 2
    block_refs, refs = refs[:chips], refs[chips:]
    out_ref, blocks, current, gate_ref, entering, totals, weights, sems = refs
    chip, core = own_place()
    first = core == 0
    half, width = current.shape
    cols = width // 2
    rows = 2 * half // spans
    own_lanes = pl.ds(pl.multiple_of(chip * width, width), width)
    pairs = []
    for mask in range(chips):
        lanes = pl.ds(pl.multiple_of((chip ^ mask) * width, width), width)
        pairs.append((block_refs[mask], blocks.at[mask]))
        for side, ref in enumerate((own_hbm, other_hbm)):
            pairs.append((ref.at[:, lanes], weights.at[mask, side]))
    pairs.append((current_hbm, current))
    pairs.append((table_hbm.at[2, :, own_lanes], gate_ref))
    if not last:
        pairs.append((incoming_hbm.at[step + 1, :, own_lanes], entering))
    copies = started(pairs, sems)
    mine = jnp.zeros((half, cols), jnp.float32)
    other = jnp.zeros((half, cols), jnp.float32)
    for mask in range(chips):
        if mask % (chips // 2) == 0:
            finished(copies[3 * mask : 3 * (mask + chips // 2)])
        block = blocks[mask]
        mine = mine + contract_last(block, weights[mask, 0])
        other = other + contract_last(block, weights[mask, 1])
    totals[:, :cols] = jnp.where(first, mine, other)
    totals[:, cols:] = jnp.where(first, other, mine)
    finished(copies[3 * chips :])
    gates = gate_ref[...].astype(jnp.float32)
    gate = []
    for block in range(chips):
        places = [span_at(block + e * chips, step, spans) for e in range(2)]
        row = jnp.where(first, *(gates[s : s + 1, :] for s in places))
        gate.append(jnp.broadcast_to(row, (rows, width)))
    state = current[...].astype(jnp.float32) + jnp.concatenate(gate, axis=0) * totals[...]
    if last:
        for target in range(chips):
            block = (target - STEPS // 2) % chips
            out_ref[target] = state[block * rows : (block + 1) * rows, :].astype(jnp.bfloat16)
    else:
        parity, block = (spans - 2 - step) % 2, (spans - 2 - step) // 2
        replaced = lax.broadcasted_iota(jnp.int32, (half, width), 0) // rows == block
        fresh = jnp.concatenate([entering[...].astype(jnp.float32)] * chips, axis=0)
        state = jnp.where(replaced & (core == parity), fresh, state)
        out_ref[...] = state.astype(jnp.bfloat16)


def output(step, spans, last, current, table, incoming, own, other, blocks):
    half, width = current.shape
    chips = spans // 2
    rows = 2 * half // spans
    return pl.pallas_call(
        functools.partial(output_kernel, step, spans, last),
        out_shape=jax.ShapeDtypeStruct(
            (chips, rows, width) if last else (half, width), jnp.bfloat16
        ),
        in_specs=[HBM_SPEC] * (5 + chips),
        out_specs=VMEM_SPEC,
        scratch_shapes=[
            pltpu.VMEM((chips, half, width), jnp.bfloat16),
            pltpu.VMEM((half, width), jnp.bfloat16),
            pltpu.VMEM((spans, width), jnp.bfloat16),
            pltpu.VMEM((rows, width), jnp.bfloat16),
            pltpu.VMEM((half, width), jnp.float32),
            pltpu.VMEM((chips, 2, width // 2, width), jnp.bfloat16),
            pltpu.SemaphoreType.DMA((3 * chips + 3,)),
        ],
        compiler_params=PARAMS,
        name="output",
    )(current, table, incoming, own, other, *blocks)


def join_kernel(in_ref, out_ref):
    chips, _, width = in_ref.shape
    for source in range(chips):
        out_ref[:, source * width : (source + 1) * width] = in_ref[source]


def join(blocks):
    chips, rows, width = blocks.shape
    return pl.pallas_call(
        join_kernel,
        out_shape=jax.ShapeDtypeStruct((rows, width * chips), jnp.bfloat16),
        in_specs=[VMEM_SPEC],
        out_specs=VMEM_SPEC,
        compiler_params=PARAMS,
        name="join",
    )(blocks)


def arrange_kernel(spans, keys_ref, values_ref, out_ref):
    width = out_ref.shape[3]
    text_half = out_ref.shape[2]
    for device in range(spans):
        lanes = slice(device // 2 * width, (device // 2 + 1) * width)
        band = slice(device % 2 * text_half, (device % 2 + 1) * text_half)
        out_ref[device, 0] = keys_ref[band, lanes]
        out_ref[device, 1] = values_ref[band, lanes]


def arrange(spans, keys, values):
    text_half = keys.shape[0] // 2
    return pl.pallas_call(
        functools.partial(arrange_kernel, spans),
        out_shape=jax.ShapeDtypeStruct(
            (spans, 2, text_half, 2 * keys.shape[1] // spans), jnp.bfloat16
        ),
        in_specs=[VMEM_SPEC] * 2,
        out_specs=VMEM_SPEC,
        compiler_params=PARAMS,
        name="arrange",
    )(keys, values)


def paired_device(
    hidden,
    incoming,
    levels,
    mod_table,
    query_weight,
    key_weight,
    value_weight,
    output_weight,
    query_gain,
    key_gain,
    text_keys,
    text_values,
):
    spans = lax.axis_size("queue")
    chips = spans // 2
    head_size = hidden.shape[1] // HEADS
    mine = gathered_over_chips(hidden)
    others = [swapped(block, 1) for block in mine]
    picked = (levels[:, None] == jnp.arange(mod_table.shape[0])[None, :]).astype(mod_table.dtype)
    table = jnp.einsum("sl,ltd->tsd", picked, mod_table, preferred_element_type=jnp.float32)
    table = table.astype(jnp.bfloat16)
    gain = jnp.stack([query_gain, key_gain])
    weights = [w.T for w in (query_weight, key_weight, value_weight)]
    output_own = output_weight.T
    output_other = swapped(output_own, 1)
    text = arrange(spans, text_keys, text_values)
    text, table, gain = lax.optimization_barrier((text, table, gain, *mine))[:3]
    text = lax.all_to_all(text, "queue", split_axis=0, concat_axis=0, tiled=True)
    current = None
    for step in range(STEPS):
        last = step == STEPS - 1
        own, send, squares, *rest = project(
            step, spans, gain, table, incoming, mine, others, weights
        )
        got = swapped(send, 1)
        squares = lax.all_to_all(squares, "queue", split_axis=0, concat_axis=0, tiled=True)
        if step == 0:
            current = rest[0]
            text = lax.optimization_barrier((text, send))[0]
            more = swapped(text, 1)
        block = attend(step, spans, head_size, own, send, got, squares, text, more)
        blocks = gathered_over_chips(block)
        result = output(
            step, spans, last, current, table, incoming, output_own, output_other, blocks
        )
        if not last:
            current = result
            mine = gathered_over_chips(current)
            others = [swapped(block, 1) for block in mine]
    same_core = [[2 * c + core for c in range(chips)] for core in range(2)]
    result = lax.all_to_all(
        result, "queue", split_axis=0, concat_axis=2, tiled=True, axis_index_groups=same_core
    )
    return result[0]


def held_in_pairs(mesh, hidden, query_weight):
    spans = mesh.shape["queue"]
    rows = hidden.shape[0] // (mesh.shape["groups"] * spans)
    cols = query_weight.shape[1] // spans
    head_size = query_weight.shape[0] // HEADS
    power = spans & (spans - 1) == 0
    return STEPS % 2 == 0 and power and spans >= 4 and 2 * cols % head_size == 0 and rows * spans == 128 and rows == 8


def solution(mesh):
    in_specs = (
        P(("groups", "queue"), None),
        P(None, "groups", None),
        P(),
        P(),
        P(None, "queue"),
        P(None, "queue"),
        P(None, "queue"),
        P(None, "queue"),
        P(),
        P(),
        P(("groups", "queue"), None),
        P(("groups", "queue"), None),
    )
    out_specs = P(("groups", "queue"), None)

    def apply(*args):
        body = paired_device if held_in_pairs(mesh, args[0], args[4]) else per_device
        return jax.shard_map(
            body, mesh=mesh, in_specs=in_specs, out_specs=out_specs, check_vma=False
        )(*args)

    return apply
```

```python
import functools
import math

import jax
import jax.numpy as jnp
from jax import lax
from jax.experimental import pallas as pl
from jax.experimental.pallas import tpu as pltpu
from jax.sharding import PartitionSpec as P

HEADS = 40
STEPS = 2


def passed_along(value, axis, steps):
    count = lax.axis_size(axis)
    initial, last = (max(0, -steps), min(count, count - steps))
    return lax.ppermute(value, axis, [(source, source + steps) for source in range(initial, last)])


def normalize(values):
    return values * lax.rsqrt(jnp.mean(values * values, axis=-1, keepdims=True) + 1e-06)


def softmax_rounded(scores):
    row_max = jnp.max(scores, axis=-1, keepdims=True)
    weights = jnp.exp(scores - row_max)
    return (weights / jnp.sum(weights, axis=-1, keepdims=True)).astype(jnp.bfloat16)


def pad_slots(values, slot_total):
    missing = slot_total - values.shape[1]
    filler = jnp.zeros((values.shape[0], missing, values.shape[2]), values.dtype)
    return jnp.concatenate([values, filler], axis=1)


def causal_block(queries, keys_all, values_all, span_rows, score_scale):
    total_rows = queries.shape[0]
    block_rows = min(512, total_rows)
    scores = (
        jnp.einsum("qsd,ksd->sqk", queries, keys_all, preferred_element_type=jnp.float32)
        * score_scale
    )
    allowed = (
        jnp.arange(0, block_rows)[:, None] // span_rows
        >= jnp.arange(block_rows)[None, :] // span_rows
    )
    scores = jnp.where(allowed[None], scores, -1e30)
    result = jnp.einsum(
        "sqk,ksd->qsd", softmax_rounded(scores), values_all, preferred_element_type=jnp.float32
    )
    pieces = result.astype(jnp.bfloat16)
    return pieces


def text_attend(queries, text_k, text_v, score_scale):
    scores = (
        jnp.einsum("qsd,tsd->sqt", queries, text_k, preferred_element_type=jnp.float32)
        * score_scale
    )
    return jnp.einsum(
        "sqt,tsd->qsd", softmax_rounded(scores), text_v, preferred_element_type=jnp.float32
    ).astype(jnp.bfloat16)


def per_device(
    hidden,
    incoming,
    levels,
    mod_table,
    query_weight,
    key_weight,
    value_weight,
    output_weight,
    query_gain,
    key_gain,
    text_keys,
    text_values,
):
    own_index = lax.axis_index("queue")
    queue_size = lax.axis_size("queue")
    span_rows, model_width = hidden.shape
    head_size = model_width // HEADS
    score_scale = 1.0 / math.sqrt(head_size)
    slot_total = -(-HEADS // queue_size) * queue_size
    own_level = lax.dynamic_index_in_dim(levels, own_index, 0, keepdims=False)
    modulation = lax.dynamic_index_in_dim(mod_table, own_level, 0, keepdims=False).astype(
        jnp.float32
    )
    stacked_weights = jnp.stack([query_weight, key_weight, value_weight])
    text_local = text_keys.shape[0]
    text_k_slots, text_v_slots = (
        lax.all_to_all(
            pad_slots(text_keys.reshape(text_local, HEADS, head_size), slot_total),
            "queue",
            split_axis=1,
            concat_axis=0,
            tiled=True,
        ),
        lax.all_to_all(
            pad_slots(text_values.reshape(text_local, HEADS, head_size), slot_total),
            "queue",
            split_axis=1,
            concat_axis=0,
            tiled=True,
        ),
    )
    queue_state = hidden
    for section_index in range(STEPS):
        shifted = passed_along(queue_state, "queue", 1)
        queue_state = jnp.where(own_index == 0, incoming[section_index], shifted)
        current = queue_state.astype(jnp.float32)
        modulated = (normalize(current) * (1.0 + modulation[1]) + modulation[0]).astype(
            jnp.bfloat16
        )
        columns = jnp.einsum(
            "rd,cdw->crw",
            lax.all_gather(modulated, "queue", axis=0, tiled=True),
            stacked_weights,
            preferred_element_type=jnp.float32,
        )
        own_rows = lax.all_to_all(
            columns.astype(jnp.bfloat16), "queue", split_axis=1, concat_axis=2, tiled=True
        ).astype(columns.dtype)
        query_heads = (
            (normalize(own_rows[0]) * query_gain)
            .astype(jnp.bfloat16)
            .reshape(span_rows, HEADS, head_size)
        )
        key_heads = (
            (normalize(own_rows[1]) * key_gain)
            .astype(jnp.bfloat16)
            .reshape(span_rows, HEADS, head_size)
        )
        value_heads = own_rows[2].astype(jnp.bfloat16).reshape(span_rows, HEADS, head_size)
        query_slots, key_slots, value_slots = (
            lax.all_to_all(
                pad_slots(query_heads, slot_total), "queue", split_axis=1, concat_axis=0, tiled=True
            ),
            lax.all_to_all(
                pad_slots(key_heads, slot_total), "queue", split_axis=1, concat_axis=0, tiled=True
            ),
            lax.all_to_all(
                pad_slots(value_heads, slot_total), "queue", split_axis=1, concat_axis=0, tiled=True
            ),
        )
        attended_slots = causal_block(query_slots, key_slots, value_slots, span_rows, score_scale)
        crossed_slots = text_attend(query_slots, text_k_slots, text_v_slots, score_scale)
        attended_back, crossed_back = (
            lax.all_to_all(attended_slots, "queue", split_axis=0, concat_axis=1, tiled=True),
            lax.all_to_all(crossed_slots, "queue", split_axis=0, concat_axis=1, tiled=True),
        )
        attended = attended_back[:, :HEADS]
        crossed = crossed_back[:, :HEADS]
        combined = (
            (attended.astype(jnp.float32) + crossed.astype(jnp.float32))
            .astype(jnp.bfloat16)
            .reshape(span_rows, model_width)
        )
        out_columns = jnp.dot(
            lax.all_gather(combined, "queue", axis=0, tiled=True),
            output_weight,
            preferred_element_type=jnp.float32,
        )
        projected = lax.all_to_all(
            out_columns.astype(jnp.bfloat16), "queue", split_axis=0, concat_axis=1, tiled=True
        ).astype(out_columns.dtype)
        queue_state = (current + modulation[2] * projected).astype(jnp.bfloat16)
    return queue_state


def swapped(value, bit):
    count = lax.axis_size("queue")
    return lax.ppermute(value, "queue", [(source, source ^ bit) for source in range(count)])


def gathered_over_chips(block):
    chips = lax.axis_size("queue") // 2
    blocks = {0: block}
    for mask in range(2, chips, 2):
        blocks[mask] = swapped(block, 2 * mask)
    for mask in range(0, chips, 2):
        blocks[mask + 1] = swapped(blocks[mask], 2)
    return [blocks[mask] for mask in range(chips)]


def contract_last(left, right):
    return lax.dot_general(
        left, right, (((1,), (1,)), ((), ())), preferred_element_type=jnp.float32
    )


HBM_SPEC = pl.BlockSpec(memory_space=pltpu.HBM)
VMEM_SPEC = pl.BlockSpec(memory_space=pltpu.VMEM)
PARAMS = pltpu.CompilerParams(vmem_limit_bytes=60 * 1024 * 1024)
MIDDLE_PARAMS = pltpu.CompilerParams(vmem_limit_bytes=52 * 1024 * 1024)
SMALL_PARAMS = pltpu.CompilerParams(vmem_limit_bytes=16 * 1024 * 1024)


def span_at(position, step, spans):
    chips = spans // 2
    return (2 * (position % chips) + position // chips + step + 1) % spans


def own_place():
    own_index = lax.axis_index("queue")
    return own_index // 2, own_index % 2


def started(pairs, sems):
    copies = [
        pltpu.make_async_copy(source, target, sems.at[i]) for i, (source, target) in enumerate(pairs)
    ]
    for copy in copies:
        copy.start()
    return copies


def finished(copies):
    for copy in copies:
        copy.wait()


def project_kernel(step, spans, gain_hbm, table_hbm, incoming_hbm, *refs):
    chips = spans // 2
    weight_refs, refs = refs[:3], refs[3:]
    mine, others = refs[:chips], refs[chips : 2 * chips]
    refs = refs[2 * chips :]
    own_hbm, send_hbm, squares_ref = refs[:3]
    refs = refs[3:]
    if step == 0:
        current_hbm, refs = refs[0], refs[1:]
    state, modulated, table, entering, gain, scale_ref, shift_ref, own, send, current, sems = refs[:11]
    fetched = step == 0
    weights = refs[11] if fetched else weight_refs
    chip, core = own_place()
    tokens, width = modulated.shape
    half = tokens // 2
    rows = tokens // spans
    pair = 2 * rows
    cols = weight_refs[0].shape[0]
    first = core == 0
    own_lanes = pl.ds(pl.multiple_of(chip * 2 * cols, 2 * cols), 2 * cols)
    pairs = []
    for side, blocks in enumerate((mine, others)):
        owner = core if side == 0 else 1 - core
        for mask in range(chips):
            other_chip = chip ^ mask
            if step == 0:
                target = state.at[owner * chips + other_chip]
            else:
                lanes = pl.ds(pl.multiple_of(other_chip * 2 * cols, 2 * cols), 2 * cols)
                target = state.at[pl.ds(pl.multiple_of(owner * half, half), half), lanes]
            pairs.append((blocks[mask], target))
    pairs += [(table_hbm, table), (gain_hbm.at[:, own_lanes], gain), (incoming_hbm, entering)]
    inputs = len(pairs)
    if fetched:
        pairs += [(weight_refs[i], weights.at[i]) for i in range(3)]
    copies = started(pairs, sems)
    copies, fetches = copies[:inputs], copies[inputs:]
    finished(copies)
    shift_ref[...] = table[0].astype(jnp.float32)
    scale_ref[...] = table[1].astype(jnp.float32) + 1.0
    leaving = []
    if step == 0:
        state[spans - 1] = entering[step]
        for slab in range(chips // 2):
            at = core * chips + 2 * slab
            both = [state[at + e, :, own_lanes].astype(jnp.float32) for e in range(2)]
            current[slab * pair : (slab + 1) * pair, :] = jnp.concatenate(both, axis=0).astype(
                jnp.bfloat16
            )
        leaving += started([(current, current_hbm)], sems.at[pl.ds(0, 1)])
    pieces = 4
    piece = width // pieces
    for slab in range(chips):
        band = slice(slab * pair, (slab + 1) * pair)

        def load(part):
            if step == 0:
                both = [state[2 * slab + e, :, part].astype(jnp.float32) for e in range(2)]
                return jnp.concatenate(both, axis=0)
            return state[band, part].astype(jnp.float32)

        total = jnp.zeros((pair, 1), jnp.float32)
        for low in range(0, width, piece):
            x = load(slice(low, low + piece))
            total = total + jnp.sum(x * x, axis=1, keepdims=True)
        factor = lax.rsqrt(total / width + 1e-06)
        at = [span_at(2 * slab + e, step, spans) for e in range(2)]
        for low in range(0, width, piece):
            part = slice(low, low + piece)
            x = load(part) * factor
            scale, shift = (
                jnp.concatenate(
                    [jnp.broadcast_to(ref[s : s + 1, part], (rows, piece)) for s in at], axis=0
                )
                for ref in (scale_ref, shift_ref)
            )
            modulated[band, part] = (x * scale + shift).astype(jnp.bfloat16)
    ident = lax.broadcasted_iota(jnp.int32, (tokens, tokens), 0) == lax.broadcasted_iota(
        jnp.int32, (tokens, tokens), 1
    )
    products = []
    for fetch, weight in ((fetches[:1], 0), (fetches[1:], 1), ([], 2)):
        finished(fetch)
        products.append(contract_last(modulated[...], weights[weight][...]))
    shape = (tokens, tokens)
    ident = lax.broadcasted_iota(jnp.int32, shape, 0) == lax.broadcasted_iota(jnp.int32, shape, 1)
    for i in range(2):
        column = jnp.sum(products[i] * products[i], axis=1, keepdims=True)
        line = jnp.sum(jnp.where(ident, column, 0.0), axis=0, keepdims=True)
        squares_ref[:, i : i + 1, :] = jnp.broadcast_to(line[None], (spans, 1, tokens))
        line = gain[i : i + 1, :]
        products[i] = products[i] * jnp.where(first, line[:, :cols], line[:, cols:])
    low, high = products[0][:half], products[0][half:]
    own[...] = jnp.where(first, low, high).astype(jnp.bfloat16)
    send[:half, :] = jnp.where(first, high, low).astype(jnp.bfloat16)
    send[half : half + tokens, :] = products[1].astype(jnp.bfloat16)
    send[half + tokens :, :] = products[2].astype(jnp.bfloat16)
    leaving += started([(own, own_hbm), (send, send_hbm)], sems.at[pl.ds(1, 2)])
    finished(leaving)


def project(step, spans, gain, table, incoming, mine, others, weights):
    rows = incoming.shape[1]
    tokens = spans * rows
    cols, width = weights[0].shape
    half = tokens // 2
    out_shape = [
        jax.ShapeDtypeStruct((half, cols), jnp.bfloat16),
        jax.ShapeDtypeStruct((half + 2 * tokens, cols), jnp.bfloat16),
        jax.ShapeDtypeStruct((spans, 2, tokens), jnp.float32),
    ]
    if step == 0:
        out_shape.append(jax.ShapeDtypeStruct((half, 2 * cols), jnp.bfloat16))
        state = (spans, rows, width)
    else:
        state = (tokens, width)
    return pl.pallas_call(
        functools.partial(project_kernel, step, spans),
        out_shape=out_shape,
        in_specs=[HBM_SPEC] * 3
        + [HBM_SPEC if step == 0 else VMEM_SPEC] * 3
        + [HBM_SPEC] * (2 * len(mine)),
        out_specs=[HBM_SPEC, HBM_SPEC, VMEM_SPEC, HBM_SPEC][: len(out_shape)],
        scratch_shapes=[
            pltpu.VMEM(state, jnp.bfloat16),
            pltpu.VMEM((tokens, width), jnp.bfloat16),
            pltpu.VMEM(table.shape, jnp.bfloat16),
            pltpu.VMEM(incoming.shape, jnp.bfloat16),
            pltpu.VMEM((2, 2 * cols), jnp.float32),
            pltpu.VMEM((spans, width), jnp.float32),
            pltpu.VMEM((spans, width), jnp.float32),
            pltpu.VMEM((half, cols), jnp.bfloat16),
            pltpu.VMEM((half + 2 * tokens, cols), jnp.bfloat16),
            pltpu.VMEM((half, 2 * cols), jnp.bfloat16),
            pltpu.SemaphoreType.DMA((spans + 6,)),
        ]
        + ([pltpu.VMEM((3, cols, width), jnp.bfloat16)] if step == 0 else []),
        compiler_params=PARAMS if step == 0 else SMALL_PARAMS,
        name="project",
    )(gain, table, incoming, *weights, *mine, *others)


def attend_kernel(
    step, spans, head_size, own_hbm, sent_hbm, got_hbm, squares_hbm, text_hbm, more_hbm,
    out_ref, own, sent, got, squares_ref, queries, keys, values, text_ref, more_ref, sems,
):
    copies = started(
        [
            (own_hbm, own),
            (sent_hbm, sent),
            (got_hbm, got),
            (squares_hbm, squares_ref),
            (text_hbm, text_ref),
            (more_hbm, more_ref),
        ],
        sems,
    )
    chip, core = own_place()
    first = core == 0
    half, width = queries.shape
    tokens = 2 * half
    rows = tokens // spans
    cols = width // 2
    finished(copies[:3])
    for target, mine_ref, low, size in (
        (queries, own, 0, half),
        (keys, sent, half, tokens),
        (values, sent, half + tokens, tokens),
    ):
        mine = mine_ref[low : low + size, :]
        other = got[low : low + size, :]
        target[:, :cols] = jnp.where(first, mine, other)
        target[:, cols:] = jnp.where(first, other, mine)
    copies[3].wait()
    factors = lax.rsqrt(jnp.sum(squares_ref[...], axis=0) / (width * (spans // 2)) + 1e-06)
    ident = lax.broadcasted_iota(jnp.int32, (tokens, tokens), 0) == lax.broadcasted_iota(
        jnp.int32, (tokens, tokens), 1
    )
    column = jnp.sum(jnp.where(ident, factors[0:1, :], 0.0), axis=1, keepdims=True)
    column = jnp.where(first, column[:half], column[half:]) * (1.0 / math.sqrt(head_size))
    row = factors[1:2, :]
    shape = (half, tokens)
    own_block = lax.broadcasted_iota(jnp.int32, shape, 0) // rows + core * (spans // 2)
    key_block = lax.broadcasted_iota(jnp.int32, shape, 1) // rows
    allowed = span_at(own_block, step, spans) >= span_at(key_block, step, spans)
    text_rows = text_ref.shape[0] * text_ref.shape[2]
    finished(copies[4:])
    heads = width // head_size
    lanes = [slice(head * head_size, (head + 1) * head_size) for head in range(heads)]
    stacked = jnp.concatenate([column] * heads, axis=0)
    scores = jnp.concatenate([contract_last(queries[:, at], keys[:, at]) for at in lanes], axis=0)
    scores = scores * stacked * row
    scores = jnp.where(jnp.concatenate([allowed] * heads, axis=0), scores, -1e30)
    parts = []
    for ref in (text_ref, more_ref):
        products = [
            contract_last(queries[:, at], ref[:, 0, :, at].reshape(text_rows, head_size))
            for at in lanes
        ]
        parts.append(jnp.concatenate(products, axis=0) * stacked)
    weights = jnp.exp(scores - jnp.max(scores, axis=1, keepdims=True))
    weights = weights * (1.0 / jnp.sum(weights, axis=1, keepdims=True))
    weights = weights.astype(jnp.bfloat16)
    most = jnp.max(jnp.maximum(*parts), axis=1, keepdims=True)
    parts = [jnp.exp(part - most) for part in parts]
    share = 1.0 / jnp.sum(parts[0] + parts[1], axis=1, keepdims=True)
    parts = [(part * share).astype(jnp.bfloat16) for part in parts]
    for head, at in enumerate(lanes):
        band = slice(head * half, (head + 1) * half)
        attended = jnp.dot(weights[band], values[:, at], preferred_element_type=jnp.float32)
        crossed = jnp.zeros((half, head_size), jnp.float32)
        for ref, part in zip((text_ref, more_ref), parts):
            text_values = ref[:, 1, :, at].reshape(text_rows, head_size)
            crossed = crossed + jnp.dot(
                part[band], text_values, preferred_element_type=jnp.float32
            )
        attended, crossed = (
            value.astype(jnp.bfloat16).astype(jnp.float32) for value in (attended, crossed)
        )
        out_ref[:, at] = (attended + crossed).astype(jnp.bfloat16)


def attend(step, spans, head_size, own, sent, got, squares, text, more):
    half, cols = own.shape
    tokens = 2 * half
    return pl.pallas_call(
        functools.partial(attend_kernel, step, spans, head_size),
        out_shape=jax.ShapeDtypeStruct((half, 2 * cols), jnp.bfloat16),
        in_specs=[HBM_SPEC] * 6,
        out_specs=VMEM_SPEC,
        scratch_shapes=[
            pltpu.VMEM(own.shape, jnp.bfloat16),
            pltpu.VMEM(sent.shape, jnp.bfloat16),
            pltpu.VMEM(got.shape, jnp.bfloat16),
            pltpu.VMEM(squares.shape, jnp.float32),
            pltpu.VMEM((half, 2 * cols), jnp.bfloat16),
            pltpu.VMEM((tokens, 2 * cols), jnp.bfloat16),
            pltpu.VMEM((tokens, 2 * cols), jnp.bfloat16),
            pltpu.VMEM(text.shape, jnp.bfloat16),
            pltpu.VMEM(more.shape, jnp.bfloat16),
            pltpu.SemaphoreType.DMA((6,)),
        ],
        compiler_params=PARAMS,
        name="attend",
    )(own, sent, got, squares, text, more)


def output_kernel(
    step, spans, last, current_hbm, table_hbm, incoming_hbm, own_hbm, other_hbm, *refs
):
    chips = spans // 2
    block_refs, refs = refs[:chips], refs[chips:]
    out_ref, blocks, current, gate_ref, entering, totals, weights, sems = refs
    chip, core = own_place()
    first = core == 0
    half, width = current.shape
    cols = width // 2
    rows = 2 * half // spans
    own_lanes = pl.ds(pl.multiple_of(chip * width, width), width)
    pairs = []
    for mask in range(chips):
        lanes = pl.ds(pl.multiple_of((chip ^ mask) * width, width), width)
        pairs.append((block_refs[mask], blocks.at[mask]))
        for side, ref in enumerate((own_hbm, other_hbm)):
            pairs.append((ref.at[:, lanes], weights.at[mask, side]))
    pairs.append((current_hbm, current))
    pairs.append((table_hbm.at[2, :, own_lanes], gate_ref))
    if not last:
        pairs.append((incoming_hbm.at[step + 1, :, own_lanes], entering))
    copies = started(pairs, sems)
    mine = jnp.zeros((half, cols), jnp.float32)
    other = jnp.zeros((half, cols), jnp.float32)
    for mask in range(chips):
        if mask % (chips // 2) == 0:
            finished(copies[3 * mask : 3 * (mask + chips // 2)])
        block = blocks[mask]
        mine = mine + contract_last(block, weights[mask, 0])
        other = other + contract_last(block, weights[mask, 1])
    totals[:, :cols] = jnp.where(first, mine, other)
    totals[:, cols:] = jnp.where(first, other, mine)
    finished(copies[3 * chips :])
    gates = gate_ref[...].astype(jnp.float32)
    gate = []
    for block in range(chips):
        places = [span_at(block + e * chips, step, spans) for e in range(2)]
        row = jnp.where(first, *(gates[s : s + 1, :] for s in places))
        gate.append(jnp.broadcast_to(row, (rows, width)))
    state = current[...].astype(jnp.float32) + jnp.concatenate(gate, axis=0) * totals[...]
    if last:
        for target in range(chips):
            block = (target - STEPS // 2) % chips
            out_ref[target] = state[block * rows : (block + 1) * rows, :].astype(jnp.bfloat16)
    else:
        parity, block = (spans - 2 - step) % 2, (spans - 2 - step) // 2
        replaced = lax.broadcasted_iota(jnp.int32, (half, width), 0) // rows == block
        fresh = jnp.concatenate([entering[...].astype(jnp.float32)] * chips, axis=0)
        state = jnp.where(replaced & (core == parity), fresh, state)
        out_ref[...] = state.astype(jnp.bfloat16)


def output(step, spans, last, current, table, incoming, own, other, blocks):
    half, width = current.shape
    chips = spans // 2
    rows = 2 * half // spans
    return pl.pallas_call(
        functools.partial(output_kernel, step, spans, last),
        out_shape=jax.ShapeDtypeStruct(
            (chips, rows, width) if last else (half, width), jnp.bfloat16
        ),
        in_specs=[HBM_SPEC] * (5 + chips),
        out_specs=VMEM_SPEC,
        scratch_shapes=[
            pltpu.VMEM((chips, half, width), jnp.bfloat16),
            pltpu.VMEM((half, width), jnp.bfloat16),
            pltpu.VMEM((spans, width), jnp.bfloat16),
            pltpu.VMEM((rows, width), jnp.bfloat16),
            pltpu.VMEM((half, width), jnp.float32),
            pltpu.VMEM((chips, 2, width // 2, width), jnp.bfloat16),
            pltpu.SemaphoreType.DMA((3 * chips + 3,)),
        ],
        compiler_params=PARAMS if last else MIDDLE_PARAMS,
        name="output",
    )(current, table, incoming, own, other, *blocks)


def arrange_kernel(spans, keys_ref, values_ref, out_ref):
    width = out_ref.shape[3]
    text_half = out_ref.shape[2]
    for device in range(spans):
        lanes = slice(device // 2 * width, (device // 2 + 1) * width)
        band = slice(device % 2 * text_half, (device % 2 + 1) * text_half)
        out_ref[device, 0] = keys_ref[band, lanes]
        out_ref[device, 1] = values_ref[band, lanes]


def arrange(spans, keys, values):
    text_half = keys.shape[0] // 2
    return pl.pallas_call(
        functools.partial(arrange_kernel, spans),
        out_shape=jax.ShapeDtypeStruct(
            (spans, 2, text_half, 2 * keys.shape[1] // spans), jnp.bfloat16
        ),
        in_specs=[VMEM_SPEC] * 2,
        out_specs=VMEM_SPEC,
        compiler_params=PARAMS,
        name="arrange",
    )(keys, values)


def paired_device(
    hidden,
    incoming,
    levels,
    mod_table,
    query_weight,
    key_weight,
    value_weight,
    output_weight,
    query_gain,
    key_gain,
    text_keys,
    text_values,
):
    spans = lax.axis_size("queue")
    chips = spans // 2
    head_size = hidden.shape[1] // HEADS
    mine = gathered_over_chips(hidden)
    others = [swapped(block, 1) for block in mine]
    picked = (levels[:, None] == jnp.arange(mod_table.shape[0])[None, :]).astype(mod_table.dtype)
    table = jnp.einsum("sl,ltd->tsd", picked, mod_table, preferred_element_type=jnp.float32)
    table = table.astype(jnp.bfloat16)
    gain = jnp.stack([query_gain, key_gain])
    weights = [w.T for w in (query_weight, key_weight, value_weight)]
    output_own = output_weight.T
    output_other = swapped(output_own, 1)
    text = arrange(spans, text_keys, text_values)
    text, table, gain = lax.optimization_barrier((text, table, gain, *mine))[:3]
    text = lax.all_to_all(text, "queue", split_axis=0, concat_axis=0, tiled=True)
    current = None
    for step in range(STEPS):
        last = step == STEPS - 1
        own, send, squares, *rest = project(
            step, spans, gain, table, incoming, mine, others, weights
        )
        got = swapped(send, 1)
        squares = lax.all_to_all(squares, "queue", split_axis=0, concat_axis=0, tiled=True)
        if step == 0:
            current = rest[0]
            text = lax.optimization_barrier((text, send))[0]
            more = swapped(text, 1)
        block = attend(step, spans, head_size, own, send, got, squares, text, more)
        blocks = gathered_over_chips(block)
        result = output(
            step, spans, last, current, table, incoming, output_own, output_other, blocks
        )
        if not last:
            current = result
            mine = gathered_over_chips(current)
            others = [swapped(block, 1) for block in mine]
    same_core = [[2 * c + core for c in range(chips)] for core in range(2)]
    result = lax.all_to_all(
        result, "queue", split_axis=0, concat_axis=2, tiled=True, axis_index_groups=same_core
    )
    return result[0]


def held_in_pairs(mesh, hidden, query_weight):
    spans = mesh.shape["queue"]
    rows = hidden.shape[0] // (mesh.shape["groups"] * spans)
    cols = query_weight.shape[1] // spans
    head_size = query_weight.shape[0] // HEADS
    power = spans & (spans - 1) == 0
    return STEPS % 2 == 0 and power and spans >= 4 and 2 * cols % head_size == 0 and rows * spans == 128 and rows == 8


def solution(mesh):
    in_specs = (
        P(("groups", "queue"), None),
        P(None, "groups", None),
        P(),
        P(),
        P(None, "queue"),
        P(None, "queue"),
        P(None, "queue"),
        P(None, "queue"),
        P(),
        P(),
        P(("groups", "queue"), None),
        P(("groups", "queue"), None),
    )
    out_specs = P(("groups", "queue"), None)

    def apply(*args):
        body = paired_device if held_in_pairs(mesh, args[0], args[4]) else per_device
        return jax.shard_map(
            body, mesh=mesh, in_specs=in_specs, out_specs=out_specs, check_vma=False
        )(*args)

    return apply
```

```python
import functools
import math

import jax
import jax.numpy as jnp
from jax import lax
from jax.experimental import pallas as pl
from jax.experimental.pallas import tpu as pltpu
from jax.sharding import PartitionSpec as P

HEADS = 40
STEPS = 2


def passed_along(value, axis, steps):
    count = lax.axis_size(axis)
    initial, last = (max(0, -steps), min(count, count - steps))
    return lax.ppermute(value, axis, [(source, source + steps) for source in range(initial, last)])


def normalize(values):
    return values * lax.rsqrt(jnp.mean(values * values, axis=-1, keepdims=True) + 1e-06)


def softmax_rounded(scores):
    row_max = jnp.max(scores, axis=-1, keepdims=True)
    weights = jnp.exp(scores - row_max)
    return (weights / jnp.sum(weights, axis=-1, keepdims=True)).astype(jnp.bfloat16)


def pad_slots(values, slot_total):
    missing = slot_total - values.shape[1]
    filler = jnp.zeros((values.shape[0], missing, values.shape[2]), values.dtype)
    return jnp.concatenate([values, filler], axis=1)


def causal_block(queries, keys_all, values_all, span_rows, score_scale):
    total_rows = queries.shape[0]
    block_rows = min(512, total_rows)
    scores = (
        jnp.einsum("qsd,ksd->sqk", queries, keys_all, preferred_element_type=jnp.float32)
        * score_scale
    )
    allowed = (
        jnp.arange(0, block_rows)[:, None] // span_rows
        >= jnp.arange(block_rows)[None, :] // span_rows
    )
    scores = jnp.where(allowed[None], scores, -1e30)
    result = jnp.einsum(
        "sqk,ksd->qsd", softmax_rounded(scores), values_all, preferred_element_type=jnp.float32
    )
    pieces = result.astype(jnp.bfloat16)
    return pieces


def text_attend(queries, text_k, text_v, score_scale):
    scores = (
        jnp.einsum("qsd,tsd->sqt", queries, text_k, preferred_element_type=jnp.float32)
        * score_scale
    )
    return jnp.einsum(
        "sqt,tsd->qsd", softmax_rounded(scores), text_v, preferred_element_type=jnp.float32
    ).astype(jnp.bfloat16)


def per_device(
    hidden,
    incoming,
    levels,
    mod_table,
    query_weight,
    key_weight,
    value_weight,
    output_weight,
    query_gain,
    key_gain,
    text_keys,
    text_values,
):
    own_index = lax.axis_index("queue")
    queue_size = lax.axis_size("queue")
    span_rows, model_width = hidden.shape
    head_size = model_width // HEADS
    score_scale = 1.0 / math.sqrt(head_size)
    slot_total = -(-HEADS // queue_size) * queue_size
    own_level = lax.dynamic_index_in_dim(levels, own_index, 0, keepdims=False)
    modulation = lax.dynamic_index_in_dim(mod_table, own_level, 0, keepdims=False).astype(
        jnp.float32
    )
    stacked_weights = jnp.stack([query_weight, key_weight, value_weight])
    text_local = text_keys.shape[0]
    text_k_slots, text_v_slots = (
        lax.all_to_all(
            pad_slots(text_keys.reshape(text_local, HEADS, head_size), slot_total),
            "queue",
            split_axis=1,
            concat_axis=0,
            tiled=True,
        ),
        lax.all_to_all(
            pad_slots(text_values.reshape(text_local, HEADS, head_size), slot_total),
            "queue",
            split_axis=1,
            concat_axis=0,
            tiled=True,
        ),
    )
    queue_state = hidden
    for section_index in range(STEPS):
        shifted = passed_along(queue_state, "queue", 1)
        queue_state = jnp.where(own_index == 0, incoming[section_index], shifted)
        current = queue_state.astype(jnp.float32)
        modulated = (normalize(current) * (1.0 + modulation[1]) + modulation[0]).astype(
            jnp.bfloat16
        )
        columns = jnp.einsum(
            "rd,cdw->crw",
            lax.all_gather(modulated, "queue", axis=0, tiled=True),
            stacked_weights,
            preferred_element_type=jnp.float32,
        )
        own_rows = lax.all_to_all(
            columns.astype(jnp.bfloat16), "queue", split_axis=1, concat_axis=2, tiled=True
        ).astype(columns.dtype)
        query_heads = (
            (normalize(own_rows[0]) * query_gain)
            .astype(jnp.bfloat16)
            .reshape(span_rows, HEADS, head_size)
        )
        key_heads = (
            (normalize(own_rows[1]) * key_gain)
            .astype(jnp.bfloat16)
            .reshape(span_rows, HEADS, head_size)
        )
        value_heads = own_rows[2].astype(jnp.bfloat16).reshape(span_rows, HEADS, head_size)
        query_slots, key_slots, value_slots = (
            lax.all_to_all(
                pad_slots(query_heads, slot_total), "queue", split_axis=1, concat_axis=0, tiled=True
            ),
            lax.all_to_all(
                pad_slots(key_heads, slot_total), "queue", split_axis=1, concat_axis=0, tiled=True
            ),
            lax.all_to_all(
                pad_slots(value_heads, slot_total), "queue", split_axis=1, concat_axis=0, tiled=True
            ),
        )
        attended_slots = causal_block(query_slots, key_slots, value_slots, span_rows, score_scale)
        crossed_slots = text_attend(query_slots, text_k_slots, text_v_slots, score_scale)
        attended_back, crossed_back = (
            lax.all_to_all(attended_slots, "queue", split_axis=0, concat_axis=1, tiled=True),
            lax.all_to_all(crossed_slots, "queue", split_axis=0, concat_axis=1, tiled=True),
        )
        attended = attended_back[:, :HEADS]
        crossed = crossed_back[:, :HEADS]
        combined = (
            (attended.astype(jnp.float32) + crossed.astype(jnp.float32))
            .astype(jnp.bfloat16)
            .reshape(span_rows, model_width)
        )
        out_columns = jnp.dot(
            lax.all_gather(combined, "queue", axis=0, tiled=True),
            output_weight,
            preferred_element_type=jnp.float32,
        )
        projected = lax.all_to_all(
            out_columns.astype(jnp.bfloat16), "queue", split_axis=0, concat_axis=1, tiled=True
        ).astype(out_columns.dtype)
        queue_state = (current + modulation[2] * projected).astype(jnp.bfloat16)
    return queue_state


def swapped(value, bit):
    count = lax.axis_size("queue")
    return lax.ppermute(value, "queue", [(source, source ^ bit) for source in range(count)])


def gathered_over_chips(block):
    chips = lax.axis_size("queue") // 2
    blocks = {0: block}
    for mask in range(2, chips, 2):
        blocks[mask] = swapped(block, 2 * mask)
    for mask in range(0, chips, 2):
        blocks[mask + 1] = swapped(blocks[mask], 2)
    return [blocks[mask] for mask in range(chips)]


def contract_last(left, right):
    return lax.dot_general(
        left, right, (((1,), (1,)), ((), ())), preferred_element_type=jnp.float32
    )


HBM_SPEC = pl.BlockSpec(memory_space=pltpu.HBM)
VMEM_SPEC = pl.BlockSpec(memory_space=pltpu.VMEM)
PARAMS = pltpu.CompilerParams(vmem_limit_bytes=60 * 1024 * 1024)
MIDDLE_PARAMS = pltpu.CompilerParams(vmem_limit_bytes=52 * 1024 * 1024)
SMALL_PARAMS = pltpu.CompilerParams(vmem_limit_bytes=16 * 1024 * 1024)


def span_at(position, step, spans):
    chips = spans // 2
    return (2 * (position % chips) + position // chips + step + 1) % spans


def own_place():
    own_index = lax.axis_index("queue")
    return own_index // 2, own_index % 2


def started(pairs, sems):
    copies = [
        pltpu.make_async_copy(source, target, sems.at[i]) for i, (source, target) in enumerate(pairs)
    ]
    for copy in copies:
        copy.start()
    return copies


def finished(copies):
    for copy in copies:
        copy.wait()


def project_kernel(step, spans, gain_hbm, table_hbm, incoming_hbm, *refs):
    chips = spans // 2
    weight_refs, refs = refs[:3], refs[3:]
    mine, others = refs[:chips], refs[chips : 2 * chips]
    refs = refs[2 * chips :]
    own_hbm, send_hbm, squares_ref = refs[:3]
    refs = refs[3:]
    if step == 0:
        current_hbm, refs = refs[0], refs[1:]
    state, modulated, table, entering, gain, scale_ref, shift_ref, own, send, current, sems = refs[:11]
    fetched = step == 0
    weights = refs[11] if fetched else weight_refs
    chip, core = own_place()
    tokens, width = modulated.shape
    half = tokens // 2
    rows = tokens // spans
    pair = 2 * rows
    cols = weight_refs[0].shape[0]
    first = core == 0
    own_lanes = pl.ds(pl.multiple_of(chip * 2 * cols, 2 * cols), 2 * cols)
    pairs = []
    for side, blocks in enumerate((mine, others)):
        owner = core if side == 0 else 1 - core
        for mask in range(chips):
            other_chip = chip ^ mask
            if step == 0:
                target = state.at[owner * chips + other_chip]
            else:
                lanes = pl.ds(pl.multiple_of(other_chip * 2 * cols, 2 * cols), 2 * cols)
                target = state.at[pl.ds(pl.multiple_of(owner * half, half), half), lanes]
            pairs.append((blocks[mask], target))
    pairs += [(table_hbm.at[pl.ds(0, 2)], table.at[pl.ds(0, 2)]), (gain_hbm.at[:, own_lanes], gain)]
    if step == 0:
        pairs.append((incoming_hbm.at[step], entering.at[step]))
    inputs = len(pairs)
    if fetched:
        pairs += [(weight_refs[i], weights.at[i]) for i in range(3)]
    copies = started(pairs, sems)
    copies, fetches = copies[:inputs], copies[inputs:]
    finished(copies)
    shift_ref[...] = table[0].astype(jnp.float32)
    scale_ref[...] = table[1].astype(jnp.float32) + 1.0
    leaving = []
    if step == 0:
        state[spans - 1] = entering[step]
        for slab in range(chips // 2):
            at = core * chips + 2 * slab
            both = [state[at + e, :, own_lanes].astype(jnp.float32) for e in range(2)]
            current[slab * pair : (slab + 1) * pair, :] = jnp.concatenate(both, axis=0).astype(
                jnp.bfloat16
            )
        leaving += started([(current, current_hbm)], sems.at[pl.ds(0, 1)])
    pieces = 4
    piece = width // pieces
    for slab in range(chips):
        band = slice(slab * pair, (slab + 1) * pair)

        def load(part):
            if step == 0:
                both = [state[2 * slab + e, :, part].astype(jnp.float32) for e in range(2)]
                return jnp.concatenate(both, axis=0)
            return state[band, part].astype(jnp.float32)

        total = jnp.zeros((pair, 1), jnp.float32)
        for low in range(0, width, piece):
            x = load(slice(low, low + piece))
            total = total + jnp.sum(x * x, axis=1, keepdims=True)
        factor = lax.rsqrt(total / width + 1e-06)
        at = [span_at(2 * slab + e, step, spans) for e in range(2)]
        for low in range(0, width, piece):
            part = slice(low, low + piece)
            x = load(part) * factor
            scale, shift = (
                jnp.concatenate(
                    [jnp.broadcast_to(ref[s : s + 1, part], (rows, piece)) for s in at], axis=0
                )
                for ref in (scale_ref, shift_ref)
            )
            modulated[band, part] = (x * scale + shift).astype(jnp.bfloat16)
    ident = lax.broadcasted_iota(jnp.int32, (tokens, tokens), 0) == lax.broadcasted_iota(
        jnp.int32, (tokens, tokens), 1
    )
    products = []
    for fetch, weight in ((fetches[:1], 0), (fetches[1:], 1), ([], 2)):
        finished(fetch)
        products.append(contract_last(modulated[...], weights[weight][...]))
    shape = (tokens, tokens)
    ident = lax.broadcasted_iota(jnp.int32, shape, 0) == lax.broadcasted_iota(jnp.int32, shape, 1)
    for i in range(2):
        column = jnp.sum(products[i] * products[i], axis=1, keepdims=True)
        line = jnp.sum(jnp.where(ident, column, 0.0), axis=0, keepdims=True)
        squares_ref[:, i : i + 1, :] = jnp.broadcast_to(line[None], (spans, 1, tokens))
        line = gain[i : i + 1, :]
        products[i] = products[i] * jnp.where(first, line[:, :cols], line[:, cols:])
    low, high = products[0][:half], products[0][half:]
    own[...] = jnp.where(first, low, high).astype(jnp.bfloat16)
    send[:half, :] = jnp.where(first, high, low).astype(jnp.bfloat16)
    send[half : half + tokens, :] = products[1].astype(jnp.bfloat16)
    send[half + tokens :, :] = products[2].astype(jnp.bfloat16)
    leaving += started([(own, own_hbm), (send, send_hbm)], sems.at[pl.ds(1, 2)])
    finished(leaving)


def project(step, spans, gain, table, incoming, mine, others, weights):
    rows = incoming.shape[1]
    tokens = spans * rows
    cols, width = weights[0].shape
    half = tokens // 2
    out_shape = [
        jax.ShapeDtypeStruct((half, cols), jnp.bfloat16),
        jax.ShapeDtypeStruct((half + 2 * tokens, cols), jnp.bfloat16),
        jax.ShapeDtypeStruct((spans, 2, tokens), jnp.float32),
    ]
    if step == 0:
        out_shape.append(jax.ShapeDtypeStruct((half, 2 * cols), jnp.bfloat16))
        state = (spans, rows, width)
    else:
        state = (tokens, width)
    return pl.pallas_call(
        functools.partial(project_kernel, step, spans),
        out_shape=out_shape,
        in_specs=[HBM_SPEC] * 3
        + [HBM_SPEC if step == 0 else VMEM_SPEC] * 3
        + [HBM_SPEC] * (2 * len(mine)),
        out_specs=[HBM_SPEC, HBM_SPEC, VMEM_SPEC, HBM_SPEC][: len(out_shape)],
        scratch_shapes=[
            pltpu.VMEM(state, jnp.bfloat16),
            pltpu.VMEM((tokens, width), jnp.bfloat16),
            pltpu.VMEM(table.shape, jnp.bfloat16),
            pltpu.VMEM(incoming.shape, jnp.bfloat16),
            pltpu.VMEM((2, 2 * cols), jnp.float32),
            pltpu.VMEM((spans, width), jnp.float32),
            pltpu.VMEM((spans, width), jnp.float32),
            pltpu.VMEM((half, cols), jnp.bfloat16),
            pltpu.VMEM((half + 2 * tokens, cols), jnp.bfloat16),
            pltpu.VMEM((half, 2 * cols), jnp.bfloat16),
            pltpu.SemaphoreType.DMA((spans + 6,)),
        ]
        + ([pltpu.VMEM((3, cols, width), jnp.bfloat16)] if step == 0 else []),
        compiler_params=PARAMS if step == 0 else SMALL_PARAMS,
        name="project",
    )(gain, table, incoming, *weights, *mine, *others)


def attend_kernel(
    step, spans, head_size, own_hbm, sent_hbm, got_hbm, squares_hbm, text_hbm, more_hbm,
    out_ref, own, sent, got, squares_ref, queries, keys, values, text_ref, more_ref, sems,
):
    copies = started(
        [
            (own_hbm, own),
            (sent_hbm, sent),
            (got_hbm, got),
            (squares_hbm, squares_ref),
            (text_hbm, text_ref),
            (more_hbm, more_ref),
        ],
        sems,
    )
    chip, core = own_place()
    first = core == 0
    half, width = queries.shape
    tokens = 2 * half
    rows = tokens // spans
    cols = width // 2
    finished(copies[:3])
    for target, mine_ref, low, size in (
        (queries, own, 0, half),
        (keys, sent, half, tokens),
        (values, sent, half + tokens, tokens),
    ):
        mine = mine_ref[low : low + size, :]
        other = got[low : low + size, :]
        target[:, :cols] = jnp.where(first, mine, other)
        target[:, cols:] = jnp.where(first, other, mine)
    copies[3].wait()
    factors = lax.rsqrt(jnp.sum(squares_ref[...], axis=0) / (width * (spans // 2)) + 1e-06)
    ident = lax.broadcasted_iota(jnp.int32, (tokens, tokens), 0) == lax.broadcasted_iota(
        jnp.int32, (tokens, tokens), 1
    )
    column = jnp.sum(jnp.where(ident, factors[0:1, :], 0.0), axis=1, keepdims=True)
    column = jnp.where(first, column[:half], column[half:]) * (1.0 / math.sqrt(head_size))
    row = factors[1:2, :]
    shape = (half, tokens)
    own_block = lax.broadcasted_iota(jnp.int32, shape, 0) // rows + core * (spans // 2)
    key_block = lax.broadcasted_iota(jnp.int32, shape, 1) // rows
    allowed = span_at(own_block, step, spans) >= span_at(key_block, step, spans)
    text_rows = text_ref.shape[0] * text_ref.shape[2]
    finished(copies[4:])
    heads = width // head_size
    lanes = [slice(head * head_size, (head + 1) * head_size) for head in range(heads)]
    stacked = jnp.concatenate([column] * heads, axis=0)
    scores = jnp.concatenate([contract_last(queries[:, at], keys[:, at]) for at in lanes], axis=0)
    scores = scores * stacked * row
    scores = jnp.where(jnp.concatenate([allowed] * heads, axis=0), scores, -1e30)
    parts = []
    for ref in (text_ref, more_ref):
        products = [
            contract_last(queries[:, at], ref[:, 0, :, at].reshape(text_rows, head_size))
            for at in lanes
        ]
        parts.append(jnp.concatenate(products, axis=0) * stacked)
    weights = jnp.exp(scores - jnp.max(scores, axis=1, keepdims=True))
    weights = weights * (1.0 / jnp.sum(weights, axis=1, keepdims=True))
    weights = weights.astype(jnp.bfloat16)
    most = jnp.max(jnp.maximum(*parts), axis=1, keepdims=True)
    parts = [jnp.exp(part - most) for part in parts]
    share = 1.0 / jnp.sum(parts[0] + parts[1], axis=1, keepdims=True)
    parts = [(part * share).astype(jnp.bfloat16) for part in parts]
    for head, at in enumerate(lanes):
        band = slice(head * half, (head + 1) * half)
        attended = jnp.dot(weights[band], values[:, at], preferred_element_type=jnp.float32)
        crossed = jnp.zeros((half, head_size), jnp.float32)
        for ref, part in zip((text_ref, more_ref), parts):
            text_values = ref[:, 1, :, at].reshape(text_rows, head_size)
            crossed = crossed + jnp.dot(
                part[band], text_values, preferred_element_type=jnp.float32
            )
        attended, crossed = (
            value.astype(jnp.bfloat16).astype(jnp.float32) for value in (attended, crossed)
        )
        out_ref[:, at] = (attended + crossed).astype(jnp.bfloat16)


def attend(step, spans, head_size, own, sent, got, squares, text, more):
    half, cols = own.shape
    tokens = 2 * half
    return pl.pallas_call(
        functools.partial(attend_kernel, step, spans, head_size),
        out_shape=jax.ShapeDtypeStruct((half, 2 * cols), jnp.bfloat16),
        in_specs=[HBM_SPEC] * 6,
        out_specs=VMEM_SPEC,
        scratch_shapes=[
            pltpu.VMEM(own.shape, jnp.bfloat16),
            pltpu.VMEM(sent.shape, jnp.bfloat16),
            pltpu.VMEM(got.shape, jnp.bfloat16),
            pltpu.VMEM(squares.shape, jnp.float32),
            pltpu.VMEM((half, 2 * cols), jnp.bfloat16),
            pltpu.VMEM((tokens, 2 * cols), jnp.bfloat16),
            pltpu.VMEM((tokens, 2 * cols), jnp.bfloat16),
            pltpu.VMEM(text.shape, jnp.bfloat16),
            pltpu.VMEM(more.shape, jnp.bfloat16),
            pltpu.SemaphoreType.DMA((6,)),
        ],
        compiler_params=PARAMS,
        name="attend",
    )(own, sent, got, squares, text, more)


def output_kernel(
    step, spans, last, current_hbm, table_hbm, incoming_hbm, own_hbm, other_hbm, *refs
):
    chips = spans // 2
    block_refs, refs = refs[:chips], refs[chips:]
    out_ref, blocks, current, gate_ref, entering, totals, weights, sems = refs
    chip, core = own_place()
    first = core == 0
    half, width = current.shape
    cols = width // 2
    rows = 2 * half // spans
    own_lanes = pl.ds(pl.multiple_of(chip * width, width), width)
    pairs = []
    for mask in range(chips):
        lanes = pl.ds(pl.multiple_of((chip ^ mask) * width, width), width)
        pairs.append((block_refs[mask], blocks.at[mask]))
        for side, ref in enumerate((own_hbm, other_hbm)):
            pairs.append((ref.at[:, lanes], weights.at[mask, side]))
    pairs.append((current_hbm, current))
    pairs.append((table_hbm.at[2, :, own_lanes], gate_ref))
    if not last:
        pairs.append((incoming_hbm.at[step + 1, :, own_lanes], entering))
    copies = started(pairs, sems)
    mine = jnp.zeros((half, cols), jnp.float32)
    other = jnp.zeros((half, cols), jnp.float32)
    for mask in range(chips):
        if mask % (chips // 2) == 0:
            finished(copies[3 * mask : 3 * (mask + chips // 2)])
        block = blocks[mask]
        mine = mine + contract_last(block, weights[mask, 0])
        other = other + contract_last(block, weights[mask, 1])
    totals[:, :cols] = jnp.where(first, mine, other)
    totals[:, cols:] = jnp.where(first, other, mine)
    finished(copies[3 * chips :])
    gates = gate_ref[...].astype(jnp.float32)
    gate = []
    for block in range(chips):
        places = [span_at(block + e * chips, step, spans) for e in range(2)]
        row = jnp.where(first, *(gates[s : s + 1, :] for s in places))
        gate.append(jnp.broadcast_to(row, (rows, width)))
    state = current[...].astype(jnp.float32) + jnp.concatenate(gate, axis=0) * totals[...]
    if last:
        for target in range(chips):
            block = (target - STEPS // 2) % chips
            out_ref[target] = state[block * rows : (block + 1) * rows, :].astype(jnp.bfloat16)
    else:
        parity, block = (spans - 2 - step) % 2, (spans - 2 - step) // 2
        replaced = lax.broadcasted_iota(jnp.int32, (half, width), 0) // rows == block
        fresh = jnp.concatenate([entering[...].astype(jnp.float32)] * chips, axis=0)
        state = jnp.where(replaced & (core == parity), fresh, state)
        out_ref[...] = state.astype(jnp.bfloat16)


def output(step, spans, last, current, table, incoming, own, other, blocks):
    half, width = current.shape
    chips = spans // 2
    rows = 2 * half // spans
    return pl.pallas_call(
        functools.partial(output_kernel, step, spans, last),
        out_shape=jax.ShapeDtypeStruct(
            (chips, rows, width) if last else (half, width), jnp.bfloat16
        ),
        in_specs=[HBM_SPEC] * (5 + chips),
        out_specs=VMEM_SPEC,
        scratch_shapes=[
            pltpu.VMEM((chips, half, width), jnp.bfloat16),
            pltpu.VMEM((half, width), jnp.bfloat16),
            pltpu.VMEM((spans, width), jnp.bfloat16),
            pltpu.VMEM((rows, width), jnp.bfloat16),
            pltpu.VMEM((half, width), jnp.float32),
            pltpu.VMEM((chips, 2, width // 2, width), jnp.bfloat16),
            pltpu.SemaphoreType.DMA((3 * chips + 3,)),
        ],
        compiler_params=PARAMS if last else MIDDLE_PARAMS,
        name="output",
    )(current, table, incoming, own, other, *blocks)


def arrange_kernel(spans, keys_ref, values_ref, out_ref):
    width = out_ref.shape[3]
    text_half = out_ref.shape[2]
    for device in range(spans):
        lanes = slice(device // 2 * width, (device // 2 + 1) * width)
        band = slice(device % 2 * text_half, (device % 2 + 1) * text_half)
        out_ref[device, 0] = keys_ref[band, lanes]
        out_ref[device, 1] = values_ref[band, lanes]


def arrange(spans, keys, values):
    text_half = keys.shape[0] // 2
    return pl.pallas_call(
        functools.partial(arrange_kernel, spans),
        out_shape=jax.ShapeDtypeStruct(
            (spans, 2, text_half, 2 * keys.shape[1] // spans), jnp.bfloat16
        ),
        in_specs=[VMEM_SPEC] * 2,
        out_specs=VMEM_SPEC,
        compiler_params=PARAMS,
        name="arrange",
    )(keys, values)


def paired_device(
    hidden,
    incoming,
    levels,
    mod_table,
    query_weight,
    key_weight,
    value_weight,
    output_weight,
    query_gain,
    key_gain,
    text_keys,
    text_values,
):
    spans = lax.axis_size("queue")
    chips = spans // 2
    head_size = hidden.shape[1] // HEADS
    mine = gathered_over_chips(hidden)
    others = [swapped(block, 1) for block in mine]
    picked = (levels[:, None] == jnp.arange(mod_table.shape[0])[None, :]).astype(mod_table.dtype)
    table = jnp.einsum("sl,ltd->tsd", picked, mod_table, preferred_element_type=jnp.float32)
    table = table.astype(jnp.bfloat16)
    gain = jnp.stack([query_gain, key_gain])
    weights = [w.T for w in (query_weight, key_weight, value_weight)]
    output_own = output_weight.T
    output_other = swapped(output_own, 1)
    text = arrange(spans, text_keys, text_values)
    text, table, gain = lax.optimization_barrier((text, table, gain, *mine))[:3]
    text = lax.all_to_all(text, "queue", split_axis=0, concat_axis=0, tiled=True)
    current = None
    for step in range(STEPS):
        last = step == STEPS - 1
        own, send, squares, *rest = project(
            step, spans, gain, table, incoming, mine, others, weights
        )
        got = swapped(send, 1)
        squares = lax.all_to_all(squares, "queue", split_axis=0, concat_axis=0, tiled=True)
        if step == 0:
            current = rest[0]
            text = lax.optimization_barrier((text, send))[0]
            more = swapped(text, 1)
        block = attend(step, spans, head_size, own, send, got, squares, text, more)
        blocks = gathered_over_chips(block)
        result = output(
            step, spans, last, current, table, incoming, output_own, output_other, blocks
        )
        if not last:
            current = result
            mine = gathered_over_chips(current)
            others = [swapped(block, 1) for block in mine]
    same_core = [[2 * c + core for c in range(chips)] for core in range(2)]
    result = lax.all_to_all(
        result, "queue", split_axis=0, concat_axis=2, tiled=True, axis_index_groups=same_core
    )
    return result[0]


def held_in_pairs(mesh, hidden, query_weight):
    spans = mesh.shape["queue"]
    rows = hidden.shape[0] // (mesh.shape["groups"] * spans)
    cols = query_weight.shape[1] // spans
    head_size = query_weight.shape[0] // HEADS
    power = spans & (spans - 1) == 0
    return STEPS % 2 == 0 and power and spans >= 4 and 2 * cols % head_size == 0 and rows * spans == 128 and rows == 8


def solution(mesh):
    in_specs = (
        P(("groups", "queue"), None),
        P(None, "groups", None),
        P(),
        P(),
        P(None, "queue"),
        P(None, "queue"),
        P(None, "queue"),
        P(None, "queue"),
        P(),
        P(),
        P(("groups", "queue"), None),
        P(("groups", "queue"), None),
    )
    out_specs = P(("groups", "queue"), None)

    def apply(*args):
        body = paired_device if held_in_pairs(mesh, args[0], args[4]) else per_device
        return jax.shard_map(
            body, mesh=mesh, in_specs=in_specs, out_specs=out_specs, check_vma=False
        )(*args)

    return apply
```
